32 devices in a mesh: pop: 2 (over y), section: 2 (over core), tensor: 4 (over z), rep: 2 (over x).
Axes of the slice: x: 2, y: 2, z: 4, core: 2. Of those that a mesh axis runs over, the one named last changes fastest.
Arguments:
- tokens: bfloat16 [768, 4096], P(('pop', 'rep'), 'tensor'), parts along dimension 0, may hold values from -6 to 6
- norm_gain: bfloat16 [2, 4096], P('section'), may hold values from 0.099609375 to 1.8984375
- gate_tiles: bfloat16 [2, 2048, 128, 128], P('section', ('tensor', 'rep')), may hold values from -0.125 to 0.125
- up_tiles: bfloat16 [2, 2048, 128, 128], P('section', ('tensor', 'rep')), may hold values from -0.125 to 0.125
- down_tiles: bfloat16 [2, 2048, 128, 128], P('section', ('tensor', 'rep')), may hold values from -0.0625 to 0.0625
- gate_slot: int32 [2, 2048], P('section', 'tensor'), may hold values from -1 to 1023, as said below
- up_slot: int32 [2, 2048], P('section', 'tensor'), may hold values from -1 to 1023, as said below
- down_slot: int32 [2, 2048], P('section', 'tensor'), may hold values from -1 to 1023, as said below
- owned_columns: int32 [2, 128], P('section'), may hold values from 0 to 127, each once within a row
- gate_left: bfloat16 [2, 8, 4096], P('section'), may hold values from -0.09375 to 0.09375
- gate_right: bfloat16 [2, 8, 16384], P('section'), may hold values from -6 to 6
- up_left: bfloat16 [2, 8, 4096], P('section'), may hold values from -0.09375 to 0.09375
- up_right: bfloat16 [2, 8, 16384], P('section'), may hold values from -6 to 6
- down_left: bfloat16 [2, 8, 16384], P('section'), may hold values from -0.046875 to 0.046875
- down_right: bfloat16 [2, 8, 4096], P('section'), may hold values from -6 to 6
- row_member: int32 [768], P(('pop', 'rep')), parts along dimension 0, may hold values from 0 to 63
- member_seed: int32 [128], P('pop'), parts along dimension 0, may hold values from 0 to 7
Outputs:
- layer_outputs: bfloat16 [2, 768, 4096], P('section', ('pop', 'rep'), 'tensor'), parts along dimension 1
The draws below stay inside these ranges and needn't reach their ends.
There are 2 independent parts, one for each index of `pop`. The reference program is written for one: setup_inputs(seed, part) draws one part's arguments, and reference() takes and returns one part's arrays. A program takes and returns all parts, laid end to end along the dimension named above; an argument that names none is the same for every part. Nothing has to cross between parts.
Inputs may be any that keep to these rules, and one draw needn't show every extreme that they name: `gate_slot`: each entry is -1 (an empty slot) or c * 32 + d, placing a tile at the owner's c-th hidden block column and block row d of the features; the codes of one owner in one layer are distinct, and in every layer some owner has all 512 slots in use. `up_slot`: as for gate_slot. `down_slot`: each entry is -1 (an empty slot) or c * 32 + d, placing a tile at the owner's c-th hidden block column (its rows) and block d of the output features (its columns); the codes of one owner in one layer are distinct, and in every layer some owner has all 512 slots in use.
All inputs are finite; a program needn't handle non-finite values.
Results may differ from the reference program's by a relative error of at most 0.015.
Values may be sent and summed in bfloat16 or wider, within the bound.
No kernel may reach another device: no remote copies, remote signals or barrier semaphores. Data moves between devices by JAX's collectives and lax.ppermute only.
A program may use at most 384 MiB of HBM per device.

```python
import jax
import jax.numpy as jnp
from jax import lax

D = 4096
FF = 16384
BLOCK = 128
NOISE = 8
MEMBERS = 64
LAYERS = 2
ROWS = 384
DB = 32
FB = 128
OWNERS = 4
OWN_COLS = 32
CAP = 512


def slot_table(key):
    count_key, owner_key, code_key, order_key = jax.random.split(key, 4)
    pair_count = LAYERS * OWNERS
    code_keys = jax.random.split(code_key, pair_count)
    chosen = jax.vmap(lambda subkey: jax.random.permutation(subkey, OWN_COLS * DB)[:CAP])(code_keys)
    counts = jax.random.randint(count_key, (LAYERS, OWNERS), CAP // 2, CAP + 1)
    fullest = jax.random.randint(owner_key, (LAYERS, 1), 0, OWNERS)
    counts = jnp.where(jnp.arange(OWNERS)[None, :] == fullest, CAP, counts).reshape(pair_count, 1)
    active = jnp.arange(CAP)[None, :] < counts
    slot_codes = jnp.where(active, chosen, -1)
    order_keys = jax.random.split(order_key, pair_count)
    orders = jax.vmap(lambda subkey: jax.random.permutation(subkey, CAP))(order_keys)
    slot_codes = jnp.take_along_axis(slot_codes, orders, axis=1)
    return slot_codes.reshape(LAYERS, OWNERS * CAP).astype(jnp.int32)


def draw_gate_slot(key, part):
    key = jax.random.fold_in(key, 11)
    return slot_table(key)


def draw_up_slot(key, part):
    key = jax.random.fold_in(key, 23)
    return slot_table(key)


def draw_down_slot(key, part):
    key = jax.random.fold_in(key, 37)
    return slot_table(key)


def touch_ends(array, key, low, largest):
    longest = array.shape.index(max(array.shape))
    spots = []
    for shift in (0, 1):
        where = [jax.random.randint(jax.random.fold_in(key, axis), (), 0, length) for axis, length in enumerate(array.shape)]
        where[longest] = (where[longest] + shift) % array.shape[longest]
        spots.append(tuple(where))
    return array.at[spots[0]].set(low).at[spots[1]].set(largest)


def shard_levels(key, shape, cuts, smallest, top_value):
    def one(axis_at, blocks):
        heights = jax.random.uniform(jax.random.fold_in(jax.random.fold_in(key, 6), axis_at), (blocks,), jnp.float32, smallest / len(cuts), top_value / len(cuts))
        return jnp.repeat(jnp.exp(heights), shape[axis_at] // blocks).reshape((-1,) + (1,) * (len(shape) - axis_at - 1))

    loudness = one(*cuts[0])
    for cut in cuts[1:]:
        loudness = loudness * one(*cut)
    return loudness


def noise(key, shape, deviation, bound, shards=(), kind=jnp.bfloat16):
    values = jax.random.normal(key, shape, jnp.float32) * deviation
    if len(shards) > 0:
        values = shard_levels(key, shape, shards, -0.22, 0.18) * values
    return jnp.clip(values, min=-bound, max=bound).astype(kind)


def setup_inputs(seed: int = 0, part: int = 0) -> dict:
    arg_keys = jax.random.split(jax.random.key(seed), 18)
    own_keys = jax.random.split(jax.random.fold_in(arg_keys[17], part), 18)
    tokens = noise(own_keys[0], (ROWS, D), 1.0, 6.0, ((0, 2), (1, 4)))
    norm_gain = jnp.clip(1.0 + 0.18 * jax.random.normal(arg_keys[1], (LAYERS, D), jnp.float32), 0.099609375, 1.8984375).astype(jnp.bfloat16)
    gate_tiles = noise(arg_keys[2], (LAYERS, OWNERS * CAP, BLOCK, BLOCK), (D // 2) ** -0.5, 0.125, ((0, 2), (1, 8)))
    up_tiles = noise(arg_keys[3], (LAYERS, OWNERS * CAP, BLOCK, BLOCK), (D // 2) ** -0.5, 0.125, ((0, 2), (1, 8)))
    down_tiles = noise(arg_keys[4], (LAYERS, OWNERS * CAP, BLOCK, BLOCK), (FF // 2) ** -0.5, 0.0625, ((0, 2), (1, 8)))
    gate_slot = draw_gate_slot(jax.random.fold_in(arg_keys[17], 71), part)
    up_slot = draw_up_slot(jax.random.fold_in(arg_keys[17], 71), part)
    down_slot = draw_down_slot(jax.random.fold_in(arg_keys[17], 71), part)
    owned_columns = jax.vmap(lambda own: jax.random.permutation(own, FB))(jax.random.split(arg_keys[8], LAYERS)).reshape((LAYERS, FB)).astype(jnp.int32)
    gate_left = noise(arg_keys[9], (LAYERS, NOISE, D), D ** -0.5, 0.09375, ((0, 2),))
    gate_right = noise(arg_keys[10], (LAYERS, NOISE, FF), 1.0, 6.0, ((0, 2),))
    up_left = noise(arg_keys[11], (LAYERS, NOISE, D), D ** -0.5, 0.09375, ((0, 2),))
    up_right = noise(arg_keys[12], (LAYERS, NOISE, FF), 1.0, 6.0, ((0, 2),))
    down_left = noise(arg_keys[13], (LAYERS, NOISE, FF), FF ** -0.5, 0.046875, ((0, 2),))
    down_right = noise(arg_keys[14], (LAYERS, NOISE, D), 1.0, 6.0, ((0, 2),))
    row_member = touch_ends(jax.random.randint(own_keys[15], (ROWS,), 0, MEMBERS), jax.random.fold_in(own_keys[15], 1), 0, MEMBERS - 1).astype(jnp.int32)
    member_seed = touch_ends(jax.random.randint(own_keys[16], (MEMBERS,), 0, NOISE), jax.random.fold_in(own_keys[16], 1), 0, NOISE - 1).astype(jnp.int32)
    return {"tokens": tokens, "norm_gain": norm_gain, "gate_tiles": gate_tiles, "up_tiles": up_tiles, "down_tiles": down_tiles, "gate_slot": gate_slot, "up_slot": up_slot, "down_slot": down_slot, "owned_columns": owned_columns, "gate_left": gate_left, "gate_right": gate_right, "up_left": up_left, "up_right": up_right, "down_left": down_left, "down_right": down_right, "row_member": row_member, "member_seed": member_seed}


perturb_scale = 0.5
epsilon = 1e-05

def pick_matrix(row_member, member_seed, noise_count):
    member_ids = jnp.arange(member_seed.shape[0], dtype=jnp.int32)
    matched = row_member[:, None] == member_ids[None, :]
    seed_of = lax.optimization_barrier(jnp.sum(jnp.where(matched, member_seed[None, :], 0), axis=1)).astype(jnp.int32)
    sign_values = (1 - 2 * (row_member % 2)).astype(jnp.float32) * perturb_scale
    noise_ids = jnp.arange(noise_count, dtype=jnp.int32)
    return jnp.where(seed_of[:, None] == noise_ids[None, :], sign_values[:, None], jnp.float32(0.0)).astype(jnp.float32)

def split_codes(slot_codes):
    active = slot_codes >= 0
    cleared = jnp.where(active, slot_codes, 0).astype(jnp.int32)
    return (cleared // DB, cleared % DB, active)

def block_product(source, tile_set, src_index, dst_index, active, out_count):
    picked = jnp.take(source, src_index, axis=1).astype(jnp.float32)
    products = jnp.einsum('rsk,skn->rsn', picked, tile_set.astype(jnp.float32), precision=lax.Precision.HIGHEST)
    targets = jnp.arange(out_count, dtype=jnp.int32)
    placing = jnp.where(active[:, None] & (dst_index[:, None] == targets[None, :]), 1.0, 0.0).astype(jnp.float32)
    return jnp.einsum('rsn,sc->rcn', products, placing, precision=lax.Precision.HIGHEST)

def column_select(noise_table, columns):
    noise_count = noise_table.shape[0]
    blocked = noise_table.reshape(noise_count, -1, BLOCK)
    return jnp.take(blocked, columns, axis=1).reshape(noise_count, -1)

def owner_partial(normed, gate_coef, up_coef, picks, gate_set, up_set, down_set, gate_codes, up_codes, down_codes, gate_cols, up_cols, down_cols, down_wide):
    row_count = normed.shape[0]
    col_count = gate_cols.shape[1] // BLOCK
    normed_blocks = normed.reshape(row_count, -1, BLOCK)
    hidden_part, feature_part, active = split_codes(gate_codes)
    gate_value = block_product(normed_blocks, gate_set, feature_part, hidden_part, active, col_count).reshape(row_count, -1)
    gate_value = gate_value + jnp.dot(gate_coef, gate_cols, preferred_element_type=jnp.float32)
    hidden_part, feature_part, active = split_codes(up_codes)
    up_value = block_product(normed_blocks, up_set, feature_part, hidden_part, active, col_count).reshape(row_count, -1)
    up_value = up_value + jnp.dot(up_coef, up_cols, preferred_element_type=jnp.float32)
    hidden = (jax.nn.silu(gate_value) * up_value).astype(jnp.bfloat16)
    hidden_part, feature_part, active = split_codes(down_codes)
    hidden_blocks = hidden.reshape(row_count, -1, BLOCK)
    partial_value = block_product(hidden_blocks, down_set, hidden_part, feature_part, active, normed_blocks.shape[1]).reshape(row_count, -1)
    down_coef = picks * jnp.dot(hidden, down_cols.T, preferred_element_type=jnp.float32)
    return partial_value + jnp.dot(down_coef, down_wide, precision=lax.Precision.HIGHEST)

def reference(tokens, norm_gain, gate_tiles, up_tiles, down_tiles, gate_slot, up_slot, down_slot, owned_columns, gate_left, gate_right, up_left, up_right, down_left, down_right, row_member, member_seed):
    picks = pick_matrix(row_member, member_seed, NOISE)
    stream = tokens
    outputs = []
    for layer_index in range(LAYERS):
        values = stream.astype(jnp.float32)
        inverse_rms = lax.rsqrt(lax.optimization_barrier(jnp.mean(values * values, axis=1, keepdims=True)) + epsilon)
        normed = (values * inverse_rms * norm_gain[layer_index].astype(jnp.float32)).astype(jnp.bfloat16)
        gate_coef = (picks * jnp.dot(normed, gate_left[layer_index].T, preferred_element_type=jnp.float32)).astype(jnp.bfloat16)
        up_coef = (picks * jnp.dot(normed, up_left[layer_index].T, preferred_element_type=jnp.float32)).astype(jnp.bfloat16)
        down_wide = down_right[layer_index].astype(jnp.float32)
        owner_items = (gate_tiles[layer_index].reshape(OWNERS, CAP, BLOCK, BLOCK), up_tiles[layer_index].reshape(OWNERS, CAP, BLOCK, BLOCK), down_tiles[layer_index].reshape(OWNERS, CAP, BLOCK, BLOCK), gate_slot[layer_index].reshape(OWNERS, CAP), up_slot[layer_index].reshape(OWNERS, CAP), down_slot[layer_index].reshape(OWNERS, CAP), owned_columns[layer_index].reshape(OWNERS, OWN_COLS))
        gate_table = gate_right[layer_index]
        up_table = up_right[layer_index]
        down_table = down_left[layer_index]

        def owner_term(summed, items):
            gate_set, up_set, down_set, gate_codes, up_codes, down_codes, columns = items
            partial_value = owner_partial(normed, gate_coef, up_coef, picks, gate_set, up_set, down_set, gate_codes, up_codes, down_codes, column_select(gate_table, columns), column_select(up_table, columns), column_select(down_table, columns), down_wide)
            rounded = lax.optimization_barrier(partial_value.astype(jnp.bfloat16))
            return (summed + rounded.astype(jnp.float32), None)
        summed, unused = lax.scan(owner_term, jnp.zeros(tokens.shape, jnp.float32), owner_items)
        stream = (values + summed).astype(jnp.bfloat16)
        outputs.append(stream)
    return jnp.stack(outputs)
```

```python
import functools

import jax
import jax.numpy as jnp
from jax import lax
from jax.experimental import pallas as pl
from jax.experimental.pallas import tpu as pltpu
from jax.sharding import PartitionSpec as P

BLOCK = 128
UNROLL = 4
VMEM_LIMIT = 56 * 1024 * 1024

perturb_scale = 0.5
epsilon = 1e-05


def hop(value, axis, steps, source, target):
    count = lax.axis_size(axis)
    pairs = [(source * count + i, target * count + (i + steps) % count) for i in range(count)]
    return lax.ppermute(value, ("section", axis), pairs)


def pick_matrix(row_member, member_seed, noise_count):
    member_ids = jnp.arange(member_seed.shape[0], dtype=jnp.int32)
    matched = row_member[:, None] == member_ids[None, :]
    seed_of = jnp.sum(jnp.where(matched, member_seed[None, :], 0), axis=1)
    sign_values = (1 - 2 * (row_member % 2)).astype(jnp.float32) * perturb_scale
    noise_ids = jnp.arange(noise_count, dtype=jnp.int32)
    return jnp.where(seed_of[:, None] == noise_ids[None, :], sign_values[:, None], jnp.float32(0.0))


def tile_plan(codes, block_rows, own_cols, owner_index, owners):
    tile_count = codes.shape[1]
    active = codes >= 0
    cleared = jnp.where(active, codes, 0)
    column = cleared // block_rows
    feature = cleared % block_rows
    per_owner = block_rows // owners
    feature = lax.rem(owner_index - feature // per_owner + owners, owners) * per_owner + feature % per_owner
    is_down = jnp.arange(3)[:, None] == 2
    major = jnp.where(is_down, feature, column)
    minor = jnp.where(is_down, column, feature)
    major_count = max(block_rows, own_cols)
    majors = jnp.arange(major_count, dtype=jnp.int32)
    filled = jnp.sum(
        jnp.where(active[:, None, :] & (major[:, None, :] == majors[None, :, None]), 1, 0), axis=2
    )
    padded = 2 * ((filled + 1) // 2)
    before = jnp.sum(jnp.where(majors[None, None, :] < major[:, :, None], padded[:, None, :], 0), axis=2)
    rank = jnp.sum(
        jnp.where(
            active[:, None, :]
            & (major[:, None, :] == major[:, :, None])
            & (minor[:, None, :] < minor[:, :, None]),
            1,
            0,
        ),
        axis=2,
    )
    place = jnp.where(active, before + rank, -1)
    length = tile_count + min(tile_count, major_count)
    group = 2 * UNROLL
    length = -(-length // group) * group
    tile_ids = jnp.arange(tile_count, dtype=jnp.int32)
    words = (tile_ids[None, :] - tile_count) + minor * 4096 + major * 1048576
    spots = jnp.arange(length, dtype=jnp.int32)
    packed = tile_count + jnp.sum(
        jnp.where(place[:, None, :] == spots[None, :, None], words[:, None, :], 0), axis=2
    )
    groups = (jnp.sum(padded, axis=1) + group - 1) // group
    return packed.astype(jnp.int32), groups.astype(jnp.int32)


def multiply_tiles(words_ref, groups_ref, which, length, read, tiles_ref, add):
    def group(i, carry):
        for u in range(UNROLL):
            at = which * length + (i * UNROLL + u) * 2
            first, second = words_ref[at], words_ref[at + 1]
            left = jnp.concatenate([read((first >> 12) & 255), read((second >> 12) & 255)], axis=1)
            right = jnp.concatenate([tiles_ref[first & 4095], tiles_ref[second & 4095]], axis=0)
            add(first >> 20, jnp.dot(left, right, preferred_element_type=jnp.float32))
        return carry

    lax.fori_loop(0, groups_ref[which], group, 0)


def expand_kernel(owners, reps, length, words_ref, groups_ref, *refs):
    blocks = refs[: owners * reps]
    gain_ref, left_ref, gate_hbm, up_hbm = refs[owners * reps : owners * reps + 4]
    own_ref, raw_ref = refs[owners * reps + 4 : owners * reps + 6]
    peer_refs = refs[owners * reps + 6 : owners * reps + 6 + reps - 1]
    x_ref, other_ref, gate_tiles, up_tiles, sems = refs[owners * reps + 6 + reps - 1 :]
    tile_count = gate_hbm.shape[0]
    copies = [
        pltpu.make_async_copy(gate_hbm, gate_tiles.at[pl.ds(0, tile_count)], sems.at[0]),
        pltpu.make_async_copy(up_hbm, up_tiles.at[pl.ds(0, tile_count)], sems.at[1]),
    ]
    for copy in copies:
        copy.start()
    gate_tiles[tile_count] = jnp.zeros((BLOCK, BLOCK), gate_tiles.dtype)
    up_tiles[tile_count] = jnp.zeros((BLOCK, BLOCK), up_tiles.dtype)
    rows, width = blocks[0].shape
    strip = 16
    for rep in range(reps):

        def norm_rows(i, carry, rep=rep):
            at = pl.multiple_of(i * strip, strip)
            total = jnp.zeros((strip, 1), jnp.float32)
            for owner in range(owners):
                values = blocks[owner * reps + rep][pl.ds(at, strip), :].astype(jnp.float32)
                total = total + jnp.sum(values * values, axis=1, keepdims=True)
            inverse = lax.rsqrt(total / (owners * width) + epsilon)
            for owner in range(owners):
                for part in range(width // BLOCK):
                    lanes = pl.ds(part * BLOCK, BLOCK)
                    values = blocks[owner * reps + rep][pl.ds(at, strip), lanes].astype(jnp.float32)
                    gain = gain_ref[:, pl.ds(owner * width + part * BLOCK, BLOCK)].astype(jnp.float32)
                    normed = (values * inverse * gain).astype(jnp.bfloat16)
                    x_ref[owner * (width // BLOCK) + part, pl.ds(rep * rows + at, strip), :] = normed
            return carry

        lax.fori_loop(0, rows // strip, norm_rows, 0)

    raw = jnp.zeros(raw_ref.shape, jnp.float32)
    for d in range(x_ref.shape[0]):
        raw = raw + lax.dot_general(
            x_ref[d, pl.ds(0, rows), :],
            left_ref[:, pl.ds(d * BLOCK, BLOCK)],
            (((1,), (1,)), ((), ())),
            preferred_element_type=jnp.float32,
        )
    raw_ref[...] = raw

    def read(block):
        return x_ref[block]

    for which, tiles in ((0, gate_tiles), (1, up_tiles)):
        own_ref[which] = jnp.zeros(own_ref.shape[1:], jnp.float32)
        other_ref[...] = jnp.zeros(other_ref.shape, jnp.float32)
        copies[which].wait()

        def add(block, product, which=which):
            own_ref[which, block] += product[:rows]
            if reps > 1:
                other_ref[block] += product[rows:]

        multiply_tiles(words_ref, groups_ref, which, length, read, tiles, add)
        for rep in range(1, reps):

            def narrow(c, carry, which=which, rep=rep):
                peer_refs[rep - 1][which, c] = other_ref[c, pl.ds((rep - 1) * rows, rows), :].astype(jnp.bfloat16)
                return carry

            lax.fori_loop(0, other_ref.shape[0], narrow, 0)


def expand(words, groups, blocks, gain, left, gate_tiles, up_tiles, own_cols):
    owners, reps = len(blocks), len(blocks[0])
    rows, width = blocks[0][0].shape
    tile_count = gate_tiles.shape[0]
    feature_blocks = owners * width // BLOCK
    length = words.shape[0] // 3
    smem = pl.BlockSpec(memory_space=pltpu.SMEM)
    vmem = pl.BlockSpec(memory_space=pltpu.VMEM)
    hbm = pl.BlockSpec(memory_space=pl.ANY)
    flat = [block for group in blocks for block in group]
    out = pl.pallas_call(
        functools.partial(expand_kernel, owners, reps, length),
        out_shape=[
            jax.ShapeDtypeStruct((2, own_cols, rows, BLOCK), jnp.float32),
            jax.ShapeDtypeStruct((rows, left.shape[0]), jnp.float32),
        ]
        + [jax.ShapeDtypeStruct((2, own_cols, rows, BLOCK), jnp.bfloat16)] * (reps - 1),
        in_specs=[smem, smem] + [vmem] * (len(flat) + 2) + [hbm, hbm],
        out_specs=[vmem] * (2 + reps - 1),
        scratch_shapes=[
            pltpu.VMEM((feature_blocks, reps * rows, BLOCK), jnp.bfloat16),
            pltpu.VMEM((own_cols, max(reps - 1, 1) * rows, BLOCK), jnp.float32),
            pltpu.VMEM((tile_count + 1, BLOCK, BLOCK), jnp.bfloat16),
            pltpu.VMEM((tile_count + 1, BLOCK, BLOCK), jnp.bfloat16),
            pltpu.SemaphoreType.DMA((2,)),
        ],
        compiler_params=pltpu.CompilerParams(vmem_limit_bytes=VMEM_LIMIT),
        cost_estimate=pl.CostEstimate(
            flops=2 * 2 * tile_count * reps * rows * BLOCK * BLOCK,
            bytes_accessed=4 * tile_count * BLOCK * BLOCK,
            transcendentals=0,
        ),
        name="expand",
    )(words, groups, *flat, gain, left, gate_tiles, up_tiles)
    return out[0], out[1], out[2:]


def activate_kernel(reps, own_ref, *refs):
    peers = refs[: reps - 1]
    raw_ref, picks_ref, gate_cols, up_cols, down_cols, hidden_ref, coef_ref = refs[reps - 1 :]
    noise = picks_ref.shape[1]

    @pl.when(pl.program_id(0) == 0)
    def _():
        coef_ref[...] = jnp.zeros_like(coef_ref)

    picks = picks_ref[...]
    coefs = [
        (picks * raw_ref[:, :noise]).astype(jnp.bfloat16),
        (picks * raw_ref[:, noise:]).astype(jnp.bfloat16),
    ]
    down = jnp.zeros(coef_ref.shape, jnp.float32)
    for c in range(own_ref.shape[1]):
        values = []
        for which, cols in ((0, gate_cols), (1, up_cols)):
            value = own_ref[which, c]
            for peer in peers:
                value = value + peer[which, c].astype(jnp.float32)
            values.append(value + jnp.dot(coefs[which], cols[c], preferred_element_type=jnp.float32))
        gate, up = values
        hidden = (gate / (1.0 + jnp.exp(-gate)) * up).astype(jnp.bfloat16)
        hidden_ref[c] = hidden
        down = down + lax.dot_general(
            hidden, down_cols[c], (((1,), (1,)), ((), ())), preferred_element_type=jnp.float32
        )
    coef_ref[...] += picks * down


def activate(own, peers, raw, picks, gate_cols, up_cols, down_cols):
    own_cols, rows = own.shape[1:3]
    noise = picks.shape[1]
    chunk = min(4, own_cols)
    wide = pl.BlockSpec((2, chunk, rows, BLOCK), lambda i: (0, i, 0, 0))
    cols = pl.BlockSpec((chunk, noise, BLOCK), lambda i: (i, 0, 0))
    return pl.pallas_call(
        functools.partial(activate_kernel, len(peers) + 1),
        grid=(own_cols // chunk,),
        out_shape=[
            jax.ShapeDtypeStruct((own_cols, rows, BLOCK), jnp.bfloat16),
            jax.ShapeDtypeStruct((rows, noise), jnp.float32),
        ],
        in_specs=[wide] * (len(peers) + 1)
        + [pl.BlockSpec(raw.shape, lambda i: (0, 0)), pl.BlockSpec(picks.shape, lambda i: (0, 0))]
        + [cols] * 3,
        out_specs=[
            pl.BlockSpec((chunk, rows, BLOCK), lambda i: (i, 0, 0)),
            pl.BlockSpec((rows, noise), lambda i: (0, 0)),
        ],
        compiler_params=pltpu.CompilerParams(vmem_limit_bytes=VMEM_LIMIT),
        name="activate",
    )(own, *peers, raw, picks, gate_cols, up_cols, down_cols)


def contract_kernel(owners, reps, length, words_ref, groups_ref, *refs):
    hiddens = refs[:reps]
    coef_ref, right_ref, tiles_hbm = refs[reps : reps + 3]
    outs = refs[reps + 3 : reps + 3 + owners]
    total_ref, tiles_ref, sem = refs[reps + 3 + owners :]
    tile_count = tiles_hbm.shape[0]
    copy = pltpu.make_async_copy(tiles_hbm, tiles_ref.at[pl.ds(0, tile_count)], sem)
    copy.start()
    tiles_ref[tile_count] = jnp.zeros((BLOCK, BLOCK), tiles_ref.dtype)
    rows = hiddens[0].shape[1]
    width = outs[0].shape[1]
    coef = coef_ref[...]
    high = coef.astype(jnp.bfloat16)
    low = (coef - high.astype(jnp.float32)).astype(jnp.bfloat16)
    for d in range(total_ref.shape[0]):
        right = right_ref[:, pl.ds(d * BLOCK, BLOCK)]
        total_ref[d, pl.ds(0, rows), :] = jnp.dot(high, right, preferred_element_type=jnp.float32) + jnp.dot(
            low, right, preferred_element_type=jnp.float32
        )
        if reps > 1:
            total_ref[d, pl.ds(rows, (reps - 1) * rows), :] = jnp.zeros(((reps - 1) * rows, BLOCK), jnp.float32)
    copy.wait()

    def read(block):
        return jnp.concatenate([hidden[block] for hidden in hiddens], axis=0)

    def add(block, product):
        total_ref[block] += product

    multiply_tiles(words_ref, groups_ref, 2, length, read, tiles_ref, add)
    for owner in range(owners):
        for part in range(width // BLOCK):
            outs[owner][:, pl.ds(part * BLOCK, BLOCK)] = total_ref[owner * (width // BLOCK) + part].astype(
                jnp.bfloat16
            )


def contract(words, groups, hiddens, coef, right, tiles, owners):
    own_cols, rows = hiddens[0].shape[:2]
    reps = len(hiddens)
    features = right.shape[1]
    tile_count = tiles.shape[0]
    smem = pl.BlockSpec(memory_space=pltpu.SMEM)
    vmem = pl.BlockSpec(memory_space=pltpu.VMEM)
    return pl.pallas_call(
        functools.partial(contract_kernel, owners, reps, words.shape[0] // 3),
        out_shape=[jax.ShapeDtypeStruct((reps * rows, features // owners), jnp.bfloat16)] * owners,
        in_specs=[smem, smem] + [vmem] * (reps + 2) + [pl.BlockSpec(memory_space=pl.ANY)],
        out_specs=[vmem] * owners,
        scratch_shapes=[
            pltpu.VMEM((features // BLOCK, reps * rows, BLOCK), jnp.float32),
            pltpu.VMEM((tile_count + 1, BLOCK, BLOCK), jnp.bfloat16),
            pltpu.SemaphoreType.DMA,
        ],
        compiler_params=pltpu.CompilerParams(vmem_limit_bytes=VMEM_LIMIT),
        cost_estimate=pl.CostEstimate(
            flops=2 * tile_count * reps * rows * BLOCK * BLOCK,
            bytes_accessed=2 * tile_count * BLOCK * BLOCK,
            transcendentals=0,
        ),
        name="contract",
    )(words, groups, *hiddens, coef, right, tiles)


def per_device(
    tokens,
    norm_gain,
    gate_tiles,
    up_tiles,
    down_tiles,
    gate_slot,
    up_slot,
    down_slot,
    owned_columns,
    gate_left,
    gate_right,
    up_left,
    up_right,
    down_left,
    down_right,
    row_member,
    member_seed,
):
    section_index = lax.axis_index("section")
    owner_index = lax.axis_index("tensor")
    rep_index = lax.axis_index("rep")
    owners, reps = lax.axis_size("tensor"), lax.axis_size("rep")
    rows, width = tokens.shape
    own_cols = owned_columns.shape[1] // owners
    block_rows = gate_left.shape[2] // BLOCK
    tile_count = gate_tiles.shape[1]

    codes = jnp.stack([gate_slot[0], up_slot[0], down_slot[0]])
    codes = lax.dynamic_slice_in_dim(codes, rep_index * tile_count, tile_count, axis=1)
    words, groups = tile_plan(codes, block_rows, own_cols, owner_index, owners)
    words = words.reshape(-1)

    rotation = lax.rem(owner_index - jnp.arange(owners, dtype=jnp.int32) + owners, owners)

    def rotated(table):
        parts = table.reshape(table.shape[0], owners, width)
        return jnp.take(parts, rotation, axis=1).reshape(table.shape)

    gain = rotated(norm_gain)
    left = rotated(jnp.concatenate([gate_left[0], up_left[0]], axis=0))
    right = rotated(down_right[0])
    columns = lax.dynamic_slice_in_dim(owned_columns[0], owner_index * own_cols, own_cols)

    def owned(table):
        blocked = table.reshape(table.shape[0], -1, BLOCK)
        return jnp.take(blocked, columns, axis=1).transpose(1, 0, 2)

    gate_cols, up_cols, down_cols = owned(gate_right[0]), owned(up_right[0]), owned(down_left[0])
    picks = pick_matrix(row_member, member_seed, gate_left.shape[1])

    def layer(streams, section, target):
        blocks = [streams] + [[hop(s, "tensor", step, section, section) for s in streams] for step in range(1, owners)]
        own, raw, partials = expand(
            words, groups, blocks, gain, left, gate_tiles[0], up_tiles[0], own_cols
        )
        received = [hop(p, "rep", -(g + 1), section, section) for g, p in enumerate(partials)]
        hidden, coef = activate(own, received, raw, picks, gate_cols, up_cols, down_cols)
        hiddens = [hidden] + [hop(hidden, "rep", g, section, section) for g in range(1, reps)]
        outs = contract(words, groups, hiddens, coef, right, down_tiles[0], owners)
        if section == target:
            summed = outs[0].astype(jnp.float32)
        else:
            summed = hop(outs[0], "tensor", 0, section, target).astype(jnp.float32)
        for step in range(1, owners):
            summed = summed + hop(outs[step], "tensor", -step, section, target).astype(jnp.float32)
        return summed

    streams = [tokens] + [hop(tokens, "rep", g, 0, 0) for g in range(1, reps)]
    residuals = [tokens] + [hop(tokens, "rep", g, 1, 1) for g in range(1, reps)]
    summed = layer(streams, 0, 1).astype(jnp.bfloat16)
    arrived = [summed] + [hop(summed, "rep", g, 1, 1) for g in range(1, reps)]
    streams = []
    for g in range(reps):
        value = residuals[g].astype(jnp.float32)
        for step in range(reps):
            at = (g - step) % reps
            value = value + arrived[step][at * rows : (at + 1) * rows].astype(jnp.float32)
        streams.append(value.astype(jnp.bfloat16))
    first = lax.ppermute(streams[0], "section", [(1, 0)])
    summed = layer(streams, 1, 1)
    value = streams[0].astype(jnp.float32) + summed[:rows]
    for g in range(1, reps):
        sent = summed[g * rows : (g + 1) * rows].astype(jnp.bfloat16)
        value = value + hop(sent, "rep", -g, 1, 1).astype(jnp.float32)
    second = value.astype(jnp.bfloat16)
    return jnp.where(section_index == 0, first, second)[None]


def solution(mesh):
    placed = (
        P(("pop", "rep"), "tensor"),
        P("section", None),
        P("section", ("tensor", "rep"), None, None),
        P("section", ("tensor", "rep"), None, None),
        P("section", ("tensor", "rep"), None, None),
        P("section", "tensor"),
        P("section", "tensor"),
        P("section", "tensor"),
        P("section", None),
        P("section", None, None),
        P("section", None, None),
        P("section", None, None),
        P("section", None, None),
        P("section", None, None),
        P("section", None, None),
        P(("pop", "rep")),
        P("pop"),
    )
    return jax.shard_map(
        per_device,
        mesh=mesh,
        in_specs=placed,
        out_specs=P("section", ("pop", "rep"), "tensor"),
        check_vma=False,
    )
```

```python
import functools

import jax
import jax.numpy as jnp
from jax import lax
from jax.experimental import pallas as pl
from jax.experimental.pallas import tpu as pltpu
from jax.sharding import PartitionSpec as P

BLOCK = 128
UNROLL = 16
MIB = 1024 * 1024
SLOW = 4

perturb_scale = 0.5
epsilon = 1e-05


def hop(value, axis, steps, source, target):
    count = lax.axis_size(axis)
    pairs = [(source * count + i, target * count + (i + steps) % count) for i in range(count)]
    return lax.ppermute(value, ("section", axis), pairs)


def pick_matrix(row_member, member_seed, noise_count):
    member_ids = jnp.arange(member_seed.shape[0], dtype=jnp.int32)
    matched = row_member[:, None] == member_ids[None, :]
    seed_of = jnp.sum(jnp.where(matched, member_seed[None, :], 0), axis=1)
    sign_values = (1 - 2 * (row_member % 2)).astype(jnp.float32) * perturb_scale
    noise_ids = jnp.arange(noise_count, dtype=jnp.int32)
    return jnp.where(seed_of[:, None] == noise_ids[None, :], sign_values[:, None], jnp.float32(0.0))


def tile_plan(codes, block_rows, own_cols, owner_index, owners):
    tile_count = codes.shape[1]
    active = codes >= 0
    cleared = jnp.where(active, codes, 0)
    column = cleared // block_rows
    feature = cleared % block_rows
    per_owner = block_rows // owners
    feature = lax.rem(owner_index - feature // per_owner + owners, owners) * per_owner + feature % per_owner
    is_down = jnp.arange(3)[:, None] == 2
    major = jnp.where(is_down, feature, column)
    minor = jnp.where(is_down, column, feature)
    major_count = max(block_rows, own_cols)
    majors = jnp.arange(major_count, dtype=jnp.int32)
    filled = jnp.sum(
        jnp.where(active[:, None, :] & (major[:, None, :] == majors[None, :, None]), 1, 0), axis=2
    )
    padded = 2 * ((filled + 1) // 2)
    before = jnp.sum(jnp.where(majors[None, None, :] < major[:, :, None], padded[:, None, :], 0), axis=2)
    rank = jnp.sum(
        jnp.where(
            active[:, None, :]
            & (major[:, None, :] == major[:, :, None])
            & (minor[:, None, :] < minor[:, :, None]),
            1,
            0,
        ),
        axis=2,
    )
    place = jnp.where(active, before + rank, -1)
    length = tile_count + min(tile_count, major_count)
    group = 2 * UNROLL
    length = -(-length // group) * group
    tile_ids = jnp.arange(tile_count, dtype=jnp.int32)
    words = (tile_ids[None, :] - tile_count) + minor * 4096 + major * 1048576
    spots = jnp.arange(length, dtype=jnp.int32)
    packed = tile_count + jnp.sum(
        jnp.where(place[:, None, :] == spots[None, :, None], words[:, None, :], 0), axis=2
    )
    groups = (jnp.sum(padded, axis=1) + group - 1) // group
    return packed.astype(jnp.int32), groups.astype(jnp.int32)


def multiply_tiles(words_ref, groups_ref, which, length, read, tiles_ref, add):
    def group(i, carry):
        for u in range(UNROLL):
            at = which * length + (i * UNROLL + u) * 2
            first, second = words_ref[at], words_ref[at + 1]
            left = jnp.concatenate([read((first >> 12) & 255), read((second >> 12) & 255)], axis=1)
            right = jnp.concatenate([tiles_ref[first & 4095], tiles_ref[second & 4095]], axis=0)
            add(first >> 20, jnp.dot(left, right, preferred_element_type=jnp.float32))
        return carry

    lax.fori_loop(0, groups_ref[which], group, 0)


def expand_kernel(owners, reps, length, words_ref, groups_ref, *refs):
    blocks = refs[:owners]
    gain_ref, left_ref, gate_hbm, up_hbm, raw_ref = refs[owners : owners + 5]
    part_refs = refs[owners + 5 : owners + 5 + reps]
    x_ref, total_ref, gate_tiles, up_tiles, sems = refs[owners + 5 + reps :]
    tile_count = gate_hbm.shape[0]
    all_rows, width = blocks[0].shape
    rows = all_rows // reps
    per_owner = width // BLOCK
    strip = 48 if all_rows % 48 == 0 else 16

    def norm_rows(i, carry):
        at = pl.ds(pl.multiple_of(i * strip, strip), strip)
        squares = jnp.zeros((strip, BLOCK), jnp.float32)
        for owner in range(owners):
            for part in range(per_owner):
                values = blocks[owner][at, pl.ds(part * BLOCK, BLOCK)].astype(jnp.float32)
                squares = squares + values * values
        total = jnp.sum(squares, axis=1, keepdims=True)
        inverse = lax.rsqrt(total / (owners * width) + epsilon)
        for owner in range(owners):
            for part in range(per_owner):
                values = blocks[owner][at, pl.ds(part * BLOCK, BLOCK)].astype(jnp.float32)
                gain = gain_ref[:, pl.ds(owner * width + part * BLOCK, BLOCK)].astype(jnp.float32)
                x_ref[owner * per_owner + part, at, :] = (values * inverse * gain).astype(jnp.bfloat16)
        return carry

    def read(block):
        return x_ref[block]

    def add(block, product):
        total_ref[block] += product

    @pl.when(groups_ref[3] == 1)
    def _():
        copies = [
            pltpu.make_async_copy(gate_hbm, gate_tiles.at[pl.ds(0, tile_count)], sems.at[0]),
            pltpu.make_async_copy(up_hbm, up_tiles.at[pl.ds(0, tile_count)], sems.at[1]),
        ]
        for copy in copies:
            copy.start()
        gate_tiles[tile_count] = jnp.zeros((BLOCK, BLOCK), gate_tiles.dtype)
        up_tiles[tile_count] = jnp.zeros((BLOCK, BLOCK), up_tiles.dtype)
        lax.fori_loop(0, all_rows // strip, norm_rows, 0)
        raw = jnp.zeros(raw_ref.shape, jnp.float32)
        step = min(8, x_ref.shape[0])
        for d in range(0, x_ref.shape[0], step):
            raw = raw + lax.dot_general(
                jnp.concatenate([x_ref[d + i, pl.ds(0, rows), :] for i in range(step)], axis=1),
                left_ref[:, pl.ds(d * BLOCK, step * BLOCK)],
                (((1,), (1,)), ((), ())),
                preferred_element_type=jnp.float32,
            )
        raw_ref[...] = raw
        for which, tiles in ((0, gate_tiles), (1, up_tiles)):
            total_ref[...] = jnp.zeros(total_ref.shape, jnp.float32)
            copies[which].wait()
            multiply_tiles(words_ref, groups_ref, which, length, read, tiles, add)
            for rep in range(reps):

                def narrow(c, carry, which=which, rep=rep):
                    part_refs[rep][which, c] = total_ref[c, pl.ds(rep * rows, rows), :].astype(jnp.bfloat16)
                    return carry

                lax.fori_loop(0, total_ref.shape[0], narrow, 0, unroll=min(4, total_ref.shape[0]))


def expand(words, groups, blocks, gain, left, gate_tiles, up_tiles, own_cols, reps):
    owners = len(blocks)
    all_rows, width = blocks[0].shape
    rows = all_rows // reps
    tile_count = gate_tiles.shape[0]
    smem = pl.BlockSpec(memory_space=pltpu.SMEM)
    vmem = pl.BlockSpec(memory_space=pltpu.VMEM)
    hbm = pl.BlockSpec(memory_space=pl.ANY)
    out = pl.pallas_call(
        functools.partial(expand_kernel, owners, reps, words.shape[0] // 3),
        out_shape=[jax.ShapeDtypeStruct((rows, left.shape[0]), jnp.float32)]
        + [jax.ShapeDtypeStruct((2, own_cols, rows, BLOCK), jnp.bfloat16)] * reps,
        in_specs=[smem, smem] + [vmem] * (owners + 2) + [hbm, hbm],
        out_specs=[vmem] * (1 + reps),
        scratch_shapes=[
            pltpu.VMEM((owners * width // BLOCK, all_rows, BLOCK), jnp.bfloat16),
            pltpu.VMEM((own_cols, all_rows, BLOCK), jnp.float32),
            pltpu.VMEM((tile_count + 1, BLOCK, BLOCK), jnp.bfloat16),
            pltpu.VMEM((tile_count + 1, BLOCK, BLOCK), jnp.bfloat16),
            pltpu.SemaphoreType.DMA((2,)),
        ],
        compiler_params=pltpu.CompilerParams(vmem_limit_bytes=36 * MIB),
        cost_estimate=pl.CostEstimate(
            flops=SLOW * 2 * 2 * tile_count * all_rows * BLOCK * BLOCK,
            bytes_accessed=4 * tile_count * BLOCK * BLOCK,
            transcendentals=0,
        ),
        name="expand",
    )(words, groups, *blocks, gain, left, gate_tiles, up_tiles)
    return out[0], out[1:]


def activate_kernel(reps, groups_ref, *refs):
    parts = refs[:reps]
    raw_ref, picks_ref, wide_cols, down_cols, hidden_ref, coef_ref = refs[reps:]
    noise = picks_ref.shape[1]
    columns, rows = hidden_ref.shape[:2]

    @pl.when(groups_ref[3] == 1)
    def _():
        picks = picks_ref[...]
        coefs = (jnp.concatenate([picks, picks], axis=1) * raw_ref[...]).astype(jnp.bfloat16)

        def pair(i, down):
            hiddens = []
            for u in range(2):
                c = i * 2 + u
                low_rank = jnp.dot(coefs, wide_cols[c], preferred_element_type=jnp.float32)
                values = []
                for which in range(2):
                    value = low_rank[:, which * BLOCK : (which + 1) * BLOCK]
                    for part in parts:
                        value = value + part[which, c].astype(jnp.float32)
                    values.append(value)
                gate, up = values
                hidden = (gate / (1.0 + jnp.exp(-gate)) * up).astype(jnp.bfloat16)
                hidden_ref[c] = hidden
                hiddens.append(hidden)
            return down + lax.dot_general(
                jnp.concatenate(hiddens, axis=1),
                down_cols[i],
                (((1,), (1,)), ((), ())),
                preferred_element_type=jnp.float32,
            )

        down = lax.fori_loop(
            0, columns // 2, pair, jnp.zeros((rows, noise), jnp.float32), unroll=min(2, columns // 2)
        )
        coef_ref[...] = picks * down


def activate(groups, parts, raw, picks, wide_cols, down_cols):
    own_cols, rows = parts[0].shape[1:3]
    noise = picks.shape[1]
    vmem = pl.BlockSpec(memory_space=pltpu.VMEM)
    return pl.pallas_call(
        functools.partial(activate_kernel, len(parts)),
        out_shape=[
            jax.ShapeDtypeStruct((own_cols, rows, BLOCK), jnp.bfloat16),
            jax.ShapeDtypeStruct((rows, noise), jnp.float32),
        ],
        in_specs=[pl.BlockSpec(memory_space=pltpu.SMEM)] + [vmem] * (len(parts) + 4),
        out_specs=[vmem] * 2,
        compiler_params=pltpu.CompilerParams(vmem_limit_bytes=16 * MIB),
        cost_estimate=pl.CostEstimate(
            flops=100 * own_cols * rows * BLOCK,
            bytes_accessed=(len(parts) * 2 + 1) * 2 * own_cols * rows * BLOCK,
            transcendentals=own_cols * rows * BLOCK,
        ),
        name="activate",
    )(groups, *parts, raw, picks, wide_cols, down_cols)


def contract_kernel(owners, reps, length, words_ref, groups_ref, *refs):
    hiddens = refs[:reps]
    coef_ref, right_ref, tiles_hbm = refs[reps : reps + 3]
    outs = refs[reps + 3 : reps + 3 + owners]
    total_ref, tiles_ref, sem = refs[reps + 3 + owners :]
    tile_count = tiles_hbm.shape[0]
    rows = hiddens[0].shape[1]
    per_owner = outs[0].shape[1] // BLOCK
    blocks = total_ref.shape[0]

    def read(block):
        return jnp.concatenate([hidden[block] for hidden in hiddens], axis=0)

    def add(block, product):
        total_ref[block] += product

    @pl.when(groups_ref[3] == 1)
    def _():
        copy = pltpu.make_async_copy(tiles_hbm, tiles_ref.at[pl.ds(0, tile_count)], sem)
        copy.start()
        tiles_ref[tile_count] = jnp.zeros((BLOCK, BLOCK), tiles_ref.dtype)
        coef = coef_ref[...]
        high = coef.astype(jnp.bfloat16)
        low = (coef - high.astype(jnp.float32)).astype(jnp.bfloat16)
        both = jnp.concatenate([high, low], axis=1)
        for d in range(0, blocks, 2):
            right = right_ref[:, pl.ds(d * BLOCK, 2 * BLOCK)]
            start = jnp.dot(both, right, preferred_element_type=jnp.float32)
            for i in range(2):
                total_ref[d + i, pl.ds(0, rows), :] = start[:, i * BLOCK : (i + 1) * BLOCK]
                if reps > 1:
                    total_ref[d + i, pl.ds(rows, (reps - 1) * rows), :] = jnp.zeros(
                        ((reps - 1) * rows, BLOCK), jnp.float32
                    )
        copy.wait()
        multiply_tiles(words_ref, groups_ref, 2, length, read, tiles_ref, add)
        for owner in range(owners):
            for part in range(per_owner):
                outs[owner][:, pl.ds(part * BLOCK, BLOCK)] = total_ref[owner * per_owner + part].astype(jnp.bfloat16)


def contract(words, groups, hiddens, coef, right, tiles, owners):
    own_cols, rows = hiddens[0].shape[:2]
    reps = len(hiddens)
    features = right.shape[1]
    tile_count = tiles.shape[0]
    smem = pl.BlockSpec(memory_space=pltpu.SMEM)
    vmem = pl.BlockSpec(memory_space=pltpu.VMEM)
    return pl.pallas_call(
        functools.partial(contract_kernel, owners, reps, words.shape[0] // 3),
        out_shape=[jax.ShapeDtypeStruct((reps * rows, features // owners), jnp.bfloat16)] * owners,
        in_specs=[smem, smem] + [vmem] * (reps + 2) + [pl.BlockSpec(memory_space=pl.ANY)],
        out_specs=[vmem] * owners,
        scratch_shapes=[
            pltpu.VMEM((features // BLOCK, reps * rows, BLOCK), jnp.float32),
            pltpu.VMEM((tile_count + 1, BLOCK, BLOCK), jnp.bfloat16),
            pltpu.SemaphoreType.DMA,
        ],
        compiler_params=pltpu.CompilerParams(vmem_limit_bytes=24 * MIB),
        cost_estimate=pl.CostEstimate(
            flops=SLOW * 2 * tile_count * reps * rows * BLOCK * BLOCK,
            bytes_accessed=2 * tile_count * BLOCK * BLOCK,
            transcendentals=0,
        ),
        name="contract",
    )(words, groups, *hiddens, coef, right, tiles)


def per_device(
    tokens,
    norm_gain,
    gate_tiles,
    up_tiles,
    down_tiles,
    gate_slot,
    up_slot,
    down_slot,
    owned_columns,
    gate_left,
    gate_right,
    up_left,
    up_right,
    down_left,
    down_right,
    row_member,
    member_seed,
):
    section_index = lax.axis_index("section")
    owner_index = lax.axis_index("tensor")
    rep_index = lax.axis_index("rep")
    owners, reps = lax.axis_size("tensor"), lax.axis_size("rep")
    rows, width = tokens.shape
    own_cols = owned_columns.shape[1] // owners
    block_rows = gate_left.shape[2] // BLOCK
    tile_count = gate_tiles.shape[1]

    codes = jnp.stack([gate_slot[0], up_slot[0], down_slot[0]])
    codes = lax.dynamic_slice_in_dim(codes, rep_index * tile_count, tile_count, axis=1)
    words, groups = tile_plan(codes, block_rows, own_cols, owner_index, owners)
    words = words.reshape(-1)

    running = [
        jnp.concatenate([groups, (section_index == section).astype(jnp.int32)[None]]) for section in range(2)
    ]

    rotation = lax.rem(owner_index - jnp.arange(owners, dtype=jnp.int32) + owners, owners)

    def rotated(table):
        parts = table.reshape(table.shape[0], owners, width)
        return jnp.take(parts, rotation, axis=1).reshape(table.shape)

    gain = rotated(norm_gain)
    left = rotated(jnp.concatenate([gate_left[0], up_left[0]], axis=0))
    right = rotated(down_right[0])
    right = jnp.concatenate([right, right], axis=0)
    columns = lax.dynamic_slice_in_dim(owned_columns[0], owner_index * own_cols, own_cols)

    def owned(table):
        blocked = table.reshape(table.shape[0], -1, BLOCK)
        return jnp.take(blocked, columns, axis=1).transpose(1, 0, 2)

    gate_cols, up_cols, down_cols = owned(gate_right[0]), owned(up_right[0]), owned(down_left[0])
    empty = jnp.zeros_like(gate_cols)
    wide_cols = jnp.concatenate(
        [jnp.concatenate([gate_cols, empty], axis=2), jnp.concatenate([empty, up_cols], axis=2)], axis=1
    )
    noise = gate_left.shape[1]
    down_cols = down_cols.reshape(own_cols // 2, 2, noise, BLOCK).transpose(0, 2, 1, 3)
    down_cols = down_cols.reshape(own_cols // 2, noise, 2 * BLOCK)
    picks = pick_matrix(row_member, member_seed, noise)

    halves = 2 if rows % 32 == 0 else 1
    half = rows // halves

    def layer(stream, picked, section, target):
        here = running[section]
        blocks = [stream] + [hop(stream, "tensor", step, section, section) for step in range(1, owners)]
        raw, parts = expand(words, here, blocks, gain, left, gate_tiles[0], up_tiles[0], own_cols, reps)
        parts = [parts[0]] + [hop(parts[g], "rep", -g, section, section) for g in range(1, reps)]
        hidden, coef = activate(here, parts, raw, picked, wide_cols, down_cols)
        hiddens = [hidden] + [hop(hidden, "rep", g, section, section) for g in range(1, reps)]
        outs = contract(words, here, hiddens, coef, right, down_tiles[0], owners)
        summed = outs[0] if section == target else hop(outs[0], "tensor", 0, section, target)
        summed = summed.astype(jnp.float32)
        for step in range(1, owners):
            summed = summed + hop(outs[step], "tensor", -step, section, target).astype(jnp.float32)
        return summed

    others = [hop(tokens, "rep", g, 0, 0) for g in range(1, reps)]
    firsts, seconds = [], []
    for h in range(halves):
        cut = slice(h * half, (h + 1) * half)
        stream = jnp.concatenate([value[cut] for value in [tokens] + others], axis=0)
        summed = layer(stream, picks[cut], 0, 1)
        own = tokens[cut].astype(jnp.float32) + summed[:half]
        summed = jnp.concatenate([own, summed[half:]], axis=0).astype(jnp.bfloat16)
        total = summed.astype(jnp.float32)
        for g in range(1, reps):
            arrived = hop(summed, "rep", g, 1, 1).astype(jnp.float32)
            total = total + jnp.roll(arrived, g * half, axis=0)
        stream = total.astype(jnp.bfloat16)
        firsts.append(stream[:half])
        summed = layer(stream, picks[cut], 1, 1)
        value = stream[:half].astype(jnp.float32) + summed[:half]
        for g in range(1, reps):
            sent = summed[g * half : (g + 1) * half].astype(jnp.bfloat16)
            value = value + hop(sent, "rep", -g, 1, 1).astype(jnp.float32)
        seconds.append(value.astype(jnp.bfloat16))
    first = lax.ppermute(jnp.concatenate(firsts, axis=0), "section", [(1, 0)])
    second = jnp.concatenate(seconds, axis=0)
    return jnp.where(section_index == 0, first, second)[None]


def solution(mesh):
    placed = (
        P(("pop", "rep"), "tensor"),
        P("section", None),
        P("section", ("tensor", "rep"), None, None),
        P("section", ("tensor", "rep"), None, None),
        P("section", ("tensor", "rep"), None, None),
        P("section", "tensor"),
        P("section", "tensor"),
        P("section", "tensor"),
        P("section", None),
        P("section", None, None),
        P("section", None, None),
        P("section", None, None),
        P("section", None, None),
        P("section", None, None),
        P("section", None, None),
        P(("pop", "rep")),
        P("pop"),
    )
    return jax.shard_map(
        per_device,
        mesh=mesh,
        in_specs=placed,
        out_specs=P("section", ("pop", "rep"), "tensor"),
        check_vma=False,
    )
```

```python
import functools

import jax
import jax.numpy as jnp
from jax import lax
from jax.experimental import pallas as pl
from jax.experimental.pallas import tpu as pltpu
from jax.sharding import PartitionSpec as P

BLOCK = 128
UNROLL = 16
MIB = 1024 * 1024
VMEM_LIMIT = 56 * MIB
PIECES = 1
SLOW = 4

perturb_scale = 0.5
epsilon = 1e-05


def hop(value, axis, steps):
    count = lax.axis_size(axis)
    return lax.ppermute(value, axis, [(i, (i + steps) % count) for i in range(count)])


def pick_matrix(row_member, member_seed, noise_count):
    member_ids = jnp.arange(member_seed.shape[0], dtype=jnp.int32)
    matched = row_member[:, None] == member_ids[None, :]
    seed_of = jnp.sum(jnp.where(matched, member_seed[None, :], 0), axis=1)
    sign_values = (1 - 2 * (row_member % 2)).astype(jnp.float32) * perturb_scale
    noise_ids = jnp.arange(noise_count, dtype=jnp.int32)
    return jnp.where(seed_of[:, None] == noise_ids[None, :], sign_values[:, None], jnp.float32(0.0))


def tile_plan(codes, block_rows, own_cols, owner_index, owners):
    tile_count = codes.shape[1]
    active = codes >= 0
    cleared = jnp.where(active, codes, 0)
    column = cleared // block_rows
    feature = cleared % block_rows
    per_owner = block_rows // owners
    feature = lax.rem(owner_index - feature // per_owner + owners, owners) * per_owner + feature % per_owner
    is_down = jnp.arange(3)[:, None] == 2
    major = jnp.where(is_down, feature, column)
    minor = jnp.where(is_down, column, feature)
    major_count = max(block_rows, own_cols)
    majors = jnp.arange(major_count, dtype=jnp.int32)
    filled = jnp.sum(
        jnp.where(active[:, None, :] & (major[:, None, :] == majors[None, :, None]), 1, 0), axis=2
    )
    padded = 2 * ((filled + 1) // 2)
    before = jnp.sum(jnp.where(majors[None, None, :] < major[:, :, None], padded[:, None, :], 0), axis=2)
    rank = jnp.sum(
        jnp.where(
            active[:, None, :]
            & (major[:, None, :] == major[:, :, None])
            & (minor[:, None, :] < minor[:, :, None]),
            1,
            0,
        ),
        axis=2,
    )
    place = jnp.where(active, before + rank, -1)
    length = tile_count + min(tile_count, major_count)
    group = 2 * UNROLL
    length = -(-length // group) * group
    tile_ids = jnp.arange(tile_count, dtype=jnp.int32)
    words = (tile_ids[None, :] - tile_count) + minor * 4096 + major * 1048576
    spots = jnp.arange(length, dtype=jnp.int32)
    packed = tile_count + jnp.sum(
        jnp.where(place[:, None, :] == spots[None, :, None], words[:, None, :], 0), axis=2
    )
    groups = (jnp.sum(padded, axis=1) + group - 1) // group
    return packed.astype(jnp.int32), groups.astype(jnp.int32)


def multiply_tiles(words_ref, groups_ref, which, length, read, tiles_ref, add):
    def group(i, carry):
        for u in range(UNROLL):
            at = which * length + (i * UNROLL + u) * 2
            first, second = words_ref[at], words_ref[at + 1]
            left = jnp.concatenate([read((first >> 12) & 255), read((second >> 12) & 255)], axis=1)
            right = jnp.concatenate([tiles_ref[first & 4095], tiles_ref[second & 4095]], axis=0)
            add(first >> 20, jnp.dot(left, right, preferred_element_type=jnp.float32))
        return carry

    lax.fori_loop(0, groups_ref[which], group, 0)


def load_tiles(own, choices, tiles, sem):
    copies = [pltpu.make_async_copy(tiles_hbm, tiles.at[pl.ds(0, tiles_hbm.shape[0])], sem) for tiles_hbm in choices]
    pl.when(own == 1)(copies[0].start)
    pl.when(own != 1)(copies[1].start)
    tiles[tiles.shape[0] - 1] = jnp.zeros((BLOCK, BLOCK), tiles.dtype)
    return copies[0]


def expand_into(words_ref, groups_ref, which, x_ref, tiles, total_ref, part_refs, copy):
    length = words_ref.shape[0] // 3
    rows = part_refs[0].shape[1]
    total_ref[...] = jnp.zeros(total_ref.shape, jnp.float32)
    copy.wait()

    def read(block):
        return x_ref[block]

    def add(block, product):
        total_ref[block] += product

    multiply_tiles(words_ref, groups_ref, which, length, read, tiles, add)
    for rep, part_ref in enumerate(part_refs):

        def narrow(c, carry, rep=rep, part_ref=part_ref):
            part_ref[c] = total_ref[c, pl.ds(rep * rows, rows), :].astype(jnp.bfloat16)
            return carry

        lax.fori_loop(0, total_ref.shape[0], narrow, 0, unroll=min(4, total_ref.shape[0]))


def gate_kernel(owners, reps, words_ref, groups_ref, *refs):
    blocks = refs[:owners]
    gain_ref, left_ref, own_hbm, other_hbm, raw_ref, x_ref = refs[owners : owners + 6]
    part_refs = refs[owners + 6 : owners + 6 + reps]
    total_ref, tiles, sem = refs[owners + 6 + reps :]
    all_rows, width = blocks[0].shape
    rows = all_rows // reps
    per_owner = width // BLOCK
    strip = 48 if all_rows % 48 == 0 else 16
    copy = load_tiles(groups_ref[3], (own_hbm, other_hbm), tiles, sem)

    def norm_rows(i, carry):
        at = pl.ds(pl.multiple_of(i * strip, strip), strip)
        squares = jnp.zeros((strip, BLOCK), jnp.float32)
        for owner in range(owners):
            for part in range(per_owner):
                values = blocks[owner][at, pl.ds(part * BLOCK, BLOCK)].astype(jnp.float32)
                squares = squares + values * values
        total = jnp.sum(squares, axis=1, keepdims=True)
        inverse = lax.rsqrt(total / (owners * width) + epsilon)
        for owner in range(owners):
            for part in range(per_owner):
                values = blocks[owner][at, pl.ds(part * BLOCK, BLOCK)].astype(jnp.float32)
                gain = gain_ref[:, pl.ds(owner * width + part * BLOCK, BLOCK)].astype(jnp.float32)
                x_ref[owner * per_owner + part, at, :] = (values * inverse * gain).astype(jnp.bfloat16)
        return carry

    lax.fori_loop(0, all_rows // strip, norm_rows, 0)
    raw = jnp.zeros(raw_ref.shape, jnp.float32)
    step = min(8, x_ref.shape[0])
    for d in range(0, x_ref.shape[0], step):
        raw = raw + lax.dot_general(
            jnp.concatenate([x_ref[d + i, pl.ds(0, rows), :] for i in range(step)], axis=1),
            left_ref[:, pl.ds(d * BLOCK, step * BLOCK)],
            (((1,), (1,)), ((), ())),
            preferred_element_type=jnp.float32,
        )
    raw_ref[...] = raw
    expand_into(words_ref, groups_ref, 0, x_ref, tiles, total_ref, part_refs, copy)


def up_kernel(reps, words_ref, groups_ref, x_ref, own_hbm, other_hbm, *refs):
    part_refs = refs[:reps]
    total_ref, tiles, sem = refs[reps:]
    copy = load_tiles(groups_ref[3], (own_hbm, other_hbm), tiles, sem)
    expand_into(words_ref, groups_ref, 1, x_ref, tiles, total_ref, part_refs, copy)


SMEM = pl.BlockSpec(memory_space=pltpu.SMEM)
VMEM = pl.BlockSpec(memory_space=pltpu.VMEM)
HBM = pl.BlockSpec(memory_space=pl.ANY)


def tile_cost(tile_count, all_rows):
    return pl.CostEstimate(
        flops=SLOW * 2 * tile_count * all_rows * BLOCK * BLOCK,
        bytes_accessed=2 * tile_count * BLOCK * BLOCK,
        transcendentals=0,
    )


def tile_scratch(tile_count, blocks, all_rows):
    return [
        pltpu.VMEM((blocks, all_rows, BLOCK), jnp.float32),
        pltpu.VMEM((tile_count + 1, BLOCK, BLOCK), jnp.bfloat16),
        pltpu.SemaphoreType.DMA,
    ]


def expand_gate(words, groups, blocks, gain, left, tiles, own_cols, reps):
    owners = len(blocks)
    all_rows, width = blocks[0].shape
    rows = all_rows // reps
    tile_count = tiles[0].shape[0]
    out = pl.pallas_call(
        functools.partial(gate_kernel, owners, reps),
        out_shape=[
            jax.ShapeDtypeStruct((rows, left.shape[0]), jnp.float32),
            jax.ShapeDtypeStruct((owners * width // BLOCK, all_rows, BLOCK), jnp.bfloat16),
        ]
        + [jax.ShapeDtypeStruct((own_cols, rows, BLOCK), jnp.bfloat16)] * reps,
        in_specs=[SMEM, SMEM] + [VMEM] * (owners + 2) + [HBM, HBM],
        out_specs=[VMEM] * (2 + reps),
        scratch_shapes=tile_scratch(tile_count, own_cols, all_rows),
        compiler_params=pltpu.CompilerParams(vmem_limit_bytes=VMEM_LIMIT),
        cost_estimate=tile_cost(tile_count, all_rows),
        name="gate",
    )(words, groups, *blocks, gain, left, *tiles)
    return out[0], out[1], out[2:]


def expand_up(words, groups, x, tiles, own_cols, reps):
    all_rows = x.shape[1]
    rows = all_rows // reps
    tile_count = tiles[0].shape[0]
    return pl.pallas_call(
        functools.partial(up_kernel, reps),
        out_shape=[jax.ShapeDtypeStruct((own_cols, rows, BLOCK), jnp.bfloat16)] * reps,
        in_specs=[SMEM, SMEM, VMEM, HBM, HBM],
        out_specs=[VMEM] * reps,
        scratch_shapes=tile_scratch(tile_count, own_cols, all_rows),
        compiler_params=pltpu.CompilerParams(vmem_limit_bytes=VMEM_LIMIT),
        cost_estimate=tile_cost(tile_count, all_rows),
        name="up",
    )(words, groups, x, *tiles)


def activate_kernel(reps, *refs):
    parts = (refs[:reps], refs[reps : 2 * reps])
    raw_ref, picks_ref, wide_cols, down_cols, hidden_ref, coef_ref = refs[2 * reps :]
    noise = picks_ref.shape[1]
    columns, rows = hidden_ref.shape[:2]
    picks = picks_ref[...]
    coefs = (jnp.concatenate([picks, picks], axis=1) * raw_ref[...]).astype(jnp.bfloat16)

    def pair(i, down):
        hiddens = []
        for u in range(2):
            c = i * 2 + u
            low_rank = jnp.dot(coefs, wide_cols[c], preferred_element_type=jnp.float32)
            values = []
            for which in range(2):
                value = low_rank[:, which * BLOCK : (which + 1) * BLOCK]
                for part in parts[which]:
                    value = value + part[c].astype(jnp.float32)
                values.append(value)
            gate, up = values
            hidden = (gate / (1.0 + jnp.exp(-gate)) * up).astype(jnp.bfloat16)
            hidden_ref[c] = hidden
            hiddens.append(hidden)
        return down + lax.dot_general(
            jnp.concatenate(hiddens, axis=1),
            down_cols[i],
            (((1,), (1,)), ((), ())),
            preferred_element_type=jnp.float32,
        )

    down = lax.fori_loop(
        0, columns // 2, pair, jnp.zeros((rows, noise), jnp.float32), unroll=min(4, columns // 2)
    )
    coef_ref[...] = picks * down


def activate(gates, ups, raw, picks, wide_cols, down_cols):
    own_cols, rows = gates[0].shape[:2]
    noise = picks.shape[1]
    reps = len(gates)
    return pl.pallas_call(
        functools.partial(activate_kernel, reps),
        out_shape=[
            jax.ShapeDtypeStruct((own_cols, rows, BLOCK), jnp.bfloat16),
            jax.ShapeDtypeStruct((rows, noise), jnp.float32),
        ],
        in_specs=[VMEM] * (2 * reps + 4),
        out_specs=[VMEM] * 2,
        compiler_params=pltpu.CompilerParams(vmem_limit_bytes=16 * MIB),
        cost_estimate=pl.CostEstimate(
            flops=100 * own_cols * rows * BLOCK,
            bytes_accessed=(reps * 2 + 1) * 2 * own_cols * rows * BLOCK,
            transcendentals=own_cols * rows * BLOCK,
        ),
        name="activate",
    )(*gates, *ups, raw, picks, wide_cols, down_cols)


def contract_kernel(owners, reps, words_ref, groups_ref, *refs):
    hiddens = refs[:reps]
    coef_ref, right_ref, own_hbm, other_hbm = refs[reps : reps + 4]
    outs = refs[reps + 4 : reps + 4 + owners]
    total_ref, tiles, sem = refs[reps + 4 + owners :]
    rows = hiddens[0].shape[1]
    per_owner = outs[0].shape[1] // BLOCK
    blocks = total_ref.shape[0]
    copy = load_tiles(groups_ref[3], (own_hbm, other_hbm), tiles, sem)

    def read(block):
        return jnp.concatenate([hidden[block] for hidden in hiddens], axis=0)

    def add(block, product):
        total_ref[block] += product

    coef = coef_ref[...]
    high = coef.astype(jnp.bfloat16)
    low = (coef - high.astype(jnp.float32)).astype(jnp.bfloat16)
    right = right_ref[...]
    both = jnp.concatenate([high, low], axis=1)
    twice = jnp.concatenate([right, right], axis=0)
    for d in range(0, blocks, 2):
        start = jnp.dot(both, twice[:, d * BLOCK : (d + 2) * BLOCK], preferred_element_type=jnp.float32)
        for i in range(2):
            total_ref[d + i, pl.ds(0, rows), :] = start[:, i * BLOCK : (i + 1) * BLOCK]
            if reps > 1:
                total_ref[d + i, pl.ds(rows, (reps - 1) * rows), :] = jnp.zeros(
                    ((reps - 1) * rows, BLOCK), jnp.float32
                )
    copy.wait()
    multiply_tiles(words_ref, groups_ref, 2, words_ref.shape[0] // 3, read, tiles, add)
    for owner in range(owners):
        for part in range(per_owner):
            outs[owner][:, pl.ds(part * BLOCK, BLOCK)] = total_ref[owner * per_owner + part].astype(jnp.bfloat16)


def contract(words, groups, hiddens, coef, right, tiles, owners):
    own_cols, rows = hiddens[0].shape[:2]
    reps = len(hiddens)
    features = right.shape[1]
    tile_count = tiles[0].shape[0]
    return pl.pallas_call(
        functools.partial(contract_kernel, owners, reps),
        out_shape=[jax.ShapeDtypeStruct((reps * rows, features // owners), jnp.bfloat16)] * owners,
        in_specs=[SMEM, SMEM] + [VMEM] * (reps + 2) + [HBM, HBM],
        out_specs=[VMEM] * owners,
        scratch_shapes=tile_scratch(tile_count, features // BLOCK, reps * rows),
        compiler_params=pltpu.CompilerParams(vmem_limit_bytes=VMEM_LIMIT),
        cost_estimate=tile_cost(tile_count, reps * rows),
        name="contract",
    )(words, groups, *hiddens, coef, right, *tiles)


def per_device(
    tokens,
    norm_gain,
    gate_tiles,
    up_tiles,
    down_tiles,
    gate_slot,
    up_slot,
    down_slot,
    owned_columns,
    gate_left,
    gate_right,
    up_left,
    up_right,
    down_left,
    down_right,
    row_member,
    member_seed,
):
    section_index = lax.axis_index("section")
    owner_index = lax.axis_index("tensor")
    rep_index = lax.axis_index("rep")
    owners, reps = lax.axis_size("tensor"), lax.axis_size("rep")
    rows, width = tokens.shape
    own_cols = owned_columns.shape[1] // owners
    block_rows = gate_left.shape[2] // BLOCK
    tile_count = gate_tiles.shape[1]

    codes = jnp.stack([gate_slot[0], up_slot[0], down_slot[0]])
    codes = lax.dynamic_slice_in_dim(codes, rep_index * tile_count, tile_count, axis=1)
    words, groups = tile_plan(codes, block_rows, own_cols, owner_index, owners)
    words = words.reshape(-1)

    rotation = lax.rem(owner_index - jnp.arange(owners, dtype=jnp.int32) + owners, owners)
    noise = gate_left.shape[1]

    def rotated(table):
        parts = table.reshape(table.shape[0], owners, width)
        return jnp.take(parts, rotation, axis=1).reshape(table.shape)

    columns = lax.dynamic_slice_in_dim(owned_columns[0], owner_index * own_cols, own_cols)

    def owned(table):
        return jnp.take(table.reshape(table.shape[0], -1, BLOCK), columns, axis=1)

    plan = jnp.concatenate([words, groups])
    wide = rotated(jnp.concatenate([gate_left[0], up_left[0], down_right[0], norm_gain], axis=0))
    cols = owned(jnp.concatenate([gate_right[0], up_right[0], down_left[0]], axis=0))
    mine = (plan, wide, cols)
    theirs = tuple(hop(table, "section", 1) for table in mine)
    gate_pair = (gate_tiles[0], hop(gate_tiles[0], "section", 1))
    up_pair = (up_tiles[0], hop(up_tiles[0], "section", 1))
    down_pair = (down_tiles[0], hop(down_tiles[0], "section", 1))
    picks = pick_matrix(row_member, member_seed, noise)

    def layer(stream, picked, section):
        own = section_index == section
        plan, wide, cols = (jnp.where(own, a, b) for a, b in zip(mine, theirs))
        words = plan[:-3]
        groups = jnp.concatenate([plan[-3:], own.astype(jnp.int32)[None]])
        left, right, gain = wide[: 2 * noise], wide[2 * noise : 3 * noise], wide[3 * noise :]
        gate_cols, up_cols, down_cols = cols[:noise], cols[noise : 2 * noise], cols[2 * noise :]
        empty = jnp.zeros_like(gate_cols)
        wide_cols = jnp.concatenate(
            [jnp.concatenate([gate_cols, empty], axis=2), jnp.concatenate([empty, up_cols], axis=2)], axis=0
        ).transpose(1, 0, 2)
        down_cols = down_cols.reshape(noise, own_cols // 2, 2 * BLOCK).transpose(1, 0, 2)

        blocks = [stream] + [hop(stream, "tensor", step) for step in range(1, owners)]
        raw, x, gates = expand_gate(words, groups, blocks, gain, left, gate_pair, own_cols, reps)
        gates = [gates[0]] + [hop(gates[g], "rep", -g) for g in range(1, reps)]
        ups = expand_up(words, groups, x, up_pair, own_cols, reps)
        ups = [ups[0]] + [hop(ups[g], "rep", -g) for g in range(1, reps)]
        hidden, coef = activate(gates, ups, raw, picked, wide_cols, down_cols)
        hiddens = [hidden] + [hop(hidden, "rep", g) for g in range(1, reps)]
        outs = contract(words, groups, hiddens, coef, right, down_pair, owners)
        summed = outs[0].astype(jnp.float32)
        for step in range(1, owners):
            summed = summed + hop(outs[step], "tensor", -step).astype(jnp.float32)
        return summed

    half = rows // 2
    mine_rows = lax.dynamic_slice_in_dim(tokens, section_index * half, half)
    mine_picks = lax.dynamic_slice_in_dim(picks, section_index * half, half)
    others = [hop(mine_rows, "rep", g) for g in range(1, reps)]
    piece = half // PIECES
    firsts, seconds = [], []
    for h in range(PIECES):
        cut = slice(h * piece, (h + 1) * piece)
        stream = jnp.concatenate([value[cut] for value in [mine_rows] + others], axis=0)
        summed = layer(stream, mine_picks[cut], 0)
        own = stream[:piece].astype(jnp.float32) + summed[:piece]
        summed = jnp.concatenate([own, summed[piece:]], axis=0).astype(jnp.bfloat16)
        total = summed.astype(jnp.float32)
        for g in range(1, reps):
            arrived = hop(summed, "rep", g).astype(jnp.float32)
            total = total + jnp.roll(arrived, g * piece, axis=0)
        stream = total.astype(jnp.bfloat16)
        firsts.append(stream[:piece])
        summed = layer(stream, mine_picks[cut], 1)
        value = stream[:piece].astype(jnp.float32) + summed[:piece]
        for g in range(1, reps):
            sent = summed[g * piece : (g + 1) * piece].astype(jnp.bfloat16)
            value = value + hop(sent, "rep", -g).astype(jnp.float32)
        seconds.append(value.astype(jnp.bfloat16))
    first = jnp.concatenate(firsts, axis=0)
    second = jnp.concatenate(seconds, axis=0)
    kept = jnp.where(section_index == 0, first, second)
    received = hop(jnp.where(section_index == 0, second, first), "section", 1)
    out = jnp.where(
        section_index == 0,
        jnp.concatenate([kept, received], axis=0),
        jnp.concatenate([received, kept], axis=0),
    )
    return out[None]


def solution(mesh):
    placed = (
        P(("pop", "rep"), "tensor"),
        P("section", None),
        P("section", ("tensor", "rep"), None, None),
        P("section", ("tensor", "rep"), None, None),
        P("section", ("tensor", "rep"), None, None),
        P("section", "tensor"),
        P("section", "tensor"),
        P("section", "tensor"),
        P("section", None),
        P("section", None, None),
        P("section", None, None),
        P("section", None, None),
        P("section", None, None),
        P("section", None, None),
        P("section", None, None),
        P(("pop", "rep")),
        P("pop"),
    )
    return jax.shard_map(
        per_device,
        mesh=mesh,
        in_specs=placed,
        out_specs=P("section", ("pop", "rep"), "tensor"),
        check_vma=False,
    )
```

```python
import functools

import jax
import jax.numpy as jnp
from jax import lax
from jax.experimental import pallas as pl
from jax.experimental.pallas import tpu as pltpu
from jax.sharding import PartitionSpec as P

BLOCK = 128
UNROLL = 16
MIB = 1024 * 1024
VMEM_LIMIT = 56 * MIB
PIECES = 2
SLOW = 4

perturb_scale = 0.5
epsilon = 1e-05


def hop(value, axis, steps):
    count = lax.axis_size(axis)
    return lax.ppermute(value, axis, [(i, (i + steps) % count) for i in range(count)])


def pick_matrix(row_member, member_seed, noise_count):
    member_ids = jnp.arange(member_seed.shape[0], dtype=jnp.int32)
    matched = row_member[:, None] == member_ids[None, :]
    seed_of = jnp.sum(jnp.where(matched, member_seed[None, :], 0), axis=1)
    sign_values = (1 - 2 * (row_member % 2)).astype(jnp.float32) * perturb_scale
    noise_ids = jnp.arange(noise_count, dtype=jnp.int32)
    return jnp.where(seed_of[:, None] == noise_ids[None, :], sign_values[:, None], jnp.float32(0.0))


def tile_plan(codes, block_rows, own_cols, owner_index, owners):
    tile_count = codes.shape[1]
    active = codes >= 0
    cleared = jnp.where(active, codes, 0)
    column = cleared // block_rows
    feature = cleared % block_rows
    per_owner = block_rows // owners
    feature = lax.rem(owner_index - feature // per_owner + owners, owners) * per_owner + feature % per_owner
    is_down = jnp.arange(codes.shape[0])[:, None] % 3 == 2
    major = jnp.where(is_down, feature, column)
    minor = jnp.where(is_down, column, feature)
    major_count = max(block_rows, own_cols)
    majors = jnp.arange(major_count, dtype=jnp.int32)
    filled = jnp.sum(
        jnp.where(active[:, None, :] & (major[:, None, :] == majors[None, :, None]), 1, 0), axis=2
    )
    padded = 2 * ((filled + 1) // 2)
    before = jnp.sum(jnp.where(majors[None, None, :] < major[:, :, None], padded[:, None, :], 0), axis=2)
    rank = jnp.sum(
        jnp.where(
            active[:, None, :]
            & (major[:, None, :] == major[:, :, None])
            & (minor[:, None, :] < minor[:, :, None]),
            1,
            0,
        ),
        axis=2,
    )
    place = jnp.where(active, before + rank, -1)
    length = tile_count + min(tile_count, major_count)
    group = 2 * UNROLL
    length = -(-length // group) * group
    tile_ids = jnp.arange(tile_count, dtype=jnp.int32)
    words = (tile_ids[None, :] - tile_count) + minor * 4096 + major * 1048576
    spots = jnp.arange(length, dtype=jnp.int32)
    packed = tile_count + jnp.sum(
        jnp.where(place[:, None, :] == spots[None, :, None], words[:, None, :], 0), axis=2
    )
    groups = (jnp.sum(padded, axis=1) + group - 1) // group
    return packed.astype(jnp.int32), groups.astype(jnp.int32)


def multiply_tiles(words_ref, groups_ref, which, length, read, tiles_ref, add):
    def group(i, carry):
        for u in range(UNROLL):
            at = which * length + (i * UNROLL + u) * 2
            first, second = words_ref[at], words_ref[at + 1]
            left = jnp.concatenate([read((first >> 12) & 255), read((second >> 12) & 255)], axis=1)
            right = jnp.concatenate([tiles_ref[first & 4095], tiles_ref[second & 4095]], axis=0)
            add(first >> 20, jnp.dot(left, right, preferred_element_type=jnp.float32))
        return carry

    lax.fori_loop(0, groups_ref[which], group, 0)


def load_tiles(own, choices, tiles, sem):
    copies = [pltpu.make_async_copy(tiles_hbm, tiles.at[pl.ds(0, tiles_hbm.shape[0])], sem) for tiles_hbm in choices]
    pl.when(own == 1)(copies[0].start)
    pl.when(own != 1)(copies[1].start)
    tiles[tiles.shape[0] - 1] = jnp.zeros((BLOCK, BLOCK), tiles.dtype)
    return copies[0]


def expand_kernel(owners, reps, words_ref, groups_ref, *refs):
    blocks = refs[:owners]
    gain_ref, left_ref, own_gate, other_gate, own_up, other_up, raw_ref = refs[owners : owners + 7]
    part_refs = refs[owners + 7 : owners + 7 + reps]
    total_ref, gate_tiles, gate_sem, up_tiles, up_sem, x_ref = refs[owners + 7 + reps :]
    all_rows, width = blocks[0].shape
    rows = all_rows // reps
    per_owner = width // BLOCK
    strip = 48 if all_rows % 48 == 0 else 16
    gate_copy = load_tiles(groups_ref[3], (own_gate, other_gate), gate_tiles, gate_sem)
    up_copy = load_tiles(groups_ref[3], (own_up, other_up), up_tiles, up_sem)

    def norm_rows(i, carry):
        at = pl.ds(pl.multiple_of(i * strip, strip), strip)
        squares = jnp.zeros((strip, BLOCK), jnp.float32)
        for owner in range(owners):
            for part in range(per_owner):
                values = blocks[owner][at, pl.ds(part * BLOCK, BLOCK)].astype(jnp.float32)
                squares = squares + values * values
        total = jnp.sum(squares, axis=1, keepdims=True)
        inverse = lax.rsqrt(total / (owners * width) + epsilon)
        for owner in range(owners):
            for part in range(per_owner):
                values = blocks[owner][at, pl.ds(part * BLOCK, BLOCK)].astype(jnp.float32)
                gain = gain_ref[:, pl.ds(owner * width + part * BLOCK, BLOCK)].astype(jnp.float32)
                x_ref[owner * per_owner + part, at, :] = (values * inverse * gain).astype(jnp.bfloat16)
        return carry

    lax.fori_loop(0, all_rows // strip, norm_rows, 0)
    raw = jnp.zeros(raw_ref.shape, jnp.float32)
    step = min(8, x_ref.shape[0])
    for d in range(0, x_ref.shape[0], step):
        raw = raw + lax.dot_general(
            jnp.concatenate([x_ref[d + i, pl.ds(0, rows), :] for i in range(step)], axis=1),
            left_ref[:, pl.ds(d * BLOCK, step * BLOCK)],
            (((1,), (1,)), ((), ())),
            preferred_element_type=jnp.float32,
        )
    raw_ref[...] = raw

    def read(block):
        return x_ref[block]

    def add(block, product):
        total_ref[block] += product

    for which, tiles, copy in ((0, gate_tiles, gate_copy), (1, up_tiles, up_copy)):
        total_ref[...] = jnp.zeros(total_ref.shape, jnp.float32)
        copy.wait()
        multiply_tiles(words_ref, groups_ref, which, words_ref.shape[0] // 3, read, tiles, add)
        for rep, part_ref in enumerate(part_refs):

            def narrow(c, carry, which=which, rep=rep, part_ref=part_ref):
                part_ref[which, c] = total_ref[c, pl.ds(rep * rows, rows), :].astype(jnp.bfloat16)
                return carry

            lax.fori_loop(0, total_ref.shape[0], narrow, 0, unroll=min(4, total_ref.shape[0]))


SMEM = pl.BlockSpec(memory_space=pltpu.SMEM)
VMEM = pl.BlockSpec(memory_space=pltpu.VMEM)
HBM = pl.BlockSpec(memory_space=pl.ANY)


def tile_cost(tile_count, all_rows):
    return pl.CostEstimate(
        flops=SLOW * 2 * tile_count * all_rows * BLOCK * BLOCK,
        bytes_accessed=2 * tile_count * BLOCK * BLOCK,
        transcendentals=0,
    )


def tile_scratch(tile_count, blocks, all_rows):
    return [
        pltpu.VMEM((blocks, all_rows, BLOCK), jnp.float32),
        pltpu.VMEM((tile_count + 1, BLOCK, BLOCK), jnp.bfloat16),
        pltpu.SemaphoreType.DMA,
    ]


def expand(words, groups, blocks, gain, left, gate_tiles, up_tiles, own_cols, reps):
    owners = len(blocks)
    all_rows, width = blocks[0].shape
    rows = all_rows // reps
    tile_count = gate_tiles[0].shape[0]
    scratch = tile_scratch(tile_count, own_cols, all_rows)
    out = pl.pallas_call(
        functools.partial(expand_kernel, owners, reps),
        out_shape=[jax.ShapeDtypeStruct((rows, left.shape[0]), jnp.float32)]
        + [jax.ShapeDtypeStruct((2, own_cols, rows, BLOCK), jnp.bfloat16)] * reps,
        in_specs=[SMEM, SMEM] + [VMEM] * (owners + 2) + [HBM] * 4,
        out_specs=[VMEM] * (1 + reps),
        scratch_shapes=scratch
        + scratch[1:]
        + [pltpu.VMEM((owners * width // BLOCK, all_rows, BLOCK), jnp.bfloat16)],
        compiler_params=pltpu.CompilerParams(vmem_limit_bytes=VMEM_LIMIT),
        cost_estimate=tile_cost(2 * tile_count, all_rows),
        name="expand",
    )(words, groups, *blocks, gain, left, *gate_tiles, *up_tiles)
    return out[0], out[1:]


def activate_kernel(reps, *refs):
    parts = refs[:reps]
    raw_ref, picks_ref, wide_cols, down_cols, hidden_ref, coef_ref = refs[reps:]
    noise = picks_ref.shape[1]
    columns, rows = hidden_ref.shape[:2]
    picks = picks_ref[...]
    coefs = (jnp.concatenate([picks, picks], axis=1) * raw_ref[...]).astype(jnp.bfloat16)

    def pair(i, down):
        hiddens = []
        for u in range(2):
            c = i * 2 + u
            low_rank = jnp.dot(coefs, wide_cols[c], preferred_element_type=jnp.float32)
            values = []
            for which in range(2):
                value = low_rank[:, which * BLOCK : (which + 1) * BLOCK]
                for part in parts:
                    value = value + part[which, c].astype(jnp.float32)
                values.append(value)
            gate, up = values
            hidden = (gate / (1.0 + jnp.exp(-gate)) * up).astype(jnp.bfloat16)
            hidden_ref[c] = hidden
            hiddens.append(hidden)
        return down + lax.dot_general(
            jnp.concatenate(hiddens, axis=1),
            down_cols[i],
            (((1,), (1,)), ((), ())),
            preferred_element_type=jnp.float32,
        )

    down = lax.fori_loop(
        0, columns // 2, pair, jnp.zeros((rows, noise), jnp.float32), unroll=min(4, columns // 2)
    )
    coef_ref[...] = picks * down


def activate(parts, raw, picks, wide_cols, down_cols):
    own_cols, rows = parts[0].shape[1:3]
    noise = picks.shape[1]
    reps = len(parts)
    return pl.pallas_call(
        functools.partial(activate_kernel, reps),
        out_shape=[
            jax.ShapeDtypeStruct((own_cols, rows, BLOCK), jnp.bfloat16),
            jax.ShapeDtypeStruct((rows, noise), jnp.float32),
        ],
        in_specs=[VMEM] * (reps + 4),
        out_specs=[VMEM] * 2,
        compiler_params=pltpu.CompilerParams(vmem_limit_bytes=16 * MIB),
        cost_estimate=pl.CostEstimate(
            flops=100 * own_cols * rows * BLOCK,
            bytes_accessed=(reps * 2 + 1) * 2 * own_cols * rows * BLOCK,
            transcendentals=own_cols * rows * BLOCK,
        ),
        name="activate",
    )(*parts, raw, picks, wide_cols, down_cols)


def contract_kernel(owners, reps, words_ref, groups_ref, *refs):
    hiddens = refs[:reps]
    coef_ref, right_ref, own_hbm, other_hbm = refs[reps : reps + 4]
    outs = refs[reps + 4 : reps + 4 + owners]
    total_ref, tiles, sem = refs[reps + 4 + owners :]
    rows = hiddens[0].shape[1]
    per_owner = outs[0].shape[1] // BLOCK
    blocks = total_ref.shape[0]
    copy = load_tiles(groups_ref[3], (own_hbm, other_hbm), tiles, sem)

    def read(block):
        return jnp.concatenate([hidden[block] for hidden in hiddens], axis=0)

    def add(block, product):
        total_ref[block] += product

    coef = coef_ref[...]
    high = coef.astype(jnp.bfloat16)
    low = (coef - high.astype(jnp.float32)).astype(jnp.bfloat16)
    right = right_ref[...]
    both = jnp.concatenate([high, low], axis=1)
    twice = jnp.concatenate([right, right], axis=0)
    for d in range(0, blocks, 2):
        start = jnp.dot(both, twice[:, d * BLOCK : (d + 2) * BLOCK], preferred_element_type=jnp.float32)
        for i in range(2):
            total_ref[d + i, pl.ds(0, rows), :] = start[:, i * BLOCK : (i + 1) * BLOCK]
            if reps > 1:
                total_ref[d + i, pl.ds(rows, (reps - 1) * rows), :] = jnp.zeros(
                    ((reps - 1) * rows, BLOCK), jnp.float32
                )
    copy.wait()
    multiply_tiles(words_ref, groups_ref, 2, words_ref.shape[0] // 3, read, tiles, add)
    for owner in range(owners):
        for part in range(per_owner):
            outs[owner][:, pl.ds(part * BLOCK, BLOCK)] = total_ref[owner * per_owner + part].astype(jnp.bfloat16)


def contract(words, groups, hiddens, coef, right, tiles, owners):
    own_cols, rows = hiddens[0].shape[:2]
    reps = len(hiddens)
    features = right.shape[1]
    tile_count = tiles[0].shape[0]
    return pl.pallas_call(
        functools.partial(contract_kernel, owners, reps),
        out_shape=[jax.ShapeDtypeStruct((reps * rows, features // owners), jnp.bfloat16)] * owners,
        in_specs=[SMEM, SMEM] + [VMEM] * (reps + 2) + [HBM, HBM],
        out_specs=[VMEM] * owners,
        scratch_shapes=tile_scratch(tile_count, features // BLOCK, reps * rows),
        compiler_params=pltpu.CompilerParams(vmem_limit_bytes=VMEM_LIMIT),
        cost_estimate=tile_cost(tile_count, reps * rows),
        name="contract",
    )(words, groups, *hiddens, coef, right, *tiles)


def per_device(
    tokens,
    norm_gain,
    gate_tiles,
    up_tiles,
    down_tiles,
    gate_slot,
    up_slot,
    down_slot,
    owned_columns,
    gate_left,
    gate_right,
    up_left,
    up_right,
    down_left,
    down_right,
    row_member,
    member_seed,
):
    section_index = lax.axis_index("section")
    owner_index = lax.axis_index("tensor")
    rep_index = lax.axis_index("rep")
    owners, reps = lax.axis_size("tensor"), lax.axis_size("rep")
    rows, width = tokens.shape
    own_cols = owned_columns.shape[1] // owners
    block_rows = gate_left.shape[2] // BLOCK
    tile_count = gate_tiles.shape[1]

    codes = jnp.stack([gate_slot[0], up_slot[0], down_slot[0]])
    codes = lax.dynamic_slice_in_dim(codes, rep_index * tile_count, tile_count, axis=1)
    wide = jnp.concatenate([gate_left[0], up_left[0], down_right[0], norm_gain], axis=0)
    other_codes, other_wide = hop(codes, "section", 1), hop(wide, "section", 1)
    other_codes, other_wide, gate_tiles, up_tiles, down_tiles = lax.optimization_barrier(
        (other_codes, other_wide, gate_tiles, up_tiles, down_tiles)
    )
    gate_pair = (gate_tiles[0], hop(gate_tiles[0], "section", 1))
    up_pair = (up_tiles[0], hop(up_tiles[0], "section", 1))
    down_pair = (down_tiles[0], hop(down_tiles[0], "section", 1))

    plans = tile_plan(jnp.concatenate([codes, other_codes]), block_rows, own_cols, owner_index, owners)
    rotation = lax.rem(owner_index - jnp.arange(owners, dtype=jnp.int32) + owners, owners)
    noise = gate_left.shape[1]

    def rotated(table):
        parts = table.reshape(table.shape[0], owners, width)
        return jnp.take(parts, rotation, axis=1).reshape(table.shape)

    columns = lax.dynamic_slice_in_dim(owned_columns[0], owner_index * own_cols, own_cols)

    def owned(table):
        return jnp.take(table.reshape(table.shape[0], -1, BLOCK), columns, axis=1)

    cols = owned(jnp.concatenate([gate_right[0], up_right[0], down_left[0]], axis=0))
    other_cols = hop(cols, "section", 1)
    picks = pick_matrix(row_member, member_seed, noise)

    def tables(section):
        own = section_index == section
        words, groups = (jnp.where(own, table[:3], table[3:]) for table in plans)
        groups = jnp.concatenate([groups, own.astype(jnp.int32)[None]])
        chosen = rotated(jnp.where(own, wide, other_wide))
        left, right, gain = chosen[: 2 * noise], chosen[2 * noise : 3 * noise], chosen[3 * noise :]
        chosen = jnp.where(own, cols, other_cols)
        gate_cols, up_cols, down_cols = chosen[:noise], chosen[noise : 2 * noise], chosen[2 * noise :]
        empty = jnp.zeros_like(gate_cols)
        wide_cols = jnp.concatenate(
            [jnp.concatenate([gate_cols, empty], axis=2), jnp.concatenate([empty, up_cols], axis=2)], axis=0
        ).transpose(1, 0, 2)
        down_cols = down_cols.reshape(noise, own_cols // 2, 2 * BLOCK).transpose(1, 0, 2)
        return words.reshape(-1), groups, left, right, gain, wide_cols, down_cols

    layers = [tables(section) for section in range(2)]

    def layer(stream, picked, section):
        words, groups, left, right, gain, wide_cols, down_cols = layers[section]
        blocks = [stream] + [hop(stream, "tensor", step) for step in range(1, owners)]
        raw, parts = expand(words, groups, blocks, gain, left, gate_pair, up_pair, own_cols, reps)
        parts = [parts[0]] + [hop(parts[g], "rep", -g) for g in range(1, reps)]
        hidden, coef = activate(parts, raw, picked, wide_cols, down_cols)
        hiddens = [hidden] + [hop(hidden, "rep", g) for g in range(1, reps)]
        outs = contract(words, groups, hiddens, coef, right, down_pair, owners)
        summed = outs[0].astype(jnp.float32)
        for step in range(1, owners):
            summed = summed + hop(outs[step], "tensor", -step).astype(jnp.float32)
        return summed

    half = rows // 2
    mine_rows = lax.dynamic_slice_in_dim(tokens, section_index * half, half)
    mine_picks = lax.dynamic_slice_in_dim(picks, section_index * half, half)
    others = [hop(mine_rows, "rep", g) for g in range(1, reps)]
    piece = half // PIECES
    firsts, seconds = [], []
    for h in range(PIECES):
        cut = slice(h * piece, (h + 1) * piece)
        stream = jnp.concatenate([value[cut] for value in [mine_rows] + others], axis=0)
        summed = layer(stream, mine_picks[cut], 0)
        own = stream[:piece].astype(jnp.float32) + summed[:piece]
        summed = jnp.concatenate([own, summed[piece:]], axis=0).astype(jnp.bfloat16)
        total = summed.astype(jnp.float32)
        for g in range(1, reps):
            arrived = hop(summed, "rep", g).astype(jnp.float32)
            total = total + jnp.roll(arrived, g * piece, axis=0)
        stream = total.astype(jnp.bfloat16)
        firsts.append(stream[:piece])
        summed = layer(stream, mine_picks[cut], 1)
        value = stream[:piece].astype(jnp.float32) + summed[:piece]
        for g in range(1, reps):
            sent = summed[g * piece : (g + 1) * piece].astype(jnp.bfloat16)
            value = value + hop(sent, "rep", -g).astype(jnp.float32)
        seconds.append(value.astype(jnp.bfloat16))
    first = jnp.concatenate(firsts, axis=0)
    second = jnp.concatenate(seconds, axis=0)
    kept = jnp.where(section_index == 0, first, second)
    received = hop(jnp.where(section_index == 0, second, first), "section", 1)
    out = jnp.where(
        section_index == 0,
        jnp.concatenate([kept, received], axis=0),
        jnp.concatenate([received, kept], axis=0),
    )
    return out[None]


def solution(mesh):
    placed = (
        P(("pop", "rep"), "tensor"),
        P("section", None),
        P("section", ("tensor", "rep"), None, None),
        P("section", ("tensor", "rep"), None, None),
        P("section", ("tensor", "rep"), None, None),
        P("section", "tensor"),
        P("section", "tensor"),
        P("section", "tensor"),
        P("section", None),
        P("section", None, None),
        P("section", None, None),
        P("section", None, None),
        P("section", None, None),
        P("section", None, None),
        P("section", None, None),
        P(("pop", "rep")),
        P("pop"),
    )
    return jax.shard_map(
        per_device,
        mesh=mesh,
        in_specs=placed,
        out_specs=P("section", ("pop", "rep"), "tensor"),
        check_vma=False,
    )
```

```python
import functools

import jax
import jax.numpy as jnp
from jax import lax
from jax.experimental import pallas as pl
from jax.experimental.pallas import tpu as pltpu
from jax.sharding import PartitionSpec as P

BLOCK = 128
UNROLL = 16
MIB = 1024 * 1024
VMEM_LIMIT = 56 * MIB
PIECES = 2
SLOW = 4

perturb_scale = 0.5
epsilon = 1e-05


def hop(value, axis, steps):
    count = lax.axis_size(axis)
    return lax.ppermute(value, axis, [(i, (i + steps) % count) for i in range(count)])


def pick_matrix(row_member, member_seed, noise_count):
    member_ids = jnp.arange(member_seed.shape[0], dtype=jnp.int32)
    matched = row_member[:, None] == member_ids[None, :]
    seed_of = jnp.sum(jnp.where(matched, member_seed[None, :], 0), axis=1)
    sign_values = (1 - 2 * (row_member % 2)).astype(jnp.float32) * perturb_scale
    noise_ids = jnp.arange(noise_count, dtype=jnp.int32)
    return jnp.where(seed_of[:, None] == noise_ids[None, :], sign_values[:, None], jnp.float32(0.0))


def tile_plan(codes, block_rows, own_cols):
    tile_count = codes.shape[1]
    active = codes >= 0
    cleared = jnp.where(active, codes, 0)
    column = cleared // block_rows
    feature = cleared % block_rows
    is_down = jnp.arange(codes.shape[0])[:, None] % 3 == 2
    major = jnp.where(is_down, feature, column)
    minor = jnp.where(is_down, column, feature)
    major_count = max(block_rows, own_cols)
    majors = jnp.arange(major_count, dtype=jnp.int32)
    filled = jnp.sum(
        jnp.where(active[:, None, :] & (major[:, None, :] == majors[None, :, None]), 1, 0), axis=2
    )
    padded = 2 * ((filled + 1) // 2)
    before = jnp.sum(jnp.where(majors[None, None, :] < major[:, :, None], padded[:, None, :], 0), axis=2)
    rank = jnp.sum(
        jnp.where(
            active[:, None, :]
            & (major[:, None, :] == major[:, :, None])
            & (minor[:, None, :] < minor[:, :, None]),
            1,
            0,
        ),
        axis=2,
    )
    place = jnp.where(active, before + rank, -1)
    length = tile_count + min(tile_count, major_count)
    group = 2 * UNROLL
    length = -(-length // group) * group
    tile_ids = jnp.arange(tile_count, dtype=jnp.int32)
    words = (tile_ids[None, :] - tile_count) + minor * 4096 + major * 1048576
    spots = jnp.arange(length, dtype=jnp.int32)
    packed = tile_count + jnp.sum(
        jnp.where(place[:, None, :] == spots[None, :, None], words[:, None, :], 0), axis=2
    )
    groups = (jnp.sum(padded, axis=1) + group - 1) // group
    return packed.astype(jnp.int32), groups.astype(jnp.int32)


def multiply_tiles(words_ref, groups_ref, which, length, read, tiles_ref, add):
    def group(i, carry):
        for u in range(UNROLL):
            at = which * length + (i * UNROLL + u) * 2
            first, second = words_ref[at], words_ref[at + 1]
            left = jnp.concatenate([read((first >> 12) & 255), read((second >> 12) & 255)], axis=1)
            right = jnp.concatenate([tiles_ref[first & 4095], tiles_ref[second & 4095]], axis=0)
            add(first >> 20, jnp.dot(left, right, preferred_element_type=jnp.float32))
        return carry

    lax.fori_loop(0, groups_ref[which], group, 0)


def load_tiles(own, choices, tiles, sem):
    copies = [pltpu.make_async_copy(tiles_hbm, tiles.at[pl.ds(0, tiles_hbm.shape[0])], sem) for tiles_hbm in choices]
    pl.when(own == 1)(copies[0].start)
    pl.when(own != 1)(copies[1].start)
    tiles[tiles.shape[0] - 1] = jnp.zeros((BLOCK, BLOCK), tiles.dtype)
    return copies[0]


def rows_of(place_ref, reps, rows, steps):
    rep = lax.rem(place_ref[4] + (reps - steps), reps)
    return pl.ds(pl.multiple_of(rep * rows, rows), rows)


def expand_kernel(reps, words_ref, groups_ref, stream_ref, *refs):
    gain_ref, left_ref, own_gate, other_gate, own_up, other_up, raw_ref = refs[:7]
    part_refs = refs[7 : 7 + reps]
    total_ref, gate_tiles, gate_sem, up_tiles, up_sem, x_ref = refs[7 + reps :]
    features = gain_ref.shape[1]
    all_rows = x_ref.shape[1]
    rows = all_rows // reps
    strip = 48 if rows % 48 == 0 else 16
    gate_copy = load_tiles(groups_ref[3], (own_gate, other_gate), gate_tiles, gate_sem)
    up_copy = load_tiles(groups_ref[3], (own_up, other_up), up_tiles, up_sem)

    for rep in range(reps):

        def norm_rows(i, carry, rep=rep):
            start = pl.multiple_of(i * strip, strip)
            at = pl.ds(rep * rows + start, strip)

            def load(d):
                if len(stream_ref.shape) == 2:
                    block = stream_ref[at, pl.ds(d * BLOCK, BLOCK)]
                else:
                    owner, lane = divmod(d * BLOCK, stream_ref.shape[2])
                    owners = features // stream_ref.shape[2]
                    block = stream_ref[rep * owners + owner, pl.ds(start, strip), pl.ds(lane, BLOCK)]
                return block.astype(jnp.float32)

            squares = jnp.zeros((strip, BLOCK), jnp.float32)
            for d in range(features // BLOCK):
                values = load(d)
                squares = squares + values * values
            inverse = lax.rsqrt(jnp.sum(squares, axis=1, keepdims=True) / features + epsilon)
            for d in range(features // BLOCK):
                gain = gain_ref[:, pl.ds(d * BLOCK, BLOCK)].astype(jnp.float32)
                x_ref[d, at, :] = (load(d) * inverse * gain).astype(jnp.bfloat16)
            return carry

        lax.fori_loop(0, rows // strip, norm_rows, 0)
    raw = jnp.zeros(raw_ref.shape, jnp.float32)
    step = min(8, x_ref.shape[0])
    own_rows = rows_of(groups_ref, reps, rows, 0)
    for d in range(0, x_ref.shape[0], step):
        raw = raw + lax.dot_general(
            jnp.concatenate([x_ref[d + i, own_rows, :] for i in range(step)], axis=1),
            left_ref[:, pl.ds(d * BLOCK, step * BLOCK)],
            (((1,), (1,)), ((), ())),
            preferred_element_type=jnp.float32,
        )
    raw_ref[...] = raw

    def read(block):
        return x_ref[block]

    def add(block, product):
        total_ref[block] += product

    for which, tiles, copy in ((0, gate_tiles, gate_copy), (1, up_tiles, up_copy)):
        total_ref[...] = jnp.zeros(total_ref.shape, jnp.float32)
        copy.wait()
        multiply_tiles(words_ref, groups_ref, which, words_ref.shape[0] // 3, read, tiles, add)
        for rep, part_ref in enumerate(part_refs):

            def narrow(c, carry, which=which, rep=rep, part_ref=part_ref):
                part_ref[which, c] = total_ref[c, rows_of(groups_ref, reps, rows, rep), :].astype(jnp.bfloat16)
                return carry

            lax.fori_loop(0, total_ref.shape[0], narrow, 0, unroll=min(4, total_ref.shape[0]))


SMEM = pl.BlockSpec(memory_space=pltpu.SMEM)
VMEM = pl.BlockSpec(memory_space=pltpu.VMEM)
HBM = pl.BlockSpec(memory_space=pl.ANY)


def tile_cost(tile_count, all_rows):
    return pl.CostEstimate(
        flops=SLOW * 2 * tile_count * all_rows * BLOCK * BLOCK,
        bytes_accessed=2 * tile_count * BLOCK * BLOCK,
        transcendentals=0,
    )


def tile_scratch(tile_count, blocks, all_rows):
    return [
        pltpu.VMEM((blocks, all_rows, BLOCK), jnp.float32),
        pltpu.VMEM((tile_count + 1, BLOCK, BLOCK), jnp.bfloat16),
        pltpu.SemaphoreType.DMA,
    ]


def expand(words, groups, stream, gain, left, gate_tiles, up_tiles, own_cols, reps):
    features = gain.shape[1]
    all_rows = stream.size // features
    rows = all_rows // reps
    tile_count = gate_tiles[0].shape[0]
    scratch = tile_scratch(tile_count, own_cols, all_rows)
    out = pl.pallas_call(
        functools.partial(expand_kernel, reps),
        out_shape=[jax.ShapeDtypeStruct((rows, left.shape[0]), jnp.float32)]
        + [jax.ShapeDtypeStruct((2, own_cols, rows, BLOCK), jnp.bfloat16)] * reps,
        in_specs=[SMEM, SMEM] + [VMEM] * 3 + [HBM] * 4,
        out_specs=[VMEM] * (1 + reps),
        scratch_shapes=scratch + scratch[1:] + [pltpu.VMEM((features // BLOCK, all_rows, BLOCK), jnp.bfloat16)],
        compiler_params=pltpu.CompilerParams(vmem_limit_bytes=VMEM_LIMIT),
        cost_estimate=tile_cost(2 * tile_count, all_rows),
        name="expand",
    )(words, groups, stream, gain, left, *gate_tiles, *up_tiles)
    return out[0], out[1:]


def activate_kernel(reps, *refs):
    parts = refs[:reps]
    raw_ref, picks_ref, wide_cols, down_cols, hidden_ref, coef_ref = refs[reps:]
    noise = picks_ref.shape[1]
    columns, rows = hidden_ref.shape[:2]
    picks = picks_ref[...]
    coefs = (jnp.concatenate([picks, picks], axis=1) * raw_ref[...]).astype(jnp.bfloat16)

    def pair(i, down):
        hiddens = []
        for u in range(2):
            c = i * 2 + u
            low_rank = jnp.dot(coefs, wide_cols[c], preferred_element_type=jnp.float32)
            values = []
            for which in range(2):
                value = low_rank[:, which * BLOCK : (which + 1) * BLOCK]
                for part in parts:
                    value = value + part[which, c].astype(jnp.float32)
                values.append(value)
            gate, up = values
            hidden = (gate / (1.0 + jnp.exp(-gate)) * up).astype(jnp.bfloat16)
            hidden_ref[c] = hidden
            hiddens.append(hidden)
        return down + lax.dot_general(
            jnp.concatenate(hiddens, axis=1),
            down_cols[i],
            (((1,), (1,)), ((), ())),
            preferred_element_type=jnp.float32,
        )

    down = lax.fori_loop(
        0, columns // 2, pair, jnp.zeros((rows, noise), jnp.float32), unroll=min(4, columns // 2)
    )
    coef_ref[...] = picks * down


def activate(parts, raw, picks, wide_cols, down_cols):
    own_cols, rows = parts[0].shape[1:3]
    noise = picks.shape[1]
    reps = len(parts)
    return pl.pallas_call(
        functools.partial(activate_kernel, reps),
        out_shape=[
            jax.ShapeDtypeStruct((own_cols, rows, BLOCK), jnp.bfloat16),
            jax.ShapeDtypeStruct((rows, noise), jnp.float32),
        ],
        in_specs=[VMEM] * (reps + 4),
        out_specs=[VMEM] * 2,
        compiler_params=pltpu.CompilerParams(vmem_limit_bytes=16 * MIB),
        cost_estimate=pl.CostEstimate(
            flops=100 * own_cols * rows * BLOCK,
            bytes_accessed=(reps * 2 + 1) * 2 * own_cols * rows * BLOCK,
            transcendentals=own_cols * rows * BLOCK,
        ),
        name="activate",
    )(*parts, raw, picks, wide_cols, down_cols)


def contract_kernel(reps, words_ref, groups_ref, *refs):
    hiddens = refs[:reps]
    coef_ref, right_ref, residual_ref, own_hbm, other_hbm, out_ref = refs[reps : reps + 6]
    total_ref, tiles, sem, hidden_ref = refs[reps + 6 :]
    columns, rows = hiddens[0].shape[:2]
    blocks = total_ref.shape[0]
    copy = load_tiles(groups_ref[3], (own_hbm, other_hbm), tiles, sem)

    def read(block):
        return hidden_ref[block]

    def add(block, product):
        total_ref[block] += product

    for rep, part_ref in enumerate(hiddens):

        def gather(c, carry, rep=rep, part_ref=part_ref):
            hidden_ref[c, rows_of(groups_ref, reps, rows, rep), :] = part_ref[c]
            return carry

        lax.fori_loop(0, columns, gather, 0, unroll=min(4, columns))

    own_rows = rows_of(groups_ref, reps, rows, 0)
    coef = coef_ref[...]
    high = coef.astype(jnp.bfloat16)
    low = (coef - high.astype(jnp.float32)).astype(jnp.bfloat16)
    right = right_ref[...]
    both = jnp.concatenate([high, low], axis=1)
    twice = jnp.concatenate([right, right], axis=0)
    total_ref[...] = jnp.zeros(total_ref.shape, jnp.float32)
    for d in range(0, blocks, 2):
        start = jnp.dot(both, twice[:, d * BLOCK : (d + 2) * BLOCK], preferred_element_type=jnp.float32)
        for i in range(2):
            total_ref[d + i, own_rows, :] = start[:, i * BLOCK : (i + 1) * BLOCK]
    own_blocks = residual_ref.shape[1] // BLOCK
    for i in range(own_blocks):
        total_ref[groups_ref[5] * own_blocks + i, own_rows, :] += residual_ref[
            :, pl.ds(i * BLOCK, BLOCK)
        ].astype(jnp.float32)
    copy.wait()
    multiply_tiles(words_ref, groups_ref, 2, words_ref.shape[0] // 3, read, tiles, add)
    for d in range(blocks):
        out_ref[:, pl.ds(d * BLOCK, BLOCK)] = total_ref[d].astype(jnp.bfloat16)


def contract(words, groups, hiddens, coef, right, residual, tiles):
    own_cols, rows = hiddens[0].shape[:2]
    reps = len(hiddens)
    features = right.shape[1]
    tile_count = tiles[0].shape[0]
    return pl.pallas_call(
        functools.partial(contract_kernel, reps),
        out_shape=jax.ShapeDtypeStruct((reps * rows, features), jnp.bfloat16),
        in_specs=[SMEM, SMEM] + [VMEM] * (reps + 3) + [HBM, HBM],
        out_specs=VMEM,
        scratch_shapes=tile_scratch(tile_count, features // BLOCK, reps * rows)
        + [pltpu.VMEM((own_cols, reps * rows, BLOCK), jnp.bfloat16)],
        compiler_params=pltpu.CompilerParams(vmem_limit_bytes=VMEM_LIMIT),
        cost_estimate=tile_cost(tile_count, reps * rows),
        name="contract",
    )(words, groups, *hiddens, coef, right, residual, *tiles)


def per_device(
    tokens,
    norm_gain,
    gate_tiles,
    up_tiles,
    down_tiles,
    gate_slot,
    up_slot,
    down_slot,
    owned_columns,
    gate_left,
    gate_right,
    up_left,
    up_right,
    down_left,
    down_right,
    row_member,
    member_seed,
):
    section_index = lax.axis_index("section")
    owner_index = lax.axis_index("tensor")
    rep_index = lax.axis_index("rep")
    owners, reps = lax.axis_size("tensor"), lax.axis_size("rep")
    rows, width = tokens.shape
    own_cols = owned_columns.shape[1] // owners
    block_rows = gate_left.shape[2] // BLOCK
    tile_count = gate_tiles.shape[1]

    codes = jnp.stack([gate_slot[0], up_slot[0], down_slot[0]])
    codes = lax.dynamic_slice_in_dim(codes, rep_index * tile_count, tile_count, axis=1)
    wide = jnp.concatenate([gate_left[0], up_left[0], down_right[0], norm_gain], axis=0)
    other_codes, other_wide = hop(codes, "section", 1), hop(wide, "section", 1)
    other_codes, other_wide, gate_tiles, up_tiles, down_tiles = lax.optimization_barrier(
        (other_codes, other_wide, gate_tiles, up_tiles, down_tiles)
    )
    gate_pair = (gate_tiles[0], hop(gate_tiles[0], "section", 1))
    up_pair = (up_tiles[0], hop(up_tiles[0], "section", 1))
    down_pair = (down_tiles[0], hop(down_tiles[0], "section", 1))

    plans = tile_plan(jnp.concatenate([codes, other_codes]), block_rows, own_cols)
    noise = gate_left.shape[1]

    columns = lax.dynamic_slice_in_dim(owned_columns[0], owner_index * own_cols, own_cols)

    def owned(table):
        return jnp.take(table.reshape(table.shape[0], -1, BLOCK), columns, axis=1)

    cols = owned(jnp.concatenate([gate_right[0], up_right[0], down_left[0]], axis=0))
    other_cols = hop(cols, "section", 1)
    picks = pick_matrix(row_member, member_seed, noise)

    def tables(section):
        own = section_index == section
        words, groups = (jnp.where(own, table[:3], table[3:]) for table in plans)
        groups = jnp.concatenate([groups, jnp.stack([own.astype(jnp.int32), rep_index, owner_index])])
        chosen = jnp.where(own, wide, other_wide)
        left, right, gain = chosen[: 2 * noise], chosen[2 * noise : 3 * noise], chosen[3 * noise :]
        chosen = jnp.where(own, cols, other_cols)
        gate_cols, up_cols, down_cols = chosen[:noise], chosen[noise : 2 * noise], chosen[2 * noise :]
        empty = jnp.zeros_like(gate_cols)
        wide_cols = jnp.concatenate(
            [jnp.concatenate([gate_cols, empty], axis=2), jnp.concatenate([empty, up_cols], axis=2)], axis=0
        ).transpose(1, 0, 2)
        down_cols = down_cols.reshape(noise, own_cols // 2, 2 * BLOCK).transpose(1, 0, 2)
        return words.reshape(-1), groups, left, right, gain, wide_cols, down_cols

    layers = [tables(section) for section in range(2)]

    def layer(stream, residual, picked, section):
        words, groups, left, right, gain, wide_cols, down_cols = layers[section]
        raw, parts = expand(words, groups, stream, gain, left, gate_pair, up_pair, own_cols, reps)
        parts = [parts[0]] + [hop(parts[g], "rep", -g) for g in range(1, reps)]
        hidden, coef = activate(parts, raw, picked, wide_cols, down_cols)
        hiddens = [hidden] + [hop(hidden, "rep", g) for g in range(1, reps)]
        return contract(words, groups, hiddens, coef, right, residual, down_pair)

    half = rows // 2
    mine_rows = lax.dynamic_slice_in_dim(tokens, section_index * half, half)
    mine_picks = lax.dynamic_slice_in_dim(picks, section_index * half, half)
    piece = half // PIECES
    firsts, seconds = [], []
    for h in range(PIECES):
        cut = slice(h * piece, (h + 1) * piece)
        residual = mine_rows[cut]
        stream = lax.all_gather(residual, ("rep", "tensor"))
        partial = layer(stream, residual, mine_picks[cut], 0)
        if h > 0:
            partial, last = lax.optimization_barrier((partial, last))
        stream = lax.psum(partial, ("tensor", "rep"))
        last = stream
        residual = lax.dynamic_slice(stream, (rep_index * piece, owner_index * width), (piece, width))
        firsts.append(residual)
        partial = layer(stream, residual, mine_picks[cut], 1)
        summed = lax.psum_scatter(partial, "tensor", scatter_dimension=1, tiled=True)
        value = lax.dynamic_slice_in_dim(summed, rep_index * piece, piece).astype(jnp.float32)
        for g in range(1, reps):
            to = lax.rem(rep_index + (reps - g), reps)
            sent = lax.dynamic_slice_in_dim(summed, to * piece, piece)
            value = value + hop(sent, "rep", -g).astype(jnp.float32)
        seconds.append(value.astype(jnp.bfloat16))
    first = jnp.concatenate(firsts, axis=0)
    second = jnp.concatenate(seconds, axis=0)
    kept = jnp.where(section_index == 0, first, second)
    received = hop(jnp.where(section_index == 0, second, first), "section", 1)
    out = jnp.where(
        section_index == 0,
        jnp.concatenate([kept, received], axis=0),
        jnp.concatenate([received, kept], axis=0),
    )
    return out[None]


def solution(mesh):
    placed = (
        P(("pop", "rep"), "tensor"),
        P("section", None),
        P("section", ("tensor", "rep"), None, None),
        P("section", ("tensor", "rep"), None, None),
        P("section", ("tensor", "rep"), None, None),
        P("section", "tensor"),
        P("section", "tensor"),
        P("section", "tensor"),
        P("section", None),
        P("section", None, None),
        P("section", None, None),
        P("section", None, None),
        P("section", None, None),
        P("section", None, None),
        P("section", None, None),
        P(("pop", "rep")),
        P("pop"),
    )
    return jax.shard_map(
        per_device,
        mesh=mesh,
        in_specs=placed,
        out_specs=P("section", ("pop", "rep"), "tensor"),
        check_vma=False,
    )
```

```python
import functools

import jax
import jax.numpy as jnp
from jax import lax
from jax.experimental import pallas as pl
from jax.experimental.pallas import tpu as pltpu
from jax.sharding import PartitionSpec as P

BLOCK = 128
UNROLL = 16
MIB = 1024 * 1024
VMEM_LIMIT = 56 * MIB
SLOW = 4

perturb_scale = 0.5
epsilon = 1e-05


def hop(value, axis, steps):
    count = lax.axis_size(axis)
    return lax.ppermute(value, axis, [(i, (i + steps) % count) for i in range(count)])


def hop_within(section, value, axis, steps):
    count = lax.axis_size(axis)
    base = section * count
    return lax.ppermute(value, ("section", axis), [(base + i, base + (i + steps) % count) for i in range(count)])


def pick_matrix(row_member, member_seed, noise_count):
    member_ids = jnp.arange(member_seed.shape[0], dtype=jnp.int32)
    matched = row_member[:, None] == member_ids[None, :]
    seed_of = jnp.sum(jnp.where(matched, member_seed[None, :], 0), axis=1)
    sign_values = (1 - 2 * (row_member % 2)).astype(jnp.float32) * perturb_scale
    noise_ids = jnp.arange(noise_count, dtype=jnp.int32)
    return jnp.where(seed_of[:, None] == noise_ids[None, :], sign_values[:, None], jnp.float32(0.0))


def tile_plan(codes, block_rows, own_cols, owner_index, owners):
    tile_count = codes.shape[1]
    active = codes >= 0
    cleared = jnp.where(active, codes, 0)
    column = cleared // block_rows
    feature = cleared % block_rows
    per_owner = block_rows // owners
    feature = lax.rem(owner_index - feature // per_owner + owners, owners) * per_owner + feature % per_owner
    is_down = jnp.arange(codes.shape[0])[:, None] % 3 == 2
    major = jnp.where(is_down, feature, column)
    minor = jnp.where(is_down, column, feature)
    major_count = max(block_rows, own_cols)
    majors = jnp.arange(major_count, dtype=jnp.int32)
    filled = jnp.sum(
        jnp.where(active[:, None, :] & (major[:, None, :] == majors[None, :, None]), 1, 0), axis=2
    )
    padded = 2 * ((filled + 1) // 2)
    before = jnp.sum(jnp.where(majors[None, None, :] < major[:, :, None], padded[:, None, :], 0), axis=2)
    rank = jnp.sum(
        jnp.where(
            active[:, None, :]
            & (major[:, None, :] == major[:, :, None])
            & (minor[:, None, :] < minor[:, :, None]),
            1,
            0,
        ),
        axis=2,
    )
    place = jnp.where(active, before + rank, -1)
    length = tile_count + min(tile_count, major_count)
    group = 2 * UNROLL
    length = -(-length // group) * group
    tile_ids = jnp.arange(tile_count, dtype=jnp.int32)
    words = (tile_ids[None, :] - tile_count) + minor * 4096 + major * 1048576
    spots = jnp.arange(length, dtype=jnp.int32)
    packed = tile_count + jnp.sum(
        jnp.where(place[:, None, :] == spots[None, :, None], words[:, None, :], 0), axis=2
    )
    groups = (jnp.sum(padded, axis=1) + group - 1) // group
    return packed.astype(jnp.int32), groups.astype(jnp.int32)


def multiply_tiles(words_ref, groups_ref, which, length, read, tiles_ref, add):
    def group(i, carry):
        for u in range(UNROLL):
            at = which * length + (i * UNROLL + u) * 2
            first, second = words_ref[at], words_ref[at + 1]
            left = jnp.concatenate([read((first >> 12) & 255), read((second >> 12) & 255)], axis=1)
            right = jnp.concatenate([tiles_ref[first & 4095], tiles_ref[second & 4095]], axis=0)
            add(first >> 20, jnp.dot(left, right, preferred_element_type=jnp.float32))
        return carry

    lax.fori_loop(0, groups_ref[which], group, 0)


def load_tiles(own, choices, tiles, sem):
    copies = [pltpu.make_async_copy(tiles_hbm, tiles.at[pl.ds(0, tiles_hbm.shape[0])], sem) for tiles_hbm in choices]
    pl.when(own == 1)(copies[0].start)
    pl.when(own != 1)(copies[1].start)
    tiles[tiles.shape[0] - 1] = jnp.zeros((BLOCK, BLOCK), tiles.dtype)
    return copies[0]


def expand_kernel(owners, reps, words_ref, groups_ref, *refs):
    blocks = refs[:owners]
    gain_ref, left_ref, own_gate, other_gate, own_up, other_up, raw_ref = refs[owners : owners + 7]
    part_refs = refs[owners + 7 : owners + 7 + reps]
    total_ref, gate_tiles, gate_sem, up_tiles, up_sem, x_ref = refs[owners + 7 + reps :]
    all_rows, width = blocks[0].shape
    rows = all_rows // reps
    per_owner = width // BLOCK
    strip = 48 if all_rows % 48 == 0 else 16
    gate_copy = load_tiles(groups_ref[3], (own_gate, other_gate), gate_tiles, gate_sem)
    up_copy = load_tiles(groups_ref[3], (own_up, other_up), up_tiles, up_sem)

    def norm_rows(i, carry):
        at = pl.ds(pl.multiple_of(i * strip, strip), strip)
        squares = jnp.zeros((strip, BLOCK), jnp.float32)
        for owner in range(owners):
            for part in range(per_owner):
                values = blocks[owner][at, pl.ds(part * BLOCK, BLOCK)].astype(jnp.float32)
                squares = squares + values * values
        total = jnp.sum(squares, axis=1, keepdims=True)
        inverse = lax.rsqrt(total / (owners * width) + epsilon)
        for owner in range(owners):
            for part in range(per_owner):
                values = blocks[owner][at, pl.ds(part * BLOCK, BLOCK)].astype(jnp.float32)
                gain = gain_ref[:, pl.ds(owner * width + part * BLOCK, BLOCK)].astype(jnp.float32)
                x_ref[owner * per_owner + part, at, :] = (values * inverse * gain).astype(jnp.bfloat16)
        return carry

    lax.fori_loop(0, all_rows // strip, norm_rows, 0)
    raw = jnp.zeros(raw_ref.shape, jnp.float32)
    step = min(8, x_ref.shape[0])
    for d in range(0, x_ref.shape[0], step):
        raw = raw + lax.dot_general(
            jnp.concatenate([x_ref[d + i, pl.ds(0, rows), :] for i in range(step)], axis=1),
            left_ref[:, pl.ds(d * BLOCK, step * BLOCK)],
            (((1,), (1,)), ((), ())),
            preferred_element_type=jnp.float32,
        )
    raw_ref[...] = raw

    def read(block):
        return x_ref[block]

    def add(block, product):
        total_ref[block] += product

    for which, tiles, copy in ((0, gate_tiles, gate_copy), (1, up_tiles, up_copy)):
        total_ref[...] = jnp.zeros(total_ref.shape, jnp.float32)
        copy.wait()
        multiply_tiles(words_ref, groups_ref, which, words_ref.shape[0] // 3, read, tiles, add)
        for rep, part_ref in enumerate(part_refs):

            def narrow(c, carry, which=which, rep=rep, part_ref=part_ref):
                part_ref[which, c] = total_ref[c, pl.ds(rep * rows, rows), :].astype(jnp.bfloat16)
                return carry

            lax.fori_loop(0, total_ref.shape[0], narrow, 0, unroll=min(4, total_ref.shape[0]))


SMEM = pl.BlockSpec(memory_space=pltpu.SMEM)
VMEM = pl.BlockSpec(memory_space=pltpu.VMEM)
HBM = pl.BlockSpec(memory_space=pl.ANY)


def tile_cost(tile_count, all_rows):
    return pl.CostEstimate(
        flops=SLOW * 2 * tile_count * all_rows * BLOCK * BLOCK,
        bytes_accessed=2 * tile_count * BLOCK * BLOCK,
        transcendentals=0,
    )


def tile_scratch(tile_count, blocks, all_rows):
    return [
        pltpu.VMEM((blocks, all_rows, BLOCK), jnp.float32),
        pltpu.VMEM((tile_count + 1, BLOCK, BLOCK), jnp.bfloat16),
        pltpu.SemaphoreType.DMA,
    ]


def expand(words, groups, blocks, gain, left, gate_tiles, up_tiles, own_cols, reps):
    owners = len(blocks)
    all_rows, width = blocks[0].shape
    rows = all_rows // reps
    tile_count = gate_tiles[0].shape[0]
    scratch = tile_scratch(tile_count, own_cols, all_rows)
    out = pl.pallas_call(
        functools.partial(expand_kernel, owners, reps),
        out_shape=[jax.ShapeDtypeStruct((rows, left.shape[0]), jnp.float32)]
        + [jax.ShapeDtypeStruct((2, own_cols, rows, BLOCK), jnp.bfloat16)] * reps,
        in_specs=[SMEM, SMEM] + [VMEM] * (owners + 2) + [HBM] * 4,
        out_specs=[VMEM] * (1 + reps),
        scratch_shapes=scratch
        + scratch[1:]
        + [pltpu.VMEM((owners * width // BLOCK, all_rows, BLOCK), jnp.bfloat16)],
        compiler_params=pltpu.CompilerParams(vmem_limit_bytes=VMEM_LIMIT),
        cost_estimate=tile_cost(2 * tile_count, all_rows),
        name="expand",
    )(words, groups, *blocks, gain, left, *gate_tiles, *up_tiles)
    return out[0], out[1:]


def activate_kernel(reps, *refs):
    parts = refs[:reps]
    raw_ref, picks_ref, wide_cols, down_cols, hidden_ref, coef_ref = refs[reps:]
    noise = picks_ref.shape[1]
    columns, rows = hidden_ref.shape[:2]
    picks = picks_ref[...]
    coefs = (jnp.concatenate([picks, picks], axis=1) * raw_ref[...]).astype(jnp.bfloat16)

    def pair(i, down):
        hiddens = []
        for u in range(2):
            c = i * 2 + u
            low_rank = jnp.dot(coefs, wide_cols[c], preferred_element_type=jnp.float32)
            values = []
            for which in range(2):
                value = low_rank[:, which * BLOCK : (which + 1) * BLOCK]
                for part in parts:
                    value = value + part[which, c].astype(jnp.float32)
                values.append(value)
            gate, up = values
            hidden = (gate / (1.0 + jnp.exp(-gate)) * up).astype(jnp.bfloat16)
            hidden_ref[c] = hidden
            hiddens.append(hidden)
        return down + lax.dot_general(
            jnp.concatenate(hiddens, axis=1),
            down_cols[i],
            (((1,), (1,)), ((), ())),
            preferred_element_type=jnp.float32,
        )

    down = lax.fori_loop(
        0, columns // 2, pair, jnp.zeros((rows, noise), jnp.float32), unroll=min(4, columns // 2)
    )
    coef_ref[...] = picks * down


def activate(parts, raw, picks, wide_cols, down_cols):
    own_cols, rows = parts[0].shape[1:3]
    noise = picks.shape[1]
    reps = len(parts)
    return pl.pallas_call(
        functools.partial(activate_kernel, reps),
        out_shape=[
            jax.ShapeDtypeStruct((own_cols, rows, BLOCK), jnp.bfloat16),
            jax.ShapeDtypeStruct((rows, noise), jnp.float32),
        ],
        in_specs=[VMEM] * (reps + 4),
        out_specs=[VMEM] * 2,
        compiler_params=pltpu.CompilerParams(vmem_limit_bytes=16 * MIB),
        cost_estimate=pl.CostEstimate(
            flops=100 * own_cols * rows * BLOCK,
            bytes_accessed=(reps * 2 + 1) * 2 * own_cols * rows * BLOCK,
            transcendentals=own_cols * rows * BLOCK,
        ),
        name="activate",
    )(*parts, raw, picks, wide_cols, down_cols)


def contract_kernel(owners, reps, words_ref, groups_ref, *refs):
    hiddens = refs[:reps]
    coef_ref, right_ref, own_hbm, other_hbm = refs[reps : reps + 4]
    outs = refs[reps + 4 : reps + 4 + owners]
    total_ref, tiles, sem = refs[reps + 4 + owners :]
    rows = hiddens[0].shape[1]
    per_owner = outs[0].shape[1] // BLOCK
    blocks = total_ref.shape[0]
    copy = load_tiles(groups_ref[3], (own_hbm, other_hbm), tiles, sem)

    def read(block):
        return jnp.concatenate([hidden[block] for hidden in hiddens], axis=0)

    def add(block, product):
        total_ref[block] += product

    coef = coef_ref[...]
    high = coef.astype(jnp.bfloat16)
    low = (coef - high.astype(jnp.float32)).astype(jnp.bfloat16)
    right = right_ref[...]
    both = jnp.concatenate([high, low], axis=1)
    twice = jnp.concatenate([right, right], axis=0)
    for d in range(0, blocks, 2):
        start = jnp.dot(both, twice[:, d * BLOCK : (d + 2) * BLOCK], preferred_element_type=jnp.float32)
        for i in range(2):
            total_ref[d + i, pl.ds(0, rows), :] = start[:, i * BLOCK : (i + 1) * BLOCK]
            if reps > 1:
                total_ref[d + i, pl.ds(rows, (reps - 1) * rows), :] = jnp.zeros(
                    ((reps - 1) * rows, BLOCK), jnp.float32
                )
    copy.wait()
    multiply_tiles(words_ref, groups_ref, 2, words_ref.shape[0] // 3, read, tiles, add)
    for owner in range(owners):
        for part in range(per_owner):
            outs[owner][:, pl.ds(part * BLOCK, BLOCK)] = total_ref[owner * per_owner + part].astype(jnp.bfloat16)


def contract(words, groups, hiddens, coef, right, tiles, owners):
    own_cols, rows = hiddens[0].shape[:2]
    reps = len(hiddens)
    features = right.shape[1]
    tile_count = tiles[0].shape[0]
    return pl.pallas_call(
        functools.partial(contract_kernel, owners, reps),
        out_shape=[jax.ShapeDtypeStruct((reps * rows, features // owners), jnp.bfloat16)] * owners,
        in_specs=[SMEM, SMEM] + [VMEM] * (reps + 2) + [HBM, HBM],
        out_specs=[VMEM] * owners,
        scratch_shapes=tile_scratch(tile_count, features // BLOCK, reps * rows),
        compiler_params=pltpu.CompilerParams(vmem_limit_bytes=VMEM_LIMIT),
        cost_estimate=tile_cost(tile_count, reps * rows),
        name="contract",
    )(words, groups, *hiddens, coef, right, *tiles)


def per_device(
    tokens,
    norm_gain,
    gate_tiles,
    up_tiles,
    down_tiles,
    gate_slot,
    up_slot,
    down_slot,
    owned_columns,
    gate_left,
    gate_right,
    up_left,
    up_right,
    down_left,
    down_right,
    row_member,
    member_seed,
):
    section_index = lax.axis_index("section")
    owner_index = lax.axis_index("tensor")
    rep_index = lax.axis_index("rep")
    owners, reps = lax.axis_size("tensor"), lax.axis_size("rep")
    rows, width = tokens.shape
    own_cols = owned_columns.shape[1] // owners
    block_rows = gate_left.shape[2] // BLOCK
    tile_count = gate_tiles.shape[1]

    half = rows // 2
    mine_rows = lax.dynamic_slice_in_dim(tokens, section_index * half, half)
    others = [hop(mine_rows, "rep", g) for g in range(1, reps)]
    stream = jnp.concatenate([mine_rows] + others, axis=0)

    codes = jnp.stack([gate_slot[0], up_slot[0], down_slot[0]])
    codes = lax.dynamic_slice_in_dim(codes, rep_index * tile_count, tile_count, axis=1)
    wide = jnp.concatenate([gate_left[0], up_left[0], down_right[0], norm_gain], axis=0)
    codes, wide, stream = lax.optimization_barrier((codes, wide, stream))
    other_codes, other_wide = hop(codes, "section", 1), hop(wide, "section", 1)
    other_codes, other_wide, gate_tiles, up_tiles, down_tiles = lax.optimization_barrier(
        (other_codes, other_wide, gate_tiles, up_tiles, down_tiles)
    )
    gate_pair = (gate_tiles[0], hop(gate_tiles[0], "section", 1))
    up_pair = (up_tiles[0], hop(up_tiles[0], "section", 1))
    down_pair = (down_tiles[0], hop(down_tiles[0], "section", 1))

    plans = tile_plan(jnp.concatenate([codes, other_codes]), block_rows, own_cols, owner_index, owners)
    rotation = lax.rem(owner_index - jnp.arange(owners, dtype=jnp.int32) + owners, owners)
    noise = gate_left.shape[1]

    def rotated(table):
        parts = table.reshape(table.shape[0], owners, width)
        return jnp.take(parts, rotation, axis=1).reshape(table.shape)

    columns = lax.dynamic_slice_in_dim(owned_columns[0], owner_index * own_cols, own_cols)

    def owned(table):
        return jnp.take(table.reshape(table.shape[0], -1, BLOCK), columns, axis=1)

    cols = owned(jnp.concatenate([gate_right[0], up_right[0], down_left[0]], axis=0))
    other_cols = hop(cols, "section", 1)
    picks = pick_matrix(row_member, member_seed, noise)

    def tables(section):
        own = section_index == section
        words, groups = (jnp.where(own, table[:3], table[3:]) for table in plans)
        groups = jnp.concatenate([groups, own.astype(jnp.int32)[None]])
        chosen = rotated(jnp.where(own, wide, other_wide))
        left, right, gain = chosen[: 2 * noise], chosen[2 * noise : 3 * noise], chosen[3 * noise :]
        chosen = jnp.where(own, cols, other_cols)
        gate_cols, up_cols, down_cols = chosen[:noise], chosen[noise : 2 * noise], chosen[2 * noise :]
        empty = jnp.zeros_like(gate_cols)
        wide_cols = jnp.concatenate(
            [jnp.concatenate([gate_cols, empty], axis=2), jnp.concatenate([empty, up_cols], axis=2)], axis=0
        ).transpose(1, 0, 2)
        down_cols = down_cols.reshape(noise, own_cols // 2, 2 * BLOCK).transpose(1, 0, 2)
        return words.reshape(-1), groups, left, right, gain, wide_cols, down_cols

    layers = [tables(section) for section in range(2)]

    def layer(blocks, picked, section):
        words, groups, left, right, gain, wide_cols, down_cols = layers[section]
        raw, parts = expand(words, groups, blocks, gain, left, gate_pair, up_pair, own_cols, reps)
        parts = [parts[0]] + [hop(parts[g], "rep", -g) for g in range(1, reps)]
        hidden, coef = activate(parts, raw, picked, wide_cols, down_cols)
        hiddens = [hidden] + [hop(hidden, "rep", g) for g in range(1, reps)]
        outs = contract(words, groups, hiddens, coef, right, down_pair, owners)
        summed = outs[0].astype(jnp.float32)
        for step in range(1, owners):
            summed = summed + hop(outs[step], "tensor", -step).astype(jnp.float32)
        return summed

    mine_picks = lax.dynamic_slice_in_dim(picks, section_index * half, half)
    early = [hop_within(0, stream, "tensor", step) for step in range(1, owners)]
    seen = early[-1][:16, :BLOCK] if owners > 1 else stream[:16, :BLOCK]
    seen = lax.ppermute(seen, "section", [(0, 1)])
    waiting = jnp.where(seen[0, 0] == seen[0, 0], stream, jnp.zeros_like(stream))
    late = [hop_within(1, waiting, "tensor", step) for step in range(1, owners)]
    blocks = [stream] + [jnp.where(section_index == 0, a, b) for a, b in zip(early, late)]
    summed = layer(blocks, mine_picks, 0)
    own = stream[:half].astype(jnp.float32) + summed[:half]
    summed = jnp.concatenate([own, summed[half:]], axis=0).astype(jnp.bfloat16)
    total = summed.astype(jnp.float32)
    for g in range(1, reps):
        arrived = hop(summed, "rep", g).astype(jnp.float32)
        total = total + jnp.roll(arrived, g * half, axis=0)
    stream = total.astype(jnp.bfloat16)
    first = stream[:half]
    blocks = [stream] + [hop(stream, "tensor", step) for step in range(1, owners)]
    summed = layer(blocks, mine_picks, 1)
    value = first.astype(jnp.float32) + summed[:half]
    for g in range(1, reps):
        sent = summed[g * half : (g + 1) * half].astype(jnp.bfloat16)
        value = value + hop(sent, "rep", -g).astype(jnp.float32)
    second = value.astype(jnp.bfloat16)
    kept = jnp.where(section_index == 0, first, second)
    received = hop(jnp.where(section_index == 0, second, first), "section", 1)
    out = jnp.where(
        section_index == 0,
        jnp.concatenate([kept, received], axis=0),
        jnp.concatenate([received, kept], axis=0),
    )
    return out[None]


def solution(mesh):
    placed = (
        P(("pop", "rep"), "tensor"),
        P("section", None),
        P("section", ("tensor", "rep"), None, None),
        P("section", ("tensor", "rep"), None, None),
        P("section", ("tensor", "rep"), None, None),
        P("section", "tensor"),
        P("section", "tensor"),
        P("section", "tensor"),
        P("section", None),
        P("section", None, None),
        P("section", None, None),
        P("section", None, None),
        P("section", None, None),
        P("section", None, None),
        P("section", None, None),
        P(("pop", "rep")),
        P("pop"),
    )
    return jax.shard_map(
        per_device,
        mesh=mesh,
        in_specs=placed,
        out_specs=P("section", ("pop", "rep"), "tensor"),
        check_vma=False,
    )
```

```python
import functools

import jax
import jax.numpy as jnp
from jax import lax
from jax.experimental import pallas as pl
from jax.experimental.pallas import tpu as pltpu
from jax.sharding import PartitionSpec as P

BLOCK = 128
UNROLL = 16
MIB = 1024 * 1024
VMEM_LIMIT = 56 * MIB
SLOW = 4

perturb_scale = 0.5
epsilon = 1e-05


def hop(value, axis, steps):
    count = lax.axis_size(axis)
    return lax.ppermute(value, axis, [(i, (i + steps) % count) for i in range(count)])


def pick_matrix(row_member, member_seed, noise_count):
    member_ids = jnp.arange(member_seed.shape[0], dtype=jnp.int32)
    matched = row_member[:, None] == member_ids[None, :]
    seed_of = jnp.sum(jnp.where(matched, member_seed[None, :], 0), axis=1)
    sign_values = (1 - 2 * (row_member % 2)).astype(jnp.float32) * perturb_scale
    noise_ids = jnp.arange(noise_count, dtype=jnp.int32)
    return jnp.where(seed_of[:, None] == noise_ids[None, :], sign_values[:, None], jnp.float32(0.0))


def tile_plan(codes, block_rows, own_cols, owner_index, owners):
    tile_count = codes.shape[1]
    active = codes >= 0
    cleared = jnp.where(active, codes, 0)
    column = cleared // block_rows
    feature = cleared % block_rows
    per_owner = block_rows // owners
    feature = lax.rem(owner_index - feature // per_owner + owners, owners) * per_owner + feature % per_owner
    is_down = jnp.arange(codes.shape[0])[:, None] % 3 == 2
    major = jnp.where(is_down, feature, column)
    minor = jnp.where(is_down, column, feature)
    major_count = max(block_rows, own_cols)
    majors = jnp.arange(major_count, dtype=jnp.int32)
    filled = jnp.sum(
        jnp.where(active[:, None, :] & (major[:, None, :] == majors[None, :, None]), 1, 0), axis=2
    )
    padded = 2 * ((filled + 1) // 2)
    before = jnp.sum(jnp.where(majors[None, None, :] < major[:, :, None], padded[:, None, :], 0), axis=2)
    rank = jnp.sum(
        jnp.where(
            active[:, None, :]
            & (major[:, None, :] == major[:, :, None])
            & (minor[:, None, :] < minor[:, :, None]),
            1,
            0,
        ),
        axis=2,
    )
    place = jnp.where(active, before + rank, -1)
    length = tile_count + min(tile_count, major_count)
    group = 2 * UNROLL
    length = -(-length // group) * group
    tile_ids = jnp.arange(tile_count, dtype=jnp.int32)
    words = (tile_ids[None, :] - tile_count) + minor * 4096 + major * 1048576
    spots = jnp.arange(length, dtype=jnp.int32)
    packed = tile_count + jnp.sum(
        jnp.where(place[:, None, :] == spots[None, :, None], words[:, None, :], 0), axis=2
    )
    groups = (jnp.sum(padded, axis=1) + group - 1) // group
    return packed.astype(jnp.int32), groups.astype(jnp.int32)


def multiply_tiles(words_ref, groups_ref, which, length, read, tiles_ref, add):
    def group(i, carry):
        for u in range(UNROLL):
            at = which * length + (i * UNROLL + u) * 2
            first, second = words_ref[at], words_ref[at + 1]
            left = jnp.concatenate([read((first >> 12) & 255), read((second >> 12) & 255)], axis=1)
            right = jnp.concatenate([tiles_ref[first & 4095], tiles_ref[second & 4095]], axis=0)
            add(first >> 20, jnp.dot(left, right, preferred_element_type=jnp.float32))
        return carry

    lax.fori_loop(0, groups_ref[which], group, 0)


def load_tiles(own, choices, tiles, sem):
    copies = [pltpu.make_async_copy(tiles_hbm, tiles.at[pl.ds(0, tiles_hbm.shape[0])], sem) for tiles_hbm in choices]
    pl.when(own == 1)(copies[0].start)
    pl.when(own != 1)(copies[1].start)
    tiles[tiles.shape[0] - 1] = jnp.zeros((BLOCK, BLOCK), tiles.dtype)
    return copies[0]


def expand_kernel(owners, reps, words_ref, groups_ref, *refs):
    spans = len(refs) - 13 - reps
    blocks = refs[:spans]
    gain_ref, left_ref, own_gate, other_gate, own_up, other_up, raw_ref = refs[spans : spans + 7]
    part_refs = refs[spans + 7 : spans + 7 + reps]
    total_ref, gate_tiles, gate_sem, up_tiles, up_sem, x_ref = refs[spans + 7 + reps :]
    span_rows, width = blocks[0].shape
    split = spans // owners
    rows = part_refs[0].shape[2]
    per_owner = width // BLOCK
    strip = 48 if rows % 48 == 0 else 16
    gate_copy = load_tiles(groups_ref[3], (own_gate, other_gate), gate_tiles, gate_sem)
    up_copy = load_tiles(groups_ref[3], (own_up, other_up), up_tiles, up_sem)

    for span in range(split):

        def norm_rows(i, carry, span=span):
            start = pl.multiple_of(i * strip, strip)
            at = pl.ds(start, strip)
            squares = jnp.zeros((strip, BLOCK), jnp.float32)
            for owner in range(owners):
                for part in range(per_owner):
                    values = blocks[owner * split + span][at, pl.ds(part * BLOCK, BLOCK)].astype(jnp.float32)
                    squares = squares + values * values
            total = jnp.sum(squares, axis=1, keepdims=True)
            inverse = lax.rsqrt(total / (owners * width) + epsilon)
            for owner in range(owners):
                for part in range(per_owner):
                    values = blocks[owner * split + span][at, pl.ds(part * BLOCK, BLOCK)].astype(jnp.float32)
                    gain = gain_ref[:, pl.ds(owner * width + part * BLOCK, BLOCK)].astype(jnp.float32)
                    normed = (values * inverse * gain).astype(jnp.bfloat16)
                    x_ref[owner * per_owner + part, pl.ds(span * span_rows + start, strip), :] = normed
            return carry

        lax.fori_loop(0, span_rows // strip, norm_rows, 0)
    raw = jnp.zeros(raw_ref.shape, jnp.float32)
    step = min(8, x_ref.shape[0])
    for d in range(0, x_ref.shape[0], step):
        raw = raw + lax.dot_general(
            jnp.concatenate([x_ref[d + i, pl.ds(0, rows), :] for i in range(step)], axis=1),
            left_ref[:, pl.ds(d * BLOCK, step * BLOCK)],
            (((1,), (1,)), ((), ())),
            preferred_element_type=jnp.float32,
        )
    raw_ref[...] = raw

    def read(block):
        return x_ref[block]

    def add(block, product):
        total_ref[block] += product

    for which, tiles, copy in ((0, gate_tiles, gate_copy), (1, up_tiles, up_copy)):
        total_ref[...] = jnp.zeros(total_ref.shape, jnp.float32)
        copy.wait()
        multiply_tiles(words_ref, groups_ref, which, words_ref.shape[0] // 3, read, tiles, add)
        for rep, part_ref in enumerate(part_refs):

            def narrow(c, carry, which=which, rep=rep, part_ref=part_ref):
                part_ref[which, c] = total_ref[c, pl.ds(rep * rows, rows), :].astype(jnp.bfloat16)
                return carry

            lax.fori_loop(0, total_ref.shape[0], narrow, 0, unroll=min(4, total_ref.shape[0]))


SMEM = pl.BlockSpec(memory_space=pltpu.SMEM)
VMEM = pl.BlockSpec(memory_space=pltpu.VMEM)
HBM = pl.BlockSpec(memory_space=pl.ANY)


def tile_cost(tile_count, all_rows):
    return pl.CostEstimate(
        flops=SLOW * 2 * tile_count * all_rows * BLOCK * BLOCK,
        bytes_accessed=2 * tile_count * BLOCK * BLOCK,
        transcendentals=0,
    )


def tile_scratch(tile_count, blocks, all_rows):
    return [
        pltpu.VMEM((blocks, all_rows, BLOCK), jnp.float32),
        pltpu.VMEM((tile_count + 1, BLOCK, BLOCK), jnp.bfloat16),
        pltpu.SemaphoreType.DMA,
    ]


def expand(words, groups, blocks, gain, left, gate_tiles, up_tiles, own_cols, reps):
    features = gain.shape[1]
    owners = features // blocks[0].shape[1]
    all_rows = sum(block.size for block in blocks) // features
    rows = all_rows // reps
    tile_count = gate_tiles[0].shape[0]
    scratch = tile_scratch(tile_count, own_cols, all_rows)
    out = pl.pallas_call(
        functools.partial(expand_kernel, owners, reps),
        out_shape=[jax.ShapeDtypeStruct((rows, left.shape[0]), jnp.float32)]
        + [jax.ShapeDtypeStruct((2, own_cols, rows, BLOCK), jnp.bfloat16)] * reps,
        in_specs=[SMEM, SMEM] + [VMEM] * (len(blocks) + 2) + [HBM] * 4,
        out_specs=[VMEM] * (1 + reps),
        scratch_shapes=scratch
        + scratch[1:]
        + [pltpu.VMEM((features // BLOCK, all_rows, BLOCK), jnp.bfloat16)],
        compiler_params=pltpu.CompilerParams(vmem_limit_bytes=VMEM_LIMIT),
        cost_estimate=tile_cost(2 * tile_count, all_rows),
        name="expand",
    )(words, groups, *blocks, gain, left, *gate_tiles, *up_tiles)
    return out[0], out[1:]


def activate_kernel(reps, *refs):
    parts = refs[:reps]
    raw_ref, picks_ref, wide_cols, down_cols = refs[reps : reps + 4]
    hidden_ref, coef_ref = refs[-2:]
    noise = picks_ref.shape[1]
    columns, rows = hidden_ref.shape[:2]
    picks = picks_ref[...]
    coefs = (jnp.concatenate([picks, picks], axis=1) * raw_ref[...]).astype(jnp.bfloat16)

    def pair(i, down):
        hiddens = []
        for u in range(2):
            c = i * 2 + u
            low_rank = jnp.dot(coefs, wide_cols[c], preferred_element_type=jnp.float32)
            values = []
            for which in range(2):
                value = low_rank[:, which * BLOCK : (which + 1) * BLOCK]
                for part in parts:
                    value = value + part[which, c].astype(jnp.float32)
                values.append(value)
            gate, up = values
            hidden = (gate / (1.0 + jnp.exp(-gate)) * up).astype(jnp.bfloat16)
            hidden_ref[c] = hidden
            hiddens.append(hidden)
        return down + lax.dot_general(
            jnp.concatenate(hiddens, axis=1),
            down_cols[i],
            (((1,), (1,)), ((), ())),
            preferred_element_type=jnp.float32,
        )

    down = lax.fori_loop(
        0, columns // 2, pair, jnp.zeros((rows, noise), jnp.float32), unroll=min(4, columns // 2)
    )
    coef_ref[...] = picks * down


def activate(parts, raw, picks, wide_cols, down_cols, after):
    own_cols, rows = parts[0].shape[1:3]
    noise = picks.shape[1]
    reps = len(parts)
    return pl.pallas_call(
        functools.partial(activate_kernel, reps),
        out_shape=[
            jax.ShapeDtypeStruct((own_cols, rows, BLOCK), jnp.bfloat16),
            jax.ShapeDtypeStruct((rows, noise), jnp.float32),
        ],
        in_specs=[VMEM] * (reps + 4) + [HBM] * len(after),
        out_specs=[VMEM] * 2,
        compiler_params=pltpu.CompilerParams(vmem_limit_bytes=16 * MIB),
        cost_estimate=pl.CostEstimate(
            flops=100 * own_cols * rows * BLOCK,
            bytes_accessed=(reps * 2 + 1) * 2 * own_cols * rows * BLOCK,
            transcendentals=own_cols * rows * BLOCK,
        ),
        name="activate",
    )(*parts, raw, picks, wide_cols, down_cols, *after)


def contract_kernel(owners, reps, words_ref, groups_ref, *refs):
    hiddens = refs[:reps]
    coef_ref, right_ref, own_hbm, other_hbm = refs[reps : reps + 4]
    outs = refs[reps + 4 : reps + 4 + owners]
    total_ref, tiles, sem = refs[reps + 4 + owners :]
    rows = hiddens[0].shape[1]
    per_owner = outs[0].shape[1] // BLOCK
    blocks = total_ref.shape[0]
    copy = load_tiles(groups_ref[3], (own_hbm, other_hbm), tiles, sem)

    def read(block):
        return jnp.concatenate([hidden[block] for hidden in hiddens], axis=0)

    def add(block, product):
        total_ref[block] += product

    coef = coef_ref[...]
    high = coef.astype(jnp.bfloat16)
    low = (coef - high.astype(jnp.float32)).astype(jnp.bfloat16)
    right = right_ref[...]
    both = jnp.concatenate([high, low], axis=1)
    twice = jnp.concatenate([right, right], axis=0)
    for d in range(0, blocks, 2):
        start = jnp.dot(both, twice[:, d * BLOCK : (d + 2) * BLOCK], preferred_element_type=jnp.float32)
        for i in range(2):
            total_ref[d + i, pl.ds(0, rows), :] = start[:, i * BLOCK : (i + 1) * BLOCK]
            if reps > 1:
                total_ref[d + i, pl.ds(rows, (reps - 1) * rows), :] = jnp.zeros(
                    ((reps - 1) * rows, BLOCK), jnp.float32
                )
    copy.wait()
    multiply_tiles(words_ref, groups_ref, 2, words_ref.shape[0] // 3, read, tiles, add)
    for owner in range(owners):
        for part in range(per_owner):
            outs[owner][:, pl.ds(part * BLOCK, BLOCK)] = total_ref[owner * per_owner + part].astype(jnp.bfloat16)


def contract(words, groups, hiddens, coef, right, tiles, owners):
    own_cols, rows = hiddens[0].shape[:2]
    reps = len(hiddens)
    features = right.shape[1]
    tile_count = tiles[0].shape[0]
    return pl.pallas_call(
        functools.partial(contract_kernel, owners, reps),
        out_shape=[jax.ShapeDtypeStruct((reps * rows, features // owners), jnp.bfloat16)] * owners,
        in_specs=[SMEM, SMEM] + [VMEM] * (reps + 2) + [HBM, HBM],
        out_specs=[VMEM] * owners,
        scratch_shapes=tile_scratch(tile_count, features // BLOCK, reps * rows),
        compiler_params=pltpu.CompilerParams(vmem_limit_bytes=VMEM_LIMIT),
        cost_estimate=tile_cost(tile_count, reps * rows),
        name="contract",
    )(words, groups, *hiddens, coef, right, *tiles)


def per_device(
    tokens,
    norm_gain,
    gate_tiles,
    up_tiles,
    down_tiles,
    gate_slot,
    up_slot,
    down_slot,
    owned_columns,
    gate_left,
    gate_right,
    up_left,
    up_right,
    down_left,
    down_right,
    row_member,
    member_seed,
):
    section_index = lax.axis_index("section")
    owner_index = lax.axis_index("tensor")
    rep_index = lax.axis_index("rep")
    owners, reps = lax.axis_size("tensor"), lax.axis_size("rep")
    rows, width = tokens.shape
    own_cols = owned_columns.shape[1] // owners
    block_rows = gate_left.shape[2] // BLOCK
    tile_count = gate_tiles.shape[1]

    half = rows // 2
    piece = half // 2
    mine_rows = lax.dynamic_slice_in_dim(tokens, section_index * half, half)
    others = [hop(mine_rows, "rep", g) for g in range(1, reps)]

    def gather(value):
        return [hop(value, "tensor", step) for step in range(1, owners)]

    first_spans = [value[:piece] for value in [mine_rows] + others]
    first_blocks = [[span] + gather(span) for span in first_spans]
    first_blocks = [first_blocks[g][step] for step in range(owners) for g in range(reps)]

    codes = jnp.stack([gate_slot[0], up_slot[0], down_slot[0]])
    codes = lax.dynamic_slice_in_dim(codes, rep_index * tile_count, tile_count, axis=1)
    wide = jnp.concatenate([gate_left[0], up_left[0], down_right[0], norm_gain], axis=0)
    other_codes, other_wide = hop(codes, "section", 1), hop(wide, "section", 1)
    other_codes, other_wide, gate_tiles, up_tiles, down_tiles = lax.optimization_barrier(
        (other_codes, other_wide, gate_tiles, up_tiles, down_tiles)
    )
    gate_pair = (gate_tiles[0], hop(gate_tiles[0], "section", 1))
    up_pair = (up_tiles[0], hop(up_tiles[0], "section", 1))
    down_pair = (down_tiles[0], hop(down_tiles[0], "section", 1))

    plans = tile_plan(jnp.concatenate([codes, other_codes]), block_rows, own_cols, owner_index, owners)
    rotation = lax.rem(owner_index - jnp.arange(owners, dtype=jnp.int32) + owners, owners)
    noise = gate_left.shape[1]

    def rotated(table):
        parts = table.reshape(table.shape[0], owners, width)
        return jnp.take(parts, rotation, axis=1).reshape(table.shape)

    columns = lax.dynamic_slice_in_dim(owned_columns[0], owner_index * own_cols, own_cols)

    def owned(table):
        return jnp.take(table.reshape(table.shape[0], -1, BLOCK), columns, axis=1)

    cols = owned(jnp.concatenate([gate_right[0], up_right[0], down_left[0]], axis=0))
    other_cols = hop(cols, "section", 1)
    picks = pick_matrix(row_member, member_seed, noise)

    def tables(section):
        own = section_index == section
        words, groups = (jnp.where(own, table[:3], table[3:]) for table in plans)
        groups = jnp.concatenate([groups, own.astype(jnp.int32)[None]])
        chosen = rotated(jnp.where(own, wide, other_wide))
        left, right, gain = chosen[: 2 * noise], chosen[2 * noise : 3 * noise], chosen[3 * noise :]
        chosen = jnp.where(own, cols, other_cols)
        gate_cols, up_cols, down_cols = chosen[:noise], chosen[noise : 2 * noise], chosen[2 * noise :]
        empty = jnp.zeros_like(gate_cols)
        wide_cols = jnp.concatenate(
            [jnp.concatenate([gate_cols, empty], axis=2), jnp.concatenate([empty, up_cols], axis=2)], axis=0
        ).transpose(1, 0, 2)
        down_cols = down_cols.reshape(noise, own_cols // 2, 2 * BLOCK).transpose(1, 0, 2)
        return words.reshape(-1), groups, left, right, gain, wide_cols, down_cols

    layers = [tables(section) for section in range(2)]

    def expanded(blocks, section):
        words, groups, left, _, gain, _, _ = layers[section]
        return expand(words, groups, blocks, gain, left, gate_pair, up_pair, own_cols, reps)

    def activated(parts, raw, picked, section, after=()):
        wide_cols, down_cols = layers[section][5:]
        received = [hop(part, "rep", -(g + 1)) for g, part in enumerate(parts[1:])]
        hidden, coef = activate([parts[0]] + received, raw, picked, wide_cols, down_cols, after)
        return coef, hidden, [hop(hidden, "rep", g) for g in range(1, reps)]

    def contracted(coef, hidden, received, section):
        words, groups, _, right, _, _, _ = layers[section]
        return contract(words, groups, [hidden] + received, coef, right, down_pair, owners)

    def scattered(outs):
        summed = outs[0].astype(jnp.float32)
        for step in range(1, owners):
            summed = summed + hop(outs[step], "tensor", -step).astype(jnp.float32)
        return summed

    def streamed(own_rows, summed):
        own = own_rows.astype(jnp.float32) + summed[:piece]
        summed = jnp.concatenate([own, summed[piece:]], axis=0).astype(jnp.bfloat16)
        total = summed.astype(jnp.float32)
        for g in range(1, reps):
            arrived = hop(summed, "rep", g).astype(jnp.float32)
            total = total + jnp.roll(arrived, g * piece, axis=0)
        return total.astype(jnp.bfloat16)

    def finished(own_rows, summed):
        value = own_rows.astype(jnp.float32) + summed[:piece]
        for g in range(1, reps):
            sent = summed[g * piece : (g + 1) * piece].astype(jnp.bfloat16)
            value = value + hop(sent, "rep", -g).astype(jnp.float32)
        return value.astype(jnp.bfloat16)

    mine_picks = lax.dynamic_slice_in_dim(picks, section_index * half, half)
    cuts = (slice(0, piece), slice(piece, half))
    picked = [mine_picks[cut] for cut in cuts]
    streams = [mine_rows[cut] for cut in cuts]
    stream = jnp.concatenate([value[cuts[1]] for value in [mine_rows] + others], axis=0)
    blocks = [first_blocks, [stream] + gather(stream)]
    results = []
    for section in range(2):
        raw, parts = expanded(blocks[0], section)
        next_raw, next_parts = expanded(blocks[1], section)
        coef, hidden, received = activated(parts, raw, picked[0], section)
        outs = contracted(coef, hidden, received, section)
        coef, hidden, received = activated(next_parts, next_raw, picked[1], section, outs[:1])
        next_outs = contracted(coef, hidden, received, section)
        if section == 0:
            first = streamed(streams[0], scattered(outs))
            first_blocks = [first] + gather(first)
            later = jnp.where(first[0, 0] == first[0, 0], streams[1], jnp.zeros_like(streams[1]))
            second = streamed(later, scattered(next_outs))
            blocks = [first_blocks, [second] + gather(second)]
            streams = [first[:piece], second[:piece]]
        else:
            streams = [finished(streams[0], scattered(outs)), finished(streams[1], scattered(next_outs))]
        results.append(jnp.concatenate(streams, axis=0))
    first, second = results
    kept = jnp.where(section_index == 0, first, second)
    received = hop(jnp.where(section_index == 0, second, first), "section", 1)
    out = jnp.where(
        section_index == 0,
        jnp.concatenate([kept, received], axis=0),
        jnp.concatenate([received, kept], axis=0),
    )
    return out[None]


def solution(mesh):
    placed = (
        P(("pop", "rep"), "tensor"),
        P("section", None),
        P("section", ("tensor", "rep"), None, None),
        P("section", ("tensor", "rep"), None, None),
        P("section", ("tensor", "rep"), None, None),
        P("section", "tensor"),
        P("section", "tensor"),
        P("section", "tensor"),
        P("section", None),
        P("section", None, None),
        P("section", None, None),
        P("section", None, None),
        P("section", None, None),
        P("section", None, None),
        P("section", None, None),
        P(("pop", "rep")),
        P("pop"),
    )
    return jax.shard_map(
        per_device,
        mesh=mesh,
        in_specs=placed,
        out_specs=P("section", ("pop", "rep"), "tensor"),
        check_vma=False,
    )
```

```python
import functools

import jax
import jax.numpy as jnp
from jax import lax
from jax.experimental import pallas as pl
from jax.experimental.pallas import tpu as pltpu
from jax.sharding import PartitionSpec as P

BLOCK = 128
UNROLL = 16
MIB = 1024 * 1024
VMEM_LIMIT = 56 * MIB
COPIES = 8
SLOW = 4

perturb_scale = 0.5
epsilon = 1e-05


def hop(value, axis, steps):
    count = lax.axis_size(axis)
    return lax.ppermute(value, axis, [(i, (i + steps) % count) for i in range(count)])


def pick_matrix(row_member, member_seed, noise_count):
    member_ids = jnp.arange(member_seed.shape[0], dtype=jnp.int32)
    matched = row_member[:, None] == member_ids[None, :]
    seed_of = jnp.sum(jnp.where(matched, member_seed[None, :], 0), axis=1)
    sign_values = (1 - 2 * (row_member % 2)).astype(jnp.float32) * perturb_scale
    noise_ids = jnp.arange(noise_count, dtype=jnp.int32)
    return jnp.where(seed_of[:, None] == noise_ids[None, :], sign_values[:, None], jnp.float32(0.0))


def tile_plan(codes, block_rows, own_cols, owner_index, owners):
    tile_count = codes.shape[1]
    active = codes >= 0
    cleared = jnp.where(active, codes, 0)
    column = cleared // block_rows
    feature = cleared % block_rows
    per_owner = block_rows // owners
    feature = lax.rem(owner_index - feature // per_owner + owners, owners) * per_owner + feature % per_owner
    is_down = jnp.arange(codes.shape[0])[:, None] % 3 == 2
    major = jnp.where(is_down, feature, column)
    minor = jnp.where(is_down, column, feature)
    major_count = max(block_rows, own_cols)
    majors = jnp.arange(major_count, dtype=jnp.int32)
    filled = jnp.sum(
        jnp.where(active[:, None, :] & (major[:, None, :] == majors[None, :, None]), 1, 0), axis=2
    )
    padded = 2 * ((filled + 1) // 2)
    before = jnp.sum(jnp.where(majors[None, None, :] < major[:, :, None], padded[:, None, :], 0), axis=2)
    rank = jnp.sum(
        jnp.where(
            active[:, None, :]
            & (major[:, None, :] == major[:, :, None])
            & (minor[:, None, :] < minor[:, :, None]),
            1,
            0,
        ),
        axis=2,
    )
    place = jnp.where(active, before + rank, -1)
    length = tile_count + min(tile_count, major_count)
    group = 2 * UNROLL
    length = -(-length // group) * group
    tile_ids = jnp.arange(tile_count, dtype=jnp.int32)
    words = (tile_ids[None, :] - tile_count) + minor * 4096 + major * 1048576
    spots = jnp.arange(length, dtype=jnp.int32)
    packed = tile_count + jnp.sum(
        jnp.where(place[:, None, :] == spots[None, :, None], words[:, None, :], 0), axis=2
    )
    groups = (jnp.sum(padded, axis=1) + group - 1) // group
    return packed.astype(jnp.int32), groups.astype(jnp.int32)


def multiply_tiles(words_ref, groups_ref, which, length, read, tiles_ref, add):
    def group(i, carry):
        for u in range(UNROLL):
            at = which * length + (i * UNROLL + u) * 2
            first, second = words_ref[at], words_ref[at + 1]
            left = jnp.concatenate([read((first >> 12) & 255), read((second >> 12) & 255)], axis=1)
            right = jnp.concatenate([tiles_ref[first & 4095], tiles_ref[second & 4095]], axis=0)
            add(first >> 20, jnp.dot(left, right, preferred_element_type=jnp.float32))
        return carry

    lax.fori_loop(0, groups_ref[which], group, 0)


def load_tiles(own, choices, tiles, sem):
    count = tiles.shape[0] - 1
    step = -(-count // COPIES)

    def copies(tiles_hbm):
        for first in range(0, count, step):
            part = pl.ds(first, min(step, count - first))
            pltpu.make_async_copy(tiles_hbm.at[part], tiles.at[part], sem).start()

    pl.when(own == 1)(functools.partial(copies, choices[0]))
    pl.when(own != 1)(functools.partial(copies, choices[1]))
    tiles[count] = jnp.zeros((BLOCK, BLOCK), tiles.dtype)
    return pltpu.make_async_copy(choices[0], tiles.at[pl.ds(0, count)], sem)


def expand_kernel(owners, reps, unread, words_ref, groups_ref, *refs):
    spans = len(refs) - 13 - reps - unread
    blocks = refs[:spans]
    gain_ref, left_ref, own_gate, other_gate, own_up, other_up = refs[spans : spans + 6]
    raw_ref, *part_refs = refs[spans + 6 + unread : spans + 7 + unread + reps]
    total_ref, gate_tiles, gate_sem, up_tiles, up_sem, x_ref = refs[-6:]
    span_rows, width = blocks[0].shape
    split = spans // owners
    rows = part_refs[0].shape[2]
    per_owner = width // BLOCK
    strip = 48 if rows % 48 == 0 else 16
    gate_copy = load_tiles(groups_ref[3], (own_gate, other_gate), gate_tiles, gate_sem)
    up_copy = load_tiles(groups_ref[3], (own_up, other_up), up_tiles, up_sem)

    for span in range(split):

        def norm_rows(i, carry, span=span):
            start = pl.multiple_of(i * strip, strip)
            at = pl.ds(start, strip)
            squares = jnp.zeros((strip, BLOCK), jnp.float32)
            for owner in range(owners):
                for part in range(per_owner):
                    values = blocks[owner * split + span][at, pl.ds(part * BLOCK, BLOCK)].astype(jnp.float32)
                    squares = squares + values * values
            total = jnp.sum(squares, axis=1, keepdims=True)
            inverse = lax.rsqrt(total / (owners * width) + epsilon)
            for owner in range(owners):
                for part in range(per_owner):
                    values = blocks[owner * split + span][at, pl.ds(part * BLOCK, BLOCK)].astype(jnp.float32)
                    gain = gain_ref[:, pl.ds(owner * width + part * BLOCK, BLOCK)].astype(jnp.float32)
                    normed = (values * inverse * gain).astype(jnp.bfloat16)
                    x_ref[owner * per_owner + part, pl.ds(span * span_rows + start, strip), :] = normed
            return carry

        lax.fori_loop(0, span_rows // strip, norm_rows, 0)
    raw = jnp.zeros(raw_ref.shape, jnp.float32)
    step = min(8, x_ref.shape[0])
    for d in range(0, x_ref.shape[0], step):
        raw = raw + lax.dot_general(
            jnp.concatenate([x_ref[d + i, pl.ds(0, rows), :] for i in range(step)], axis=1),
            left_ref[:, pl.ds(d * BLOCK, step * BLOCK)],
            (((1,), (1,)), ((), ())),
            preferred_element_type=jnp.float32,
        )
    raw_ref[...] = raw

    def read(block):
        return x_ref[block]

    def add(block, product):
        total_ref[block] += product

    for which, tiles, copy in ((0, gate_tiles, gate_copy), (1, up_tiles, up_copy)):
        total_ref[...] = jnp.zeros(total_ref.shape, jnp.float32)
        copy.wait()
        multiply_tiles(words_ref, groups_ref, which, words_ref.shape[0] // 3, read, tiles, add)
        for rep, part_ref in enumerate(part_refs):

            def narrow(c, carry, which=which, rep=rep, part_ref=part_ref):
                part_ref[which, c] = total_ref[c, pl.ds(rep * rows, rows), :].astype(jnp.bfloat16)
                return carry

            lax.fori_loop(0, total_ref.shape[0], narrow, 0, unroll=min(4, total_ref.shape[0]))


SMEM = pl.BlockSpec(memory_space=pltpu.SMEM)
VMEM = pl.BlockSpec(memory_space=pltpu.VMEM)
HBM = pl.BlockSpec(memory_space=pl.ANY)


def tile_cost(tile_count, all_rows):
    return pl.CostEstimate(
        flops=SLOW * 2 * tile_count * all_rows * BLOCK * BLOCK,
        bytes_accessed=2 * tile_count * BLOCK * BLOCK,
        transcendentals=0,
    )


def tile_scratch(tile_count, blocks, all_rows):
    return [
        pltpu.VMEM((blocks, all_rows, BLOCK), jnp.float32),
        pltpu.VMEM((tile_count + 1, BLOCK, BLOCK), jnp.bfloat16),
        pltpu.SemaphoreType.DMA,
    ]


def expand(words, groups, blocks, gain, left, gate_tiles, up_tiles, own_cols, reps, after):
    features = gain.shape[1]
    owners = features // blocks[0].shape[1]
    all_rows = sum(block.size for block in blocks) // features
    rows = all_rows // reps
    tile_count = gate_tiles[0].shape[0]
    scratch = tile_scratch(tile_count, own_cols, all_rows)
    out = pl.pallas_call(
        functools.partial(expand_kernel, owners, reps, len(after)),
        out_shape=[jax.ShapeDtypeStruct((rows, left.shape[0]), jnp.float32)]
        + [jax.ShapeDtypeStruct((2, own_cols, rows, BLOCK), jnp.bfloat16)] * reps,
        in_specs=[SMEM, SMEM] + [VMEM] * (len(blocks) + 2) + [HBM] * (4 + len(after)),
        out_specs=[VMEM] * (1 + reps),
        scratch_shapes=scratch
        + scratch[1:]
        + [pltpu.VMEM((features // BLOCK, all_rows, BLOCK), jnp.bfloat16)],
        compiler_params=pltpu.CompilerParams(vmem_limit_bytes=VMEM_LIMIT),
        cost_estimate=tile_cost(2 * tile_count, all_rows),
        name="expand",
    )(words, groups, *blocks, gain, left, *gate_tiles, *up_tiles, *after)
    return out[0], out[1:]


def activate_kernel(reps, *refs):
    parts = refs[:reps]
    raw_ref, picks_ref, wide_cols, down_cols = refs[reps : reps + 4]
    hidden_ref, coef_ref = refs[-2:]
    noise = picks_ref.shape[1]
    columns, rows = hidden_ref.shape[:2]
    picks = picks_ref[...]
    coefs = (jnp.concatenate([picks, picks], axis=1) * raw_ref[...]).astype(jnp.bfloat16)

    def pair(i, down):
        hiddens = []
        for u in range(2):
            c = i * 2 + u
            low_rank = jnp.dot(coefs, wide_cols[c], preferred_element_type=jnp.float32)
            values = []
            for which in range(2):
                value = low_rank[:, which * BLOCK : (which + 1) * BLOCK]
                for part in parts:
                    value = value + part[which, c].astype(jnp.float32)
                values.append(value)
            gate, up = values
            hidden = (gate / (1.0 + jnp.exp(-gate)) * up).astype(jnp.bfloat16)
            hidden_ref[c] = hidden
            hiddens.append(hidden)
        return down + lax.dot_general(
            jnp.concatenate(hiddens, axis=1),
            down_cols[i],
            (((1,), (1,)), ((), ())),
            preferred_element_type=jnp.float32,
        )

    down = lax.fori_loop(
        0, columns // 2, pair, jnp.zeros((rows, noise), jnp.float32), unroll=min(4, columns // 2)
    )
    coef_ref[...] = picks * down


def activate(parts, raw, picks, wide_cols, down_cols, after):
    own_cols, rows = parts[0].shape[1:3]
    noise = picks.shape[1]
    reps = len(parts)
    return pl.pallas_call(
        functools.partial(activate_kernel, reps),
        out_shape=[
            jax.ShapeDtypeStruct((own_cols, rows, BLOCK), jnp.bfloat16),
            jax.ShapeDtypeStruct((rows, noise), jnp.float32),
        ],
        in_specs=[VMEM] * (reps + 4) + [HBM] * len(after),
        out_specs=[VMEM] * 2,
        compiler_params=pltpu.CompilerParams(vmem_limit_bytes=16 * MIB),
        cost_estimate=pl.CostEstimate(
            flops=100 * own_cols * rows * BLOCK,
            bytes_accessed=(reps * 2 + 1) * 2 * own_cols * rows * BLOCK,
            transcendentals=own_cols * rows * BLOCK,
        ),
        name="activate",
    )(*parts, raw, picks, wide_cols, down_cols, *after)


def contract_kernel(owners, reps, words_ref, groups_ref, *refs):
    hiddens = refs[:reps]
    coef_ref, right_ref, own_hbm, other_hbm = refs[reps : reps + 4]
    outs = refs[-3 - owners : -3]
    total_ref, tiles, sem = refs[-3:]
    rows = hiddens[0].shape[1]
    per_owner = outs[0].shape[1] // BLOCK
    blocks = total_ref.shape[0]
    copy = load_tiles(groups_ref[3], (own_hbm, other_hbm), tiles, sem)

    def read(block):
        return jnp.concatenate([hidden[block] for hidden in hiddens], axis=0)

    def add(block, product):
        total_ref[block] += product

    coef = coef_ref[...]
    high = coef.astype(jnp.bfloat16)
    low = (coef - high.astype(jnp.float32)).astype(jnp.bfloat16)
    right = right_ref[...]
    both = jnp.concatenate([high, low], axis=1)
    twice = jnp.concatenate([right, right], axis=0)
    for d in range(0, blocks, 2):
        start = jnp.dot(both, twice[:, d * BLOCK : (d + 2) * BLOCK], preferred_element_type=jnp.float32)
        for i in range(2):
            total_ref[d + i, pl.ds(0, rows), :] = start[:, i * BLOCK : (i + 1) * BLOCK]
            if reps > 1:
                total_ref[d + i, pl.ds(rows, (reps - 1) * rows), :] = jnp.zeros(
                    ((reps - 1) * rows, BLOCK), jnp.float32
                )
    copy.wait()
    multiply_tiles(words_ref, groups_ref, 2, words_ref.shape[0] // 3, read, tiles, add)
    for owner in range(owners):
        for part in range(per_owner):
            outs[owner][:, pl.ds(part * BLOCK, BLOCK)] = total_ref[owner * per_owner + part].astype(jnp.bfloat16)


def contract(words, groups, hiddens, coef, right, tiles, owners, after):
    own_cols, rows = hiddens[0].shape[:2]
    reps = len(hiddens)
    features = right.shape[1]
    tile_count = tiles[0].shape[0]
    return pl.pallas_call(
        functools.partial(contract_kernel, owners, reps),
        out_shape=[jax.ShapeDtypeStruct((reps * rows, features // owners), jnp.bfloat16)] * owners,
        in_specs=[SMEM, SMEM] + [VMEM] * (reps + 2) + [HBM] * (2 + len(after)),
        out_specs=[VMEM] * owners,
        scratch_shapes=tile_scratch(tile_count, features // BLOCK, reps * rows),
        compiler_params=pltpu.CompilerParams(vmem_limit_bytes=VMEM_LIMIT),
        cost_estimate=tile_cost(tile_count, reps * rows),
        name="contract",
    )(words, groups, *hiddens, coef, right, *tiles, *after)


def per_device(
    tokens,
    norm_gain,
    gate_tiles,
    up_tiles,
    down_tiles,
    gate_slot,
    up_slot,
    down_slot,
    owned_columns,
    gate_left,
    gate_right,
    up_left,
    up_right,
    down_left,
    down_right,
    row_member,
    member_seed,
):
    section_index = lax.axis_index("section")
    owner_index = lax.axis_index("tensor")
    rep_index = lax.axis_index("rep")
    owners, reps = lax.axis_size("tensor"), lax.axis_size("rep")
    rows, width = tokens.shape
    own_cols = owned_columns.shape[1] // owners
    block_rows = gate_left.shape[2] // BLOCK
    tile_count = gate_tiles.shape[1]

    half = rows // 2
    piece = half // 2
    mine_rows = lax.dynamic_slice_in_dim(tokens, section_index * half, half)
    others = [hop(mine_rows, "rep", g) for g in range(1, reps)]

    def gather(value):
        return [hop(value, "tensor", step) for step in range(1, owners)]

    first_spans = [value[:piece] for value in [mine_rows] + others]
    first_blocks = [[span] + gather(span) for span in first_spans]
    first_blocks = [first_blocks[g][step] for step in range(owners) for g in range(reps)]

    codes = jnp.stack([gate_slot[0], up_slot[0], down_slot[0]])
    codes = lax.dynamic_slice_in_dim(codes, rep_index * tile_count, tile_count, axis=1)
    wide = jnp.concatenate([gate_left[0], up_left[0], down_right[0], norm_gain], axis=0)
    other_codes, other_wide = hop(codes, "section", 1), hop(wide, "section", 1)
    other_codes, other_wide, gate_tiles, up_tiles, down_tiles = lax.optimization_barrier(
        (other_codes, other_wide, gate_tiles, up_tiles, down_tiles)
    )
    gate_pair = (gate_tiles[0], hop(gate_tiles[0], "section", 1))
    up_pair = (up_tiles[0], hop(up_tiles[0], "section", 1))
    down_pair = (down_tiles[0], hop(down_tiles[0], "section", 1))

    plans = tile_plan(jnp.concatenate([codes, other_codes]), block_rows, own_cols, owner_index, owners)
    rotation = lax.rem(owner_index - jnp.arange(owners, dtype=jnp.int32) + owners, owners)
    noise = gate_left.shape[1]

    def rotated(table):
        parts = table.reshape(table.shape[0], owners, width)
        return jnp.take(parts, rotation, axis=1).reshape(table.shape)

    columns = lax.dynamic_slice_in_dim(owned_columns[0], owner_index * own_cols, own_cols)

    def owned(table):
        return jnp.take(table.reshape(table.shape[0], -1, BLOCK), columns, axis=1)

    cols = owned(jnp.concatenate([gate_right[0], up_right[0], down_left[0]], axis=0))
    other_cols = hop(cols, "section", 1)
    picks = pick_matrix(row_member, member_seed, noise)

    def tables(section):
        own = section_index == section
        words, groups = (jnp.where(own, table[:3], table[3:]) for table in plans)
        groups = jnp.concatenate([groups, own.astype(jnp.int32)[None]])
        chosen = rotated(jnp.where(own, wide, other_wide))
        left, right, gain = chosen[: 2 * noise], chosen[2 * noise : 3 * noise], chosen[3 * noise :]
        chosen = jnp.where(own, cols, other_cols)
        gate_cols, up_cols, down_cols = chosen[:noise], chosen[noise : 2 * noise], chosen[2 * noise :]
        empty = jnp.zeros_like(gate_cols)
        wide_cols = jnp.concatenate(
            [jnp.concatenate([gate_cols, empty], axis=2), jnp.concatenate([empty, up_cols], axis=2)], axis=0
        ).transpose(1, 0, 2)
        down_cols = down_cols.reshape(noise, own_cols // 2, 2 * BLOCK).transpose(1, 0, 2)
        return words.reshape(-1), groups, left, right, gain, wide_cols, down_cols

    layers = [tables(section) for section in range(2)]

    def expanded(blocks, section, after=()):
        words, groups, left, _, gain, _, _ = layers[section]
        return expand(words, groups, blocks, gain, left, gate_pair, up_pair, own_cols, reps, after)

    def activated(parts, raw, picked, section, after=()):
        wide_cols, down_cols = layers[section][5:]
        received = [hop(part, "rep", -(g + 1)) for g, part in enumerate(parts[1:])]
        hidden, coef = activate([parts[0]] + received, raw, picked, wide_cols, down_cols, after)
        return coef, hidden, [hop(hidden, "rep", g) for g in range(1, reps)]

    def contracted(coef, hidden, received, section, after=()):
        words, groups, _, right, _, _, _ = layers[section]
        return contract(words, groups, [hidden] + received, coef, right, down_pair, owners, after)

    def scattered(outs):
        summed = outs[0].astype(jnp.float32)
        for step in range(1, owners):
            summed = summed + hop(outs[step], "tensor", -step).astype(jnp.float32)
        return summed

    def streamed(own_rows, summed):
        own = own_rows.astype(jnp.float32) + summed[:piece]
        summed = jnp.concatenate([own, summed[piece:]], axis=0).astype(jnp.bfloat16)
        total = summed.astype(jnp.float32)
        for g in range(1, reps):
            arrived = hop(summed, "rep", g).astype(jnp.float32)
            total = total + jnp.roll(arrived, g * piece, axis=0)
        return total.astype(jnp.bfloat16)

    def finished(own_rows, summed):
        value = own_rows.astype(jnp.float32) + summed[:piece]
        for g in range(1, reps):
            sent = summed[g * piece : (g + 1) * piece].astype(jnp.bfloat16)
            value = value + hop(sent, "rep", -g).astype(jnp.float32)
        return value.astype(jnp.bfloat16)

    mine_picks = lax.dynamic_slice_in_dim(picks, section_index * half, half)
    cuts = (slice(0, piece), slice(piece, half))
    picked = [mine_picks[cut] for cut in cuts]
    streams = [mine_rows[cut] for cut in cuts]
    stream = jnp.concatenate([value[cuts[1]] for value in [mine_rows] + others], axis=0)
    blocks = [first_blocks, [stream] + gather(stream)]
    results = []
    raw, parts = expanded(blocks[0], 0)
    for section in range(2):
        coef, hidden, received = activated(parts, raw, picked[0], section)
        next_raw, parts = expanded(blocks[1], section, after=(received if section else [coef])[:1])
        outs = contracted(coef, hidden, received, section, after=(next_raw,))
        coef, hidden, received = activated(parts, next_raw, picked[1], section, after=(outs[0],))
        streams[0] = jnp.where(coef[0, 0] == coef[0, 0], streams[0], jnp.zeros_like(streams[0]))
        next_outs = contracted(coef, hidden, received, section)
        if section == 0:
            first = streamed(streams[0], scattered(outs))
            raw, parts = expanded([first] + gather(first), 1)
            later = jnp.where(raw[0, 0] == raw[0, 0], streams[1], jnp.zeros_like(streams[1]))
            second = streamed(later, scattered(next_outs))
            blocks = [None, [second] + gather(second)]
            streams = [first[:piece], second[:piece]]
        else:
            streams = [finished(streams[0], scattered(outs)), finished(streams[1], scattered(next_outs))]
        results.append(jnp.concatenate(streams, axis=0))
    first, second = results
    kept = jnp.where(section_index == 0, first, second)
    received = hop(jnp.where(section_index == 0, second, first), "section", 1)
    out = jnp.where(
        section_index == 0,
        jnp.concatenate([kept, received], axis=0),
        jnp.concatenate([received, kept], axis=0),
    )
    return out[None]


def solution(mesh):
    placed = (
        P(("pop", "rep"), "tensor"),
        P("section", None),
        P("section", ("tensor", "rep"), None, None),
        P("section", ("tensor", "rep"), None, None),
        P("section", ("tensor", "rep"), None, None),
        P("section", "tensor"),
        P("section", "tensor"),
        P("section", "tensor"),
        P("section", None),
        P("section", None, None),
        P("section", None, None),
        P("section", None, None),
        P("section", None, None),
        P("section", None, None),
        P("section", None, None),
        P(("pop", "rep")),
        P("pop"),
    )
    return jax.shard_map(
        per_device,
        mesh=mesh,
        in_specs=placed,
        out_specs=P("section", ("pop", "rep"), "tensor"),
        check_vma=False,
    )
```

```python
import functools

import jax
import jax.numpy as jnp
from jax import lax
from jax.experimental import pallas as pl
from jax.experimental.pallas import tpu as pltpu
from jax.sharding import PartitionSpec as P

BLOCK = 128
UNROLL = 16
MIB = 1024 * 1024
VMEM_LIMIT = 56 * MIB
COPIES = 8
SLOW = 4

perturb_scale = 0.5
epsilon = 1e-05


def hop(value, axis, steps):
    count = lax.axis_size(axis)
    return lax.ppermute(value, axis, [(i, (i + steps) % count) for i in range(count)])


def pick_matrix(row_member, member_seed, noise_count):
    member_ids = jnp.arange(member_seed.shape[0], dtype=jnp.int32)
    matched = row_member[:, None] == member_ids[None, :]
    seed_of = jnp.sum(jnp.where(matched, member_seed[None, :], 0), axis=1)
    sign_values = (1 - 2 * (row_member % 2)).astype(jnp.float32) * perturb_scale
    noise_ids = jnp.arange(noise_count, dtype=jnp.int32)
    return jnp.where(seed_of[:, None] == noise_ids[None, :], sign_values[:, None], jnp.float32(0.0))


def tile_plan(codes, block_rows, own_cols, owner_index, owners):
    tile_count = codes.shape[1]
    active = codes >= 0
    cleared = jnp.where(active, codes, 0)
    column = cleared // block_rows
    feature = cleared % block_rows
    per_owner = block_rows // owners
    feature = lax.rem(owner_index - feature // per_owner + owners, owners) * per_owner + feature % per_owner
    is_down = jnp.arange(codes.shape[0])[:, None] % 3 == 2
    major = jnp.where(is_down, feature, column)
    minor = jnp.where(is_down, column, feature)
    major_count = max(block_rows, own_cols)
    majors = jnp.arange(major_count, dtype=jnp.int32)
    filled = jnp.sum(
        jnp.where(active[:, None, :] & (major[:, None, :] == majors[None, :, None]), 1, 0), axis=2
    )
    padded = 2 * ((filled + 1) // 2)
    before = jnp.sum(jnp.where(majors[None, None, :] < major[:, :, None], padded[:, None, :], 0), axis=2)
    rank = jnp.sum(
        jnp.where(
            active[:, None, :]
            & (major[:, None, :] == major[:, :, None])
            & (minor[:, None, :] < minor[:, :, None]),
            1,
            0,
        ),
        axis=2,
    )
    place = jnp.where(active, before + rank, -1)
    length = tile_count + min(tile_count, major_count)
    group = 2 * UNROLL
    length = -(-length // group) * group
    tile_ids = jnp.arange(tile_count, dtype=jnp.int32)
    words = (tile_ids[None, :] - tile_count) + minor * 4096 + major * 1048576
    spots = jnp.arange(length, dtype=jnp.int32)
    packed = tile_count + jnp.sum(
        jnp.where(place[:, None, :] == spots[None, :, None], words[:, None, :], 0), axis=2
    )
    groups = (jnp.sum(padded, axis=1) + group - 1) // group
    return packed.astype(jnp.int32), groups.astype(jnp.int32)


def multiply_tiles(words_ref, groups_ref, which, length, read, tiles_ref, add):
    def group(i, carry):
        for u in range(UNROLL):
            at = which * length + (i * UNROLL + u) * 2
            first, second = words_ref[at], words_ref[at + 1]
            left = jnp.concatenate([read((first >> 12) & 255), read((second >> 12) & 255)], axis=1)
            right = jnp.concatenate([tiles_ref[first & 4095], tiles_ref[second & 4095]], axis=0)
            add(first >> 20, jnp.dot(left, right, preferred_element_type=jnp.float32))
        return carry

    lax.fori_loop(0, groups_ref[which], group, 0)


def load_tiles(own, choices, tiles, sem):
    count = tiles.shape[0] - 1
    step = -(-count // COPIES)

    def copies(tiles_hbm):
        for first in range(0, count, step):
            part = pl.ds(first, min(step, count - first))
            pltpu.make_async_copy(tiles_hbm.at[part], tiles.at[part], sem).start()

    pl.when(own == 1)(functools.partial(copies, choices[0]))
    pl.when(own != 1)(functools.partial(copies, choices[1]))
    tiles[count] = jnp.zeros((BLOCK, BLOCK), tiles.dtype)
    return pltpu.make_async_copy(choices[0], tiles.at[pl.ds(0, count)], sem)


def expand_kernel(reps, words_ref, groups_ref, *refs):
    stacks = refs[:reps]
    gain_ref, left_ref, own_gate, other_gate, own_up, other_up = refs[reps : reps + 6]
    raw_ref, *part_refs = refs[reps + 6 : 2 * reps + 7]
    total_ref, gate_tiles, gate_sem, up_tiles, up_sem, x_ref = refs[-6:]
    owners, rows, width = stacks[0].shape
    per_owner = width // BLOCK
    strip = 48 if rows % 48 == 0 else 16
    gate_copy = load_tiles(groups_ref[3], (own_gate, other_gate), gate_tiles, gate_sem)

    for rep in range(reps):

        def norm_rows(i, carry, rep=rep):
            start = pl.multiple_of(i * strip, strip)
            at = pl.ds(start, strip)

            def load(owner, part):
                return stacks[rep][owner, at, pl.ds(part * BLOCK, BLOCK)].astype(jnp.float32)

            squares = jnp.zeros((strip, BLOCK), jnp.float32)
            for owner in range(owners):
                for part in range(per_owner):
                    values = load(owner, part)
                    squares = squares + values * values
            total = jnp.sum(squares, axis=1, keepdims=True)
            inverse = lax.rsqrt(total / (owners * width) + epsilon)
            for owner in range(owners):
                for part in range(per_owner):
                    gain = gain_ref[:, pl.ds(owner * width + part * BLOCK, BLOCK)].astype(jnp.float32)
                    normed = (load(owner, part) * inverse * gain).astype(jnp.bfloat16)
                    x_ref[owner * per_owner + part, pl.ds(rep * rows + start, strip), :] = normed
            return carry

        lax.fori_loop(0, rows // strip, norm_rows, 0)
    raw = jnp.zeros(raw_ref.shape, jnp.float32)
    step = min(8, x_ref.shape[0])
    for d in range(0, x_ref.shape[0], step):
        raw = raw + lax.dot_general(
            jnp.concatenate([x_ref[d + i, pl.ds(0, rows), :] for i in range(step)], axis=1),
            left_ref[:, pl.ds(d * BLOCK, step * BLOCK)],
            (((1,), (1,)), ((), ())),
            preferred_element_type=jnp.float32,
        )
    raw_ref[...] = raw

    def read(block):
        return x_ref[block]

    def add(block, product):
        total_ref[block] += product

    for which, tiles in ((0, gate_tiles), (1, up_tiles)):
        total_ref[...] = jnp.zeros(total_ref.shape, jnp.float32)
        if which == 0:
            gate_copy.wait()
            up_copy = load_tiles(groups_ref[3], (own_up, other_up), up_tiles, up_sem)
        else:
            up_copy.wait()
        multiply_tiles(words_ref, groups_ref, which, words_ref.shape[0] // 3, read, tiles, add)
        for rep, part_ref in enumerate(part_refs):

            def narrow(c, carry, which=which, rep=rep, part_ref=part_ref):
                part_ref[which, c] = total_ref[c, pl.ds(rep * rows, rows), :].astype(jnp.bfloat16)
                return carry

            lax.fori_loop(0, total_ref.shape[0], narrow, 0, unroll=min(4, total_ref.shape[0]))


SMEM = pl.BlockSpec(memory_space=pltpu.SMEM)
VMEM = pl.BlockSpec(memory_space=pltpu.VMEM)
HBM = pl.BlockSpec(memory_space=pl.ANY)


def tile_cost(tile_count, all_rows):
    return pl.CostEstimate(
        flops=SLOW * 2 * tile_count * all_rows * BLOCK * BLOCK,
        bytes_accessed=2 * tile_count * BLOCK * BLOCK,
        transcendentals=0,
    )


def tile_scratch(tile_count, blocks, all_rows):
    return [
        pltpu.VMEM((blocks, all_rows, BLOCK), jnp.float32),
        pltpu.VMEM((tile_count + 1, BLOCK, BLOCK), jnp.bfloat16),
        pltpu.SemaphoreType.DMA,
    ]


def expand(words, groups, stacks, gain, left, gate_tiles, up_tiles, own_cols):
    reps = len(stacks)
    features = gain.shape[1]
    rows = stacks[0].shape[1]
    tile_count = gate_tiles[0].shape[0]
    scratch = tile_scratch(tile_count, own_cols, reps * rows)
    out = pl.pallas_call(
        functools.partial(expand_kernel, reps),
        out_shape=[jax.ShapeDtypeStruct((rows, left.shape[0]), jnp.float32)]
        + [jax.ShapeDtypeStruct((2, own_cols, rows, BLOCK), jnp.bfloat16)] * reps,
        in_specs=[SMEM, SMEM] + [VMEM] * (reps + 2) + [HBM] * 4,
        out_specs=[VMEM] * (1 + reps),
        scratch_shapes=scratch
        + scratch[1:]
        + [pltpu.VMEM((features // BLOCK, reps * rows, BLOCK), jnp.bfloat16)],
        compiler_params=pltpu.CompilerParams(vmem_limit_bytes=VMEM_LIMIT),
        cost_estimate=tile_cost(2 * tile_count, reps * rows),
        name="expand",
    )(words, groups, *stacks, gain, left, *gate_tiles, *up_tiles)
    return out[0], out[1:]


def activate_kernel(reps, *refs):
    parts = refs[:reps]
    raw_ref, picks_ref, wide_cols, down_cols = refs[reps : reps + 4]
    hidden_ref, coef_ref = refs[-2:]
    noise = picks_ref.shape[1]
    columns, rows = hidden_ref.shape[:2]
    picks = picks_ref[...]
    coefs = (jnp.concatenate([picks, picks], axis=1) * raw_ref[...]).astype(jnp.bfloat16)

    def pair(i, down):
        hiddens = []
        for u in range(2):
            c = i * 2 + u
            low_rank = jnp.dot(coefs, wide_cols[c], preferred_element_type=jnp.float32)
            values = []
            for which in range(2):
                value = low_rank[:, which * BLOCK : (which + 1) * BLOCK]
                for part in parts:
                    value = value + part[which, c].astype(jnp.float32)
                values.append(value)
            gate, up = values
            hidden = (gate / (1.0 + jnp.exp(-gate)) * up).astype(jnp.bfloat16)
            hidden_ref[c] = hidden
            hiddens.append(hidden)
        return down + lax.dot_general(
            jnp.concatenate(hiddens, axis=1),
            down_cols[i],
            (((1,), (1,)), ((), ())),
            preferred_element_type=jnp.float32,
        )

    down = lax.fori_loop(
        0, columns // 2, pair, jnp.zeros((rows, noise), jnp.float32), unroll=min(4, columns // 2)
    )
    coef_ref[...] = picks * down


def activate(parts, raw, picks, wide_cols, down_cols):
    own_cols, rows = parts[0].shape[1:3]
    noise = picks.shape[1]
    reps = len(parts)
    return pl.pallas_call(
        functools.partial(activate_kernel, reps),
        out_shape=[
            jax.ShapeDtypeStruct((own_cols, rows, BLOCK), jnp.bfloat16),
            jax.ShapeDtypeStruct((rows, noise), jnp.float32),
        ],
        in_specs=[VMEM] * (reps + 4),
        out_specs=[VMEM] * 2,
        compiler_params=pltpu.CompilerParams(vmem_limit_bytes=16 * MIB),
        cost_estimate=pl.CostEstimate(
            flops=100 * own_cols * rows * BLOCK,
            bytes_accessed=(reps * 2 + 1) * 2 * own_cols * rows * BLOCK,
            transcendentals=own_cols * rows * BLOCK,
        ),
        name="activate",
    )(*parts, raw, picks, wide_cols, down_cols)


def contract_kernel(reps, words_ref, groups_ref, *refs):
    hiddens = refs[:reps]
    coef_ref, right_ref, own_hbm, other_hbm = refs[reps : reps + 4]
    outs = refs[-3 - reps : -3]
    total_ref, tiles, sem = refs[-3:]
    rows = hiddens[0].shape[1]
    blocks = total_ref.shape[0]
    copy = load_tiles(groups_ref[3], (own_hbm, other_hbm), tiles, sem)

    def read(block):
        return jnp.concatenate([hidden[block] for hidden in hiddens], axis=0)

    def add(block, product):
        total_ref[block] += product

    coef = coef_ref[...]
    high = coef.astype(jnp.bfloat16)
    low = (coef - high.astype(jnp.float32)).astype(jnp.bfloat16)
    right = right_ref[...]
    both = jnp.concatenate([high, low], axis=1)
    twice = jnp.concatenate([right, right], axis=0)
    for d in range(0, blocks, 2):
        start = jnp.dot(both, twice[:, d * BLOCK : (d + 2) * BLOCK], preferred_element_type=jnp.float32)
        for i in range(2):
            total_ref[d + i, pl.ds(0, rows), :] = start[:, i * BLOCK : (i + 1) * BLOCK]
            if reps > 1:
                total_ref[d + i, pl.ds(rows, (reps - 1) * rows), :] = jnp.zeros(
                    ((reps - 1) * rows, BLOCK), jnp.float32
                )
    copy.wait()
    multiply_tiles(words_ref, groups_ref, 2, words_ref.shape[0] // 3, read, tiles, add)
    for rep in range(reps):
        for d in range(blocks):
            outs[rep][:, pl.ds(d * BLOCK, BLOCK)] = total_ref[d, pl.ds(rep * rows, rows), :].astype(jnp.bfloat16)


def contract(words, groups, hiddens, coef, right, tiles):
    own_cols, rows = hiddens[0].shape[:2]
    reps = len(hiddens)
    features = right.shape[1]
    tile_count = tiles[0].shape[0]
    return pl.pallas_call(
        functools.partial(contract_kernel, reps),
        out_shape=[jax.ShapeDtypeStruct((rows, features), jnp.bfloat16)] * reps,
        in_specs=[SMEM, SMEM] + [VMEM] * (reps + 2) + [HBM] * 2,
        out_specs=[VMEM] * reps,
        scratch_shapes=tile_scratch(tile_count, features // BLOCK, reps * rows),
        compiler_params=pltpu.CompilerParams(vmem_limit_bytes=VMEM_LIMIT),
        cost_estimate=tile_cost(tile_count, reps * rows),
        name="contract",
    )(words, groups, *hiddens, coef, right, *tiles)


def per_device(
    tokens,
    norm_gain,
    gate_tiles,
    up_tiles,
    down_tiles,
    gate_slot,
    up_slot,
    down_slot,
    owned_columns,
    gate_left,
    gate_right,
    up_left,
    up_right,
    down_left,
    down_right,
    row_member,
    member_seed,
):
    section_index = lax.axis_index("section")
    owner_index = lax.axis_index("tensor")
    rep_index = lax.axis_index("rep")
    owners, reps = lax.axis_size("tensor"), lax.axis_size("rep")
    rows, width = tokens.shape
    own_cols = owned_columns.shape[1] // owners
    block_rows = gate_left.shape[2] // BLOCK
    tile_count = gate_tiles.shape[1]

    half = rows // 2
    piece = half // 2
    mine_rows = lax.dynamic_slice_in_dim(tokens, section_index * half, half)
    streams = [mine_rows[:piece], mine_rows[piece:]]

    def gathered(own):
        stack = jnp.stack([own] + [hop(own, "tensor", step) for step in range(1, owners)])
        return [stack] + [hop(stack, "rep", g) for g in range(1, reps)]

    stacks = [gathered(stream) for stream in streams]

    codes = jnp.stack([gate_slot[0], up_slot[0], down_slot[0]])
    codes = lax.dynamic_slice_in_dim(codes, rep_index * tile_count, tile_count, axis=1)
    wide = jnp.concatenate([gate_left[0], up_left[0], down_right[0], norm_gain], axis=0)
    other_codes, other_wide = hop(codes, "section", 1), hop(wide, "section", 1)
    other_codes, other_wide, gate_tiles, up_tiles, down_tiles = lax.optimization_barrier(
        (other_codes, other_wide, gate_tiles, up_tiles, down_tiles)
    )
    gate_pair = (gate_tiles[0], hop(gate_tiles[0], "section", 1))
    up_pair = (up_tiles[0], hop(up_tiles[0], "section", 1))
    down_pair = (down_tiles[0], hop(down_tiles[0], "section", 1))

    plans = tile_plan(jnp.concatenate([codes, other_codes]), block_rows, own_cols, owner_index, owners)
    rotation = lax.rem(owner_index - jnp.arange(owners, dtype=jnp.int32) + owners, owners)
    noise = gate_left.shape[1]

    def rotated(table):
        parts = table.reshape(table.shape[0], owners, width)
        return jnp.take(parts, rotation, axis=1).reshape(table.shape)

    columns = lax.dynamic_slice_in_dim(owned_columns[0], owner_index * own_cols, own_cols)

    def owned(table):
        return jnp.take(table.reshape(table.shape[0], -1, BLOCK), columns, axis=1)

    cols = owned(jnp.concatenate([gate_right[0], up_right[0], down_left[0]], axis=0))
    other_cols = hop(cols, "section", 1)
    picks = pick_matrix(row_member, member_seed, noise)

    def tables(section):
        own = section_index == section
        words, groups = (jnp.where(own, table[:3], table[3:]) for table in plans)
        groups = jnp.concatenate([groups, own.astype(jnp.int32)[None]])
        chosen = rotated(jnp.where(own, wide, other_wide))
        left, right, gain = chosen[: 2 * noise], chosen[2 * noise : 3 * noise], chosen[3 * noise :]
        chosen = jnp.where(own, cols, other_cols)
        gate_cols, up_cols, down_cols = chosen[:noise], chosen[noise : 2 * noise], chosen[2 * noise :]
        empty = jnp.zeros_like(gate_cols)
        wide_cols = jnp.concatenate(
            [jnp.concatenate([gate_cols, empty], axis=2), jnp.concatenate([empty, up_cols], axis=2)], axis=0
        ).transpose(1, 0, 2)
        down_cols = down_cols.reshape(noise, own_cols // 2, 2 * BLOCK).transpose(1, 0, 2)
        return words.reshape(-1), groups, left, right, gain, wide_cols, down_cols

    layers = [tables(section) for section in range(2)]

    mine_picks = lax.dynamic_slice_in_dim(picks, section_index * half, half)
    picked = [mine_picks[:piece], mine_picks[piece:]]

    def layer(stacks, picked, section):
        words, groups, left, right, gain, wide_cols, down_cols = layers[section]
        raw, parts = expand(words, groups, stacks, gain, left, gate_pair, up_pair, own_cols)
        parts = [parts[0]] + [hop(parts[g], "rep", -g) for g in range(1, reps)]
        hidden, coef = activate(parts, raw, picked, wide_cols, down_cols)
        hiddens = [hidden] + [hop(hidden, "rep", g) for g in range(1, reps)]
        return contract(words, groups, hiddens, coef, right, down_pair)

    def scattered(own, outs):
        total = outs[0].astype(jnp.float32)
        for g in range(1, reps):
            total = total + hop(outs[g], "rep", -g).astype(jnp.float32)
        value = own.astype(jnp.float32) + total[:, :width]
        for step in range(1, owners):
            sent = total[:, step * width : (step + 1) * width].astype(jnp.bfloat16)
            value = value + hop(sent, "tensor", -step).astype(jnp.float32)
        return value.astype(jnp.bfloat16)

    results = []
    for section in range(2):
        streams = [scattered(own, layer(stack, p, section)) for own, stack, p in zip(streams, stacks, picked)]
        results.append(jnp.concatenate(streams, axis=0))
        if section == 0:
            stacks = [gathered(stream) for stream in streams]
    first, second = results
    kept = jnp.where(section_index == 0, first, second)
    received = hop(jnp.where(section_index == 0, second, first), "section", 1)
    out = jnp.where(
        section_index == 0,
        jnp.concatenate([kept, received], axis=0),
        jnp.concatenate([received, kept], axis=0),
    )
    return out[None]


def solution(mesh):
    placed = (
        P(("pop", "rep"), "tensor"),
        P("section", None),
        P("section", ("tensor", "rep"), None, None),
        P("section", ("tensor", "rep"), None, None),
        P("section", ("tensor", "rep"), None, None),
        P("section", "tensor"),
        P("section", "tensor"),
        P("section", "tensor"),
        P("section", None),
        P("section", None, None),
        P("section", None, None),
        P("section", None, None),
        P("section", None, None),
        P("section", None, None),
        P("section", None, None),
        P(("pop", "rep")),
        P("pop"),
    )
    return jax.shard_map(
        per_device,
        mesh=mesh,
        in_specs=placed,
        out_specs=P("section", ("pop", "rep"), "tensor"),
        check_vma=False,
    )
```

```python
import functools

import jax
import jax.numpy as jnp
from jax import lax
from jax.experimental import pallas as pl
from jax.experimental.pallas import tpu as pltpu
from jax.sharding import PartitionSpec as P

BLOCK = 128
UNROLL = 16
MIB = 1024 * 1024
VMEM_LIMIT = 56 * MIB
COPIES = 8
SLOW = 4

perturb_scale = 0.5
epsilon = 1e-05


def hop(value, axis, steps):
    count = lax.axis_size(axis)
    return lax.ppermute(value, axis, [(i, (i + steps) % count) for i in range(count)])


def pick_matrix(row_member, member_seed, noise_count):
    member_ids = jnp.arange(member_seed.shape[0], dtype=jnp.int32)
    matched = row_member[:, None] == member_ids[None, :]
    seed_of = jnp.sum(jnp.where(matched, member_seed[None, :], 0), axis=1)
    sign_values = (1 - 2 * (row_member % 2)).astype(jnp.float32) * perturb_scale
    noise_ids = jnp.arange(noise_count, dtype=jnp.int32)
    return jnp.where(seed_of[:, None] == noise_ids[None, :], sign_values[:, None], jnp.float32(0.0))


def tile_plan(codes, block_rows, own_cols, owner_index, owners):
    tile_count = codes.shape[1]
    active = codes >= 0
    cleared = jnp.where(active, codes, 0)
    column = cleared // block_rows
    feature = cleared % block_rows
    per_owner = block_rows // owners
    feature = lax.rem(owner_index - feature // per_owner + owners, owners) * per_owner + feature % per_owner
    is_down = jnp.arange(codes.shape[0])[:, None] % 3 == 2
    major = jnp.where(is_down, feature, column)
    minor = jnp.where(is_down, column, feature)
    major_count = max(block_rows, own_cols)
    majors = jnp.arange(major_count, dtype=jnp.int32)
    filled = jnp.sum(
        jnp.where(active[:, None, :] & (major[:, None, :] == majors[None, :, None]), 1, 0), axis=2
    )
    padded = 2 * ((filled + 1) // 2)
    before = jnp.sum(jnp.where(majors[None, None, :] < major[:, :, None], padded[:, None, :], 0), axis=2)
    rank = jnp.sum(
        jnp.where(
            active[:, None, :]
            & (major[:, None, :] == major[:, :, None])
            & (minor[:, None, :] < minor[:, :, None]),
            1,
            0,
        ),
        axis=2,
    )
    place = jnp.where(active, before + rank, -1)
    length = tile_count + min(tile_count, major_count)
    group = 2 * UNROLL
    length = -(-length // group) * group
    tile_ids = jnp.arange(tile_count, dtype=jnp.int32)
    words = (tile_ids[None, :] - tile_count) + minor * 4096 + major * 1048576
    spots = jnp.arange(length, dtype=jnp.int32)
    packed = tile_count + jnp.sum(
        jnp.where(place[:, None, :] == spots[None, :, None], words[:, None, :], 0), axis=2
    )
    groups = (jnp.sum(padded, axis=1) + group - 1) // group
    return packed.astype(jnp.int32), groups.astype(jnp.int32)


def multiply_tiles(words_ref, groups_ref, which, length, read, tiles_ref, add):
    def group(i, carry):
        for u in range(UNROLL):
            at = which * length + (i * UNROLL + u) * 2
            first, second = words_ref[at], words_ref[at + 1]
            left = jnp.concatenate([read((first >> 12) & 255), read((second >> 12) & 255)], axis=1)
            right = jnp.concatenate([tiles_ref[first & 4095], tiles_ref[second & 4095]], axis=0)
            add(first >> 20, jnp.dot(left, right, preferred_element_type=jnp.float32))
        return carry

    lax.fori_loop(0, groups_ref[which], group, 0)


def load_tiles(own, choices, tiles, sem, parts):
    count = tiles.shape[0] - 1
    step = -(-count // parts)

    def copies(tiles_hbm):
        for first in range(0, count, step):
            part = pl.ds(first, min(step, count - first))
            pltpu.make_async_copy(tiles_hbm.at[part], tiles.at[part], sem).start()

    pl.when(own == 1)(functools.partial(copies, choices[0]))
    pl.when(own != 1)(functools.partial(copies, choices[1]))
    tiles[count] = jnp.zeros((BLOCK, BLOCK), tiles.dtype)
    return pltpu.make_async_copy(choices[0], tiles.at[pl.ds(0, count)], sem)


def expand_kernel(reps, words_ref, groups_ref, *refs):
    stacks = refs[:reps]
    gain_ref, left_ref, own_gate, other_gate, own_up, other_up = refs[reps : reps + 6]
    raw_ref, *part_refs = refs[reps + 6 : 2 * reps + 7]
    total_ref, gate_tiles, gate_sem, up_tiles, up_sem, x_ref = refs[-6:]
    owners, rows, width = stacks[0].shape
    per_owner = width // BLOCK
    strip = 48 if rows % 48 == 0 else 16
    gate_copy = load_tiles(groups_ref[3], (own_gate, other_gate), gate_tiles, gate_sem, 1)
    up_copy = load_tiles(groups_ref[3], (own_up, other_up), up_tiles, up_sem, 1)

    for rep in range(reps):

        def norm_rows(i, carry, rep=rep):
            start = pl.multiple_of(i * strip, strip)
            at = pl.ds(start, strip)

            def load(owner, part):
                return stacks[rep][owner, at, pl.ds(part * BLOCK, BLOCK)].astype(jnp.float32)

            squares = jnp.zeros((strip, BLOCK), jnp.float32)
            for owner in range(owners):
                for part in range(per_owner):
                    values = load(owner, part)
                    squares = squares + values * values
            total = jnp.sum(squares, axis=1, keepdims=True)
            inverse = lax.rsqrt(total / (owners * width) + epsilon)
            for owner in range(owners):
                for part in range(per_owner):
                    gain = gain_ref[:, pl.ds(owner * width + part * BLOCK, BLOCK)].astype(jnp.float32)
                    normed = (load(owner, part) * inverse * gain).astype(jnp.bfloat16)
                    x_ref[owner * per_owner + part, pl.ds(rep * rows + start, strip), :] = normed
            return carry

        lax.fori_loop(0, rows // strip, norm_rows, 0)
    raw = jnp.zeros(raw_ref.shape, jnp.float32)
    step = min(8, x_ref.shape[0])
    for d in range(0, x_ref.shape[0], step):
        raw = raw + lax.dot_general(
            jnp.concatenate([x_ref[d + i, pl.ds(0, rows), :] for i in range(step)], axis=1),
            left_ref[:, pl.ds(d * BLOCK, step * BLOCK)],
            (((1,), (1,)), ((), ())),
            preferred_element_type=jnp.float32,
        )
    raw_ref[...] = raw

    def read(block):
        return x_ref[block]

    def add(block, product):
        total_ref[block] += product

    for which, tiles in ((0, gate_tiles), (1, up_tiles)):
        total_ref[...] = jnp.zeros(total_ref.shape, jnp.float32)
        (gate_copy, up_copy)[which].wait()
        multiply_tiles(words_ref, groups_ref, which, words_ref.shape[0] // 3, read, tiles, add)
        for rep, part_ref in enumerate(part_refs):

            def narrow(c, carry, which=which, rep=rep, part_ref=part_ref):
                part_ref[which, c] = total_ref[c, pl.ds(rep * rows, rows), :].astype(jnp.bfloat16)
                return carry

            lax.fori_loop(0, total_ref.shape[0], narrow, 0, unroll=min(4, total_ref.shape[0]))


SMEM = pl.BlockSpec(memory_space=pltpu.SMEM)
VMEM = pl.BlockSpec(memory_space=pltpu.VMEM)
HBM = pl.BlockSpec(memory_space=pl.ANY)


def tile_cost(tile_count, all_rows):
    return pl.CostEstimate(
        flops=SLOW * 2 * tile_count * all_rows * BLOCK * BLOCK,
        bytes_accessed=2 * tile_count * BLOCK * BLOCK,
        transcendentals=0,
    )


def tile_scratch(tile_count, blocks, all_rows):
    return [
        pltpu.VMEM((blocks, all_rows, BLOCK), jnp.float32),
        pltpu.VMEM((tile_count + 1, BLOCK, BLOCK), jnp.bfloat16),
        pltpu.SemaphoreType.DMA,
    ]


def expand(words, groups, stacks, gain, left, gate_tiles, up_tiles, own_cols):
    reps = len(stacks)
    features = gain.shape[1]
    rows = stacks[0].shape[1]
    tile_count = gate_tiles[0].shape[0]
    scratch = tile_scratch(tile_count, own_cols, reps * rows)
    out = pl.pallas_call(
        functools.partial(expand_kernel, reps),
        out_shape=[jax.ShapeDtypeStruct((rows, left.shape[0]), jnp.float32)]
        + [jax.ShapeDtypeStruct((2, own_cols, rows, BLOCK), jnp.bfloat16)] * reps,
        in_specs=[SMEM, SMEM] + [VMEM] * (reps + 2) + [HBM] * 4,
        out_specs=[VMEM] * (1 + reps),
        scratch_shapes=scratch
        + scratch[1:]
        + [pltpu.VMEM((features // BLOCK, reps * rows, BLOCK), jnp.bfloat16)],
        compiler_params=pltpu.CompilerParams(vmem_limit_bytes=VMEM_LIMIT),
        cost_estimate=tile_cost(2 * tile_count, reps * rows),
        name="expand",
    )(words, groups, *stacks, gain, left, *gate_tiles, *up_tiles)
    return out[0], out[1:]


def activate_kernel(reps, *refs):
    parts = refs[:reps]
    raw_ref, picks_ref, wide_cols, down_cols = refs[reps : reps + 4]
    hidden_ref, coef_ref = refs[-2:]
    noise = picks_ref.shape[1]
    columns, rows = hidden_ref.shape[:2]
    picks = picks_ref[...]
    coefs = (jnp.concatenate([picks, picks], axis=1) * raw_ref[...]).astype(jnp.bfloat16)

    def pair(i, down):
        hiddens = []
        for u in range(2):
            c = i * 2 + u
            low_rank = jnp.dot(coefs, wide_cols[c], preferred_element_type=jnp.float32)
            values = []
            for which in range(2):
                value = low_rank[:, which * BLOCK : (which + 1) * BLOCK]
                for part in parts:
                    value = value + part[which, c].astype(jnp.float32)
                values.append(value)
            gate, up = values
            hidden = (gate / (1.0 + jnp.exp(-gate)) * up).astype(jnp.bfloat16)
            hidden_ref[c] = hidden
            hiddens.append(hidden)
        return down + lax.dot_general(
            jnp.concatenate(hiddens, axis=1),
            down_cols[i],
            (((1,), (1,)), ((), ())),
            preferred_element_type=jnp.float32,
        )

    down = lax.fori_loop(
        0, columns // 2, pair, jnp.zeros((rows, noise), jnp.float32), unroll=min(4, columns // 2)
    )
    coef_ref[...] = picks * down


def activate(parts, raw, picks, wide_cols, down_cols):
    own_cols, rows = parts[0].shape[1:3]
    noise = picks.shape[1]
    reps = len(parts)
    return pl.pallas_call(
        functools.partial(activate_kernel, reps),
        out_shape=[
            jax.ShapeDtypeStruct((own_cols, rows, BLOCK), jnp.bfloat16),
            jax.ShapeDtypeStruct((rows, noise), jnp.float32),
        ],
        in_specs=[VMEM] * (reps + 4),
        out_specs=[VMEM] * 2,
        compiler_params=pltpu.CompilerParams(vmem_limit_bytes=16 * MIB),
        cost_estimate=pl.CostEstimate(
            flops=100 * own_cols * rows * BLOCK,
            bytes_accessed=(reps * 2 + 1) * 2 * own_cols * rows * BLOCK,
            transcendentals=own_cols * rows * BLOCK,
        ),
        name="activate",
    )(*parts, raw, picks, wide_cols, down_cols)


def contract_kernel(reps, words_ref, groups_ref, *refs):
    hiddens = refs[:reps]
    coef_ref, right_ref, own_hbm, other_hbm = refs[reps : reps + 4]
    outs = refs[-3 - reps : -3]
    total_ref, tiles, sem = refs[-3:]
    rows = hiddens[0].shape[1]
    blocks = total_ref.shape[0]
    copy = load_tiles(groups_ref[3], (own_hbm, other_hbm), tiles, sem, COPIES)

    def read(block):
        return jnp.concatenate([hidden[block] for hidden in hiddens], axis=0)

    def add(block, product):
        total_ref[block] += product

    coef = coef_ref[...]
    high = coef.astype(jnp.bfloat16)
    low = (coef - high.astype(jnp.float32)).astype(jnp.bfloat16)
    right = right_ref[...]
    both = jnp.concatenate([high, low], axis=1)
    twice = jnp.concatenate([right, right], axis=0)
    for d in range(0, blocks, 2):
        start = jnp.dot(both, twice[:, d * BLOCK : (d + 2) * BLOCK], preferred_element_type=jnp.float32)
        for i in range(2):
            total_ref[d + i, pl.ds(0, rows), :] = start[:, i * BLOCK : (i + 1) * BLOCK]
            if reps > 1:
                total_ref[d + i, pl.ds(rows, (reps - 1) * rows), :] = jnp.zeros(
                    ((reps - 1) * rows, BLOCK), jnp.float32
                )
    copy.wait()
    multiply_tiles(words_ref, groups_ref, 2, words_ref.shape[0] // 3, read, tiles, add)
    for rep in range(reps):
        for d in range(blocks):
            outs[rep][:, pl.ds(d * BLOCK, BLOCK)] = total_ref[d, pl.ds(rep * rows, rows), :].astype(jnp.bfloat16)


def contract(words, groups, hiddens, coef, right, tiles):
    own_cols, rows = hiddens[0].shape[:2]
    reps = len(hiddens)
    features = right.shape[1]
    tile_count = tiles[0].shape[0]
    return pl.pallas_call(
        functools.partial(contract_kernel, reps),
        out_shape=[jax.ShapeDtypeStruct((rows, features), jnp.bfloat16)] * reps,
        in_specs=[SMEM, SMEM] + [VMEM] * (reps + 2) + [HBM] * 2,
        out_specs=[VMEM] * reps,
        scratch_shapes=tile_scratch(tile_count, features // BLOCK, reps * rows),
        compiler_params=pltpu.CompilerParams(vmem_limit_bytes=VMEM_LIMIT),
        cost_estimate=tile_cost(tile_count, reps * rows),
        name="contract",
    )(words, groups, *hiddens, coef, right, *tiles)


def per_device(
    tokens,
    norm_gain,
    gate_tiles,
    up_tiles,
    down_tiles,
    gate_slot,
    up_slot,
    down_slot,
    owned_columns,
    gate_left,
    gate_right,
    up_left,
    up_right,
    down_left,
    down_right,
    row_member,
    member_seed,
):
    section_index = lax.axis_index("section")
    owner_index = lax.axis_index("tensor")
    rep_index = lax.axis_index("rep")
    owners, reps = lax.axis_size("tensor"), lax.axis_size("rep")
    rows, width = tokens.shape
    own_cols = owned_columns.shape[1] // owners
    block_rows = gate_left.shape[2] // BLOCK
    tile_count = gate_tiles.shape[1]

    half = rows // 2
    piece = half // 2
    mine_rows = lax.dynamic_slice_in_dim(tokens, section_index * half, half)
    streams = [mine_rows[:piece], mine_rows[piece:]]

    def gathered(own):
        stack = jnp.stack([own] + [hop(own, "tensor", step) for step in range(1, owners)])
        return [stack] + [hop(stack, "rep", g) for g in range(1, reps)]

    stacks = [gathered(stream) for stream in streams]

    codes = jnp.stack([gate_slot[0], up_slot[0], down_slot[0]])
    codes = lax.dynamic_slice_in_dim(codes, rep_index * tile_count, tile_count, axis=1)
    wide = jnp.concatenate([gate_left[0], up_left[0], down_right[0], norm_gain], axis=0)
    other_codes, other_wide = hop(codes, "section", 1), hop(wide, "section", 1)
    other_codes, other_wide, gate_tiles, up_tiles = lax.optimization_barrier(
        (other_codes, other_wide, gate_tiles, up_tiles)
    )
    gate_pair = (gate_tiles[0], hop(gate_tiles[0], "section", 1))
    up_pair = (up_tiles[0], hop(up_tiles[0], "section", 1))
    stacks, down_tiles = lax.optimization_barrier((stacks, down_tiles))
    down_pair = (down_tiles[0], hop(down_tiles[0], "section", 1))

    plans = tile_plan(jnp.concatenate([codes, other_codes]), block_rows, own_cols, owner_index, owners)
    rotation = lax.rem(owner_index - jnp.arange(owners, dtype=jnp.int32) + owners, owners)
    noise = gate_left.shape[1]

    def rotated(table):
        parts = table.reshape(table.shape[0], owners, width)
        return jnp.take(parts, rotation, axis=1).reshape(table.shape)

    columns = lax.dynamic_slice_in_dim(owned_columns[0], owner_index * own_cols, own_cols)

    def owned(table):
        return jnp.take(table.reshape(table.shape[0], -1, BLOCK), columns, axis=1)

    cols = owned(jnp.concatenate([gate_right[0], up_right[0], down_left[0]], axis=0))
    other_cols = hop(cols, "section", 1)
    picks = pick_matrix(row_member, member_seed, noise)

    def tables(section):
        own = section_index == section
        words, groups = (jnp.where(own, table[:3], table[3:]) for table in plans)
        groups = jnp.concatenate([groups, own.astype(jnp.int32)[None]])
        chosen = rotated(jnp.where(own, wide, other_wide))
        left, right, gain = chosen[: 2 * noise], chosen[2 * noise : 3 * noise], chosen[3 * noise :]
        chosen = jnp.where(own, cols, other_cols)
        gate_cols, up_cols, down_cols = chosen[:noise], chosen[noise : 2 * noise], chosen[2 * noise :]
        empty = jnp.zeros_like(gate_cols)
        wide_cols = jnp.concatenate(
            [jnp.concatenate([gate_cols, empty], axis=2), jnp.concatenate([empty, up_cols], axis=2)], axis=0
        ).transpose(1, 0, 2)
        down_cols = down_cols.reshape(noise, own_cols // 2, 2 * BLOCK).transpose(1, 0, 2)
        return words.reshape(-1), groups, left, right, gain, wide_cols, down_cols

    layers = [tables(section) for section in range(2)]

    mine_picks = lax.dynamic_slice_in_dim(picks, section_index * half, half)
    picked = [mine_picks[:piece], mine_picks[piece:]]

    def layer(stacks, picked, section):
        words, groups, left, right, gain, wide_cols, down_cols = layers[section]
        raw, parts = expand(words, groups, stacks, gain, left, gate_pair, up_pair, own_cols)
        parts = [parts[0]] + [hop(parts[g], "rep", -g) for g in range(1, reps)]
        hidden, coef = activate(parts, raw, picked, wide_cols, down_cols)
        hiddens = [hidden] + [hop(hidden, "rep", g) for g in range(1, reps)]
        return contract(words, groups, hiddens, coef, right, down_pair)

    def scattered(own, outs):
        total = outs[0].astype(jnp.float32)
        for g in range(1, reps):
            total = total + hop(outs[g], "rep", -g).astype(jnp.float32)
        value = own.astype(jnp.float32) + total[:, :width]
        for step in range(1, owners):
            sent = total[:, step * width : (step + 1) * width].astype(jnp.bfloat16)
            value = value + hop(sent, "tensor", -step).astype(jnp.float32)
        return value.astype(jnp.bfloat16)

    results = []
    for section in range(2):
        streams = [scattered(own, layer(stack, p, section)) for own, stack, p in zip(streams, stacks, picked)]
        results.append(jnp.concatenate(streams, axis=0))
        if section == 0:
            stacks = [gathered(stream) for stream in streams]
    first, second = results
    kept = jnp.where(section_index == 0, first, second)
    received = hop(jnp.where(section_index == 0, second, first), "section", 1)
    out = jnp.where(
        section_index == 0,
        jnp.concatenate([kept, received], axis=0),
        jnp.concatenate([received, kept], axis=0),
    )
    return out[None]


def solution(mesh):
    placed = (
        P(("pop", "rep"), "tensor"),
        P("section", None),
        P("section", ("tensor", "rep"), None, None),
        P("section", ("tensor", "rep"), None, None),
        P("section", ("tensor", "rep"), None, None),
        P("section", "tensor"),
        P("section", "tensor"),
        P("section", "tensor"),
        P("section", None),
        P("section", None, None),
        P("section", None, None),
        P("section", None, None),
        P("section", None, None),
        P("section", None, None),
        P("section", None, None),
        P(("pop", "rep")),
        P("pop"),
    )
    return jax.shard_map(
        per_device,
        mesh=mesh,
        in_specs=placed,
        out_specs=P("section", ("pop", "rep"), "tensor"),
        check_vma=False,
    )
```

```python
import functools

import jax
import jax.numpy as jnp
from jax import lax
from jax.experimental import pallas as pl
from jax.experimental.pallas import tpu as pltpu
from jax.sharding import PartitionSpec as P

BLOCK = 128
UNROLL = 16
MIB = 1024 * 1024
VMEM_LIMIT = 56 * MIB
COPIES = 8
SLOW = 4

perturb_scale = 0.5
epsilon = 1e-05


def hop(value, axis, steps):
    count = lax.axis_size(axis)
    return lax.ppermute(value, axis, [(i, (i + steps) % count) for i in range(count)])


def pick_matrix(row_member, member_seed, noise_count):
    member_ids = jnp.arange(member_seed.shape[0], dtype=jnp.int32)
    matched = row_member[:, None] == member_ids[None, :]
    seed_of = jnp.sum(jnp.where(matched, member_seed[None, :], 0), axis=1)
    sign_values = (1 - 2 * (row_member % 2)).astype(jnp.float32) * perturb_scale
    noise_ids = jnp.arange(noise_count, dtype=jnp.int32)
    return jnp.where(seed_of[:, None] == noise_ids[None, :], sign_values[:, None], jnp.float32(0.0))


def tile_plan(codes, block_rows, own_cols, owner_index, owners):
    tile_count = codes.shape[1]
    active = codes >= 0
    cleared = jnp.where(active, codes, 0)
    column = cleared // block_rows
    feature = cleared % block_rows
    per_owner = block_rows // owners
    feature = lax.rem(owner_index - feature // per_owner + owners, owners) * per_owner + feature % per_owner
    is_down = jnp.arange(codes.shape[0])[:, None] % 3 == 2
    major = jnp.where(is_down, feature, column)
    minor = jnp.where(is_down, column, feature)
    major_count = max(block_rows, own_cols)
    majors = jnp.arange(major_count, dtype=jnp.int32)
    filled = jnp.sum(
        jnp.where(active[:, None, :] & (major[:, None, :] == majors[None, :, None]), 1, 0), axis=2
    )
    padded = 2 * ((filled + 1) // 2)
    before = jnp.sum(jnp.where(majors[None, None, :] < major[:, :, None], padded[:, None, :], 0), axis=2)
    rank = jnp.sum(
        jnp.where(
            active[:, None, :]
            & (major[:, None, :] == major[:, :, None])
            & (minor[:, None, :] < minor[:, :, None]),
            1,
            0,
        ),
        axis=2,
    )
    place = jnp.where(active, before + rank, -1)
    length = tile_count + min(tile_count, major_count)
    group = 2 * UNROLL
    length = -(-length // group) * group
    tile_ids = jnp.arange(tile_count, dtype=jnp.int32)
    words = (tile_ids[None, :] - tile_count) + minor * 4096 + major * 1048576
    spots = jnp.arange(length, dtype=jnp.int32)
    packed = tile_count + jnp.sum(
        jnp.where(place[:, None, :] == spots[None, :, None], words[:, None, :], 0), axis=2
    )
    groups = (jnp.sum(padded, axis=1) + group - 1) // group
    return packed.astype(jnp.int32), groups.astype(jnp.int32)


def multiply_tiles(words_ref, groups_ref, which, length, read, tiles_ref, add):
    def group(i, carry):
        for u in range(UNROLL):
            at = which * length + (i * UNROLL + u) * 2
            first, second = words_ref[at], words_ref[at + 1]
            left = jnp.concatenate([read((first >> 12) & 255), read((second >> 12) & 255)], axis=1)
            right = jnp.concatenate([tiles_ref[first & 4095], tiles_ref[second & 4095]], axis=0)
            add(first >> 20, jnp.dot(left, right, preferred_element_type=jnp.float32))
        return carry

    lax.fori_loop(0, groups_ref[which], group, 0)


def load_tiles(own, choices, tiles, sem):
    count = tiles.shape[0] - 1
    step = -(-count // COPIES)

    def copies(tiles_hbm):
        for first in range(0, count, step):
            part = pl.ds(first, min(step, count - first))
            pltpu.make_async_copy(tiles_hbm.at[part], tiles.at[part], sem).start()

    pl.when(own == 1)(functools.partial(copies, choices[0]))
    pl.when(own != 1)(functools.partial(copies, choices[1]))
    tiles[count] = jnp.zeros((BLOCK, BLOCK), tiles.dtype)
    return pltpu.make_async_copy(choices[0], tiles.at[pl.ds(0, count)], sem)


def expand_kernel(reps, words_ref, groups_ref, *refs):
    stacks = refs[:reps]
    gain_ref, left_ref, own_gate, other_gate, own_up, other_up = refs[reps : reps + 6]
    raw_ref, *part_refs = refs[reps + 6 : 2 * reps + 7]
    total_ref, gate_tiles, gate_sem, up_tiles, up_sem, x_ref = refs[-6:]
    owners, rows, width = stacks[0].shape
    per_owner = width // BLOCK
    strip = 48 if rows % 48 == 0 else 16
    gate_copy = load_tiles(groups_ref[3], (own_gate, other_gate), gate_tiles, gate_sem)

    for rep in range(reps):

        def norm_rows(i, carry, rep=rep):
            start = pl.multiple_of(i * strip, strip)
            at = pl.ds(start, strip)

            def load(owner, part):
                return stacks[rep][owner, at, pl.ds(part * BLOCK, BLOCK)].astype(jnp.float32)

            squares = jnp.zeros((strip, BLOCK), jnp.float32)
            for owner in range(owners):
                for part in range(per_owner):
                    values = load(owner, part)
                    squares = squares + values * values
            total = jnp.sum(squares, axis=1, keepdims=True)
            inverse = lax.rsqrt(total / (owners * width) + epsilon)
            for owner in range(owners):
                for part in range(per_owner):
                    gain = gain_ref[:, pl.ds(owner * width + part * BLOCK, BLOCK)].astype(jnp.float32)
                    normed = (load(owner, part) * inverse * gain).astype(jnp.bfloat16)
                    x_ref[owner * per_owner + part, pl.ds(rep * rows + start, strip), :] = normed
            return carry

        lax.fori_loop(0, rows // strip, norm_rows, 0)
    raw = jnp.zeros(raw_ref.shape, jnp.float32)
    step = min(8, x_ref.shape[0])
    for d in range(0, x_ref.shape[0], step):
        raw = raw + lax.dot_general(
            jnp.concatenate([x_ref[d + i, pl.ds(0, rows), :] for i in range(step)], axis=1),
            left_ref[:, pl.ds(d * BLOCK, step * BLOCK)],
            (((1,), (1,)), ((), ())),
            preferred_element_type=jnp.float32,
        )
    raw_ref[...] = raw

    def read(block):
        return x_ref[block]

    def add(block, product):
        total_ref[block] += product

    for which, tiles in ((0, gate_tiles), (1, up_tiles)):
        total_ref[...] = jnp.zeros(total_ref.shape, jnp.float32)
        if which == 0:
            gate_copy.wait()
            up_copy = load_tiles(groups_ref[3], (own_up, other_up), up_tiles, up_sem)
        else:
            up_copy.wait()
        multiply_tiles(words_ref, groups_ref, which, words_ref.shape[0] // 3, read, tiles, add)
        for rep, part_ref in enumerate(part_refs):

            def narrow(c, carry, which=which, rep=rep, part_ref=part_ref):
                part_ref[which, c] = total_ref[c, pl.ds(rep * rows, rows), :].astype(jnp.bfloat16)
                return carry

            lax.fori_loop(0, total_ref.shape[0], narrow, 0, unroll=min(4, total_ref.shape[0]))


SMEM = pl.BlockSpec(memory_space=pltpu.SMEM)
VMEM = pl.BlockSpec(memory_space=pltpu.VMEM)
HBM = pl.BlockSpec(memory_space=pl.ANY)


def tile_cost(tile_count, all_rows):
    return pl.CostEstimate(
        flops=SLOW * 2 * tile_count * all_rows * BLOCK * BLOCK,
        bytes_accessed=2 * tile_count * BLOCK * BLOCK,
        transcendentals=0,
    )


def tile_scratch(tile_count, blocks, all_rows):
    return [
        pltpu.VMEM((blocks, all_rows, BLOCK), jnp.float32),
        pltpu.VMEM((tile_count + 1, BLOCK, BLOCK), jnp.bfloat16),
        pltpu.SemaphoreType.DMA,
    ]


def expand(words, groups, stacks, gain, left, gate_tiles, up_tiles, own_cols):
    reps = len(stacks)
    features = gain.shape[1]
    rows = stacks[0].shape[1]
    tile_count = gate_tiles[0].shape[0]
    scratch = tile_scratch(tile_count, own_cols, reps * rows)
    out = pl.pallas_call(
        functools.partial(expand_kernel, reps),
        out_shape=[jax.ShapeDtypeStruct((rows, left.shape[0]), jnp.float32)]
        + [jax.ShapeDtypeStruct((2, own_cols, rows, BLOCK), jnp.bfloat16)] * reps,
        in_specs=[SMEM, SMEM] + [VMEM] * (reps + 2) + [HBM] * 4,
        out_specs=[VMEM] * (1 + reps),
        scratch_shapes=scratch
        + scratch[1:]
        + [pltpu.VMEM((features // BLOCK, reps * rows, BLOCK), jnp.bfloat16)],
        compiler_params=pltpu.CompilerParams(vmem_limit_bytes=VMEM_LIMIT),
        cost_estimate=tile_cost(2 * tile_count, reps * rows),
        name="expand",
    )(words, groups, *stacks, gain, left, *gate_tiles, *up_tiles)
    return out[0], out[1:]


def activate_kernel(reps, *refs):
    parts = refs[:reps]
    raw_ref, picks_ref, wide_cols, down_cols = refs[reps : reps + 4]
    hidden_ref, coef_ref = refs[-2:]
    noise = picks_ref.shape[1]
    columns, rows = hidden_ref.shape[:2]
    picks = picks_ref[...]
    coefs = (jnp.concatenate([picks, picks], axis=1) * raw_ref[...]).astype(jnp.bfloat16)

    def pair(i, down):
        hiddens = []
        for u in range(2):
            c = i * 2 + u
            low_rank = jnp.dot(coefs, wide_cols[c], preferred_element_type=jnp.float32)
            values = []
            for which in range(2):
                value = low_rank[:, which * BLOCK : (which + 1) * BLOCK]
                for part in parts:
                    value = value + part[which, c].astype(jnp.float32)
                values.append(value)
            gate, up = values
            hidden = (gate / (1.0 + jnp.exp(-gate)) * up).astype(jnp.bfloat16)
            hidden_ref[c] = hidden
            hiddens.append(hidden)
        return down + lax.dot_general(
            jnp.concatenate(hiddens, axis=1),
            down_cols[i],
            (((1,), (1,)), ((), ())),
            preferred_element_type=jnp.float32,
        )

    down = lax.fori_loop(
        0, columns // 2, pair, jnp.zeros((rows, noise), jnp.float32), unroll=min(4, columns // 2)
    )
    coef_ref[...] = picks * down


def activate(parts, raw, picks, wide_cols, down_cols):
    own_cols, rows = parts[0].shape[1:3]
    noise = picks.shape[1]
    reps = len(parts)
    return pl.pallas_call(
        functools.partial(activate_kernel, reps),
        out_shape=[
            jax.ShapeDtypeStruct((own_cols, rows, BLOCK), jnp.bfloat16),
            jax.ShapeDtypeStruct((rows, noise), jnp.float32),
        ],
        in_specs=[VMEM] * (reps + 4),
        out_specs=[VMEM] * 2,
        compiler_params=pltpu.CompilerParams(vmem_limit_bytes=16 * MIB),
        cost_estimate=pl.CostEstimate(
            flops=100 * own_cols * rows * BLOCK,
            bytes_accessed=(reps * 2 + 1) * 2 * own_cols * rows * BLOCK,
            transcendentals=own_cols * rows * BLOCK,
        ),
        name="activate",
    )(*parts, raw, picks, wide_cols, down_cols)


def contract_kernel(reps, words_ref, groups_ref, *refs):
    hiddens = refs[:reps]
    coef_ref, right_ref, own_hbm, other_hbm = refs[reps : reps + 4]
    outs = refs[-3 - reps : -3]
    total_ref, tiles, sem = refs[-3:]
    rows = hiddens[0].shape[1]
    blocks = total_ref.shape[0]
    copy = load_tiles(groups_ref[3], (own_hbm, other_hbm), tiles, sem)

    def read(block):
        return jnp.concatenate([hidden[block] for hidden in hiddens], axis=0)

    def add(block, product):
        total_ref[block] += product

    coef = coef_ref[...]
    high = coef.astype(jnp.bfloat16)
    low = (coef - high.astype(jnp.float32)).astype(jnp.bfloat16)
    right = right_ref[...]
    both = jnp.concatenate([high, low], axis=1)
    twice = jnp.concatenate([right, right], axis=0)
    for d in range(0, blocks, 2):
        start = jnp.dot(both, twice[:, d * BLOCK : (d + 2) * BLOCK], preferred_element_type=jnp.float32)
        for i in range(2):
            total_ref[d + i, pl.ds(0, rows), :] = start[:, i * BLOCK : (i + 1) * BLOCK]
            if reps > 1:
                total_ref[d + i, pl.ds(rows, (reps - 1) * rows), :] = jnp.zeros(
                    ((reps - 1) * rows, BLOCK), jnp.float32
                )
    copy.wait()
    multiply_tiles(words_ref, groups_ref, 2, words_ref.shape[0] // 3, read, tiles, add)
    for rep in range(reps):
        for d in range(blocks):
            outs[rep][:, pl.ds(d * BLOCK, BLOCK)] = total_ref[d, pl.ds(rep * rows, rows), :].astype(jnp.bfloat16)


def contract(words, groups, hiddens, coef, right, tiles):
    own_cols, rows = hiddens[0].shape[:2]
    reps = len(hiddens)
    features = right.shape[1]
    tile_count = tiles[0].shape[0]
    return pl.pallas_call(
        functools.partial(contract_kernel, reps),
        out_shape=[jax.ShapeDtypeStruct((rows, features), jnp.bfloat16)] * reps,
        in_specs=[SMEM, SMEM] + [VMEM] * (reps + 2) + [HBM] * 2,
        out_specs=[VMEM] * reps,
        scratch_shapes=tile_scratch(tile_count, features // BLOCK, reps * rows),
        compiler_params=pltpu.CompilerParams(vmem_limit_bytes=VMEM_LIMIT),
        cost_estimate=tile_cost(tile_count, reps * rows),
        name="contract",
    )(words, groups, *hiddens, coef, right, *tiles)


def per_device(
    tokens,
    norm_gain,
    gate_tiles,
    up_tiles,
    down_tiles,
    gate_slot,
    up_slot,
    down_slot,
    owned_columns,
    gate_left,
    gate_right,
    up_left,
    up_right,
    down_left,
    down_right,
    row_member,
    member_seed,
):
    section_index = lax.axis_index("section")
    owner_index = lax.axis_index("tensor")
    rep_index = lax.axis_index("rep")
    owners, reps = lax.axis_size("tensor"), lax.axis_size("rep")
    rows, width = tokens.shape
    own_cols = owned_columns.shape[1] // owners
    block_rows = gate_left.shape[2] // BLOCK
    tile_count = gate_tiles.shape[1]

    half = rows // 2
    piece = half // 2
    mine_rows = lax.dynamic_slice_in_dim(tokens, section_index * half, half)
    streams = [mine_rows[:piece], mine_rows[piece:]]

    def gathered(own):
        stack = jnp.stack([own] + [hop(own, "tensor", step) for step in range(1, owners)])
        return [stack] + [hop(stack, "rep", g) for g in range(1, reps)]

    codes = jnp.stack([gate_slot[0], up_slot[0], down_slot[0]])
    codes = lax.dynamic_slice_in_dim(codes, rep_index * tile_count, tile_count, axis=1)
    wide = jnp.concatenate([gate_left[0], up_left[0], down_right[0], norm_gain], axis=0)
    codes, wide, streams[0] = lax.optimization_barrier((codes, wide, streams[0]))
    other_codes, other_wide = hop(codes, "section", 1), hop(wide, "section", 1)
    stacks = [gathered(stream) for stream in streams]
    other_codes, other_wide, gate_tiles, up_tiles, down_tiles = lax.optimization_barrier(
        (other_codes, other_wide, gate_tiles, up_tiles, down_tiles)
    )
    gate_pair = (gate_tiles[0], hop(gate_tiles[0], "section", 1))
    up_pair = (up_tiles[0], hop(up_tiles[0], "section", 1))
    down_pair = (down_tiles[0], hop(down_tiles[0], "section", 1))

    plans = tile_plan(jnp.concatenate([codes, other_codes]), block_rows, own_cols, owner_index, owners)
    rotation = lax.rem(owner_index - jnp.arange(owners, dtype=jnp.int32) + owners, owners)
    noise = gate_left.shape[1]

    def rotated(table):
        parts = table.reshape(table.shape[0], owners, width)
        return jnp.take(parts, rotation, axis=1).reshape(table.shape)

    columns = lax.dynamic_slice_in_dim(owned_columns[0], owner_index * own_cols, own_cols)

    def owned(table):
        return jnp.take(table.reshape(table.shape[0], -1, BLOCK), columns, axis=1)

    cols = owned(jnp.concatenate([gate_right[0], up_right[0], down_left[0]], axis=0))
    other_cols = hop(cols, "section", 1)
    picks = pick_matrix(row_member, member_seed, noise)

    def tables(section):
        own = section_index == section
        words, groups = (jnp.where(own, table[:3], table[3:]) for table in plans)
        groups = jnp.concatenate([groups, own.astype(jnp.int32)[None]])
        chosen = rotated(jnp.where(own, wide, other_wide))
        left, right, gain = chosen[: 2 * noise], chosen[2 * noise : 3 * noise], chosen[3 * noise :]
        chosen = jnp.where(own, cols, other_cols)
        gate_cols, up_cols, down_cols = chosen[:noise], chosen[noise : 2 * noise], chosen[2 * noise :]
        empty = jnp.zeros_like(gate_cols)
        wide_cols = jnp.concatenate(
            [jnp.concatenate([gate_cols, empty], axis=2), jnp.concatenate([empty, up_cols], axis=2)], axis=0
        ).transpose(1, 0, 2)
        down_cols = down_cols.reshape(noise, own_cols // 2, 2 * BLOCK).transpose(1, 0, 2)
        return words.reshape(-1), groups, left, right, gain, wide_cols, down_cols

    layers = [tables(section) for section in range(2)]

    mine_picks = lax.dynamic_slice_in_dim(picks, section_index * half, half)
    picked = [mine_picks[:piece], mine_picks[piece:]]

    def layer(stacks, picked, section):
        words, groups, left, right, gain, wide_cols, down_cols = layers[section]
        raw, parts = expand(words, groups, stacks, gain, left, gate_pair, up_pair, own_cols)
        parts = [parts[0]] + [hop(parts[g], "rep", -g) for g in range(1, reps)]
        hidden, coef = activate(parts, raw, picked, wide_cols, down_cols)
        hiddens = [hidden] + [hop(hidden, "rep", g) for g in range(1, reps)]
        return contract(words, groups, hiddens, coef, right, down_pair)

    def scattered(own, outs):
        total = outs[0].astype(jnp.float32)
        for g in range(1, reps):
            total = total + hop(outs[g], "rep", -g).astype(jnp.float32)
        value = own.astype(jnp.float32) + total[:, :width]
        for step in range(1, owners):
            sent = total[:, step * width : (step + 1) * width].astype(jnp.bfloat16)
            value = value + hop(sent, "tensor", -step).astype(jnp.float32)
        return value.astype(jnp.bfloat16)

    results = []
    for section in range(2):
        streams = [scattered(own, layer(stack, p, section)) for own, stack, p in zip(streams, stacks, picked)]
        results.append(jnp.concatenate(streams, axis=0))
        if section == 0:
            stacks = [gathered(stream) for stream in streams]
    first, second = results
    kept = jnp.where(section_index == 0, first, second)
    received = hop(jnp.where(section_index == 0, second, first), "section", 1)
    out = jnp.where(
        section_index == 0,
        jnp.concatenate([kept, received], axis=0),
        jnp.concatenate([received, kept], axis=0),
    )
    return out[None]


def solution(mesh):
    placed = (
        P(("pop", "rep"), "tensor"),
        P("section", None),
        P("section", ("tensor", "rep"), None, None),
        P("section", ("tensor", "rep"), None, None),
        P("section", ("tensor", "rep"), None, None),
        P("section", "tensor"),
        P("section", "tensor"),
        P("section", "tensor"),
        P("section", None),
        P("section", None, None),
        P("section", None, None),
        P("section", None, None),
        P("section", None, None),
        P("section", None, None),
        P("section", None, None),
        P(("pop", "rep")),
        P("pop"),
    )
    return jax.shard_map(
        per_device,
        mesh=mesh,
        in_specs=placed,
        out_specs=P("section", ("pop", "rep"), "tensor"),
        check_vma=False,
    )
```
